32 devices in a mesh: fsdp: 8 (over y, x, core), tensor: 4 (over z).
Axes of the slice: x: 2, y: 2, z: 4, core: 2. Of those that a mesh axis runs over, the one named last changes fastest.
Arguments:
- tokens: bfloat16 [8192, 1536], P(('fsdp', 'tensor')), may hold values from -6 to 6
- w_query: bfloat16 [1536, 1536], P('fsdp', 'tensor'), may hold values from -0.15625 to 0.15625
- key_weight_matrix: bfloat16 [1536, 768], P('fsdp', 'tensor'), may hold values from -0.15625 to 0.15625
- value_weight_matrix: bfloat16 [1536, 768], P('fsdp', 'tensor'), may hold values from -0.15625 to 0.15625
- w_out: bfloat16 [1536, 1536], P('tensor', 'fsdp'), may hold values from -6 to 6
- w_gate: bfloat16 [1536, 4096], P('fsdp', 'tensor'), may hold values from -0.15625 to 0.15625
- w_up: bfloat16 [1536, 4096], P('fsdp', 'tensor'), may hold values from -0.15625 to 0.15625
- w_down: bfloat16 [4096, 1536], P('tensor', 'fsdp'), may hold values from -0.1875 to 0.1875
- norm_attn: bfloat16 [1536], P('fsdp'), may hold values from 0.5 to 1.5
- norm_ffn: bfloat16 [1536], P('fsdp'), may hold values from 0.5 to 1.5
- grad_out: bfloat16 [8192, 1536], P(('fsdp', 'tensor')), may hold values from -6 to 6
Outputs:
- layer_out: bfloat16 [8192, 1536], P(('fsdp', 'tensor'))
- grad_tokens: bfloat16 [8192, 1536], P(('fsdp', 'tensor'))
- grad_query: float32 [1536, 1536], P('fsdp', 'tensor')
- grad_key: float32 [1536, 768], P('fsdp', 'tensor')
- grad_value: float32 [1536, 768], P('fsdp', 'tensor')
- grad_outproj: float32 [1536, 1536], P('tensor', 'fsdp')
- grad_gate: float32 [1536, 4096], P('fsdp', 'tensor')
- grad_upproj: float32 [1536, 4096], P('fsdp', 'tensor')
- grad_down: float32 [4096, 1536], P('tensor', 'fsdp')
- grad_norm_attn: float32 [1536], P('fsdp')
- grad_norm_ffn: float32 [1536], P('fsdp')
- rms_stats: float32 [3], replicated
The draws below stay inside these ranges and needn't reach their ends.
All inputs are finite; a program needn't handle non-finite values.
Results may differ from the reference program's by a relative error of at most 0.024.
Values may be sent and summed in bfloat16 or wider, within the bound.
No kernel may reach another device: no remote copies, remote signals or barrier semaphores. Data moves between devices by JAX's collectives and lax.ppermute only.
A program may use at most 192 MiB of HBM per device.

```python
import jax
import jax.numpy as jnp
from jax import lax

MODEL_WIDTH = 1536
QUERY_HEAD_COUNT = 16
KEY_VALUE_HEADS = 8
HEAD_WIDTH = 96
FF = 4096
SEQUENCE_LENGTH = 4096
TOKEN_COUNT = 8192


def block_scale(key, extent, shards, least, high):
    loudness, own = 1.0, jax.random.fold_in(key, 6)
    for position, parts in shards:
        draws = jnp.exp(jax.random.uniform(jax.random.fold_in(own, position), (parts,), jnp.float32, least / len(shards), high / len(shards)))
        loudness = loudness * jnp.repeat(draws, extent[position] // parts).reshape([-1 if axis == position else 1 for axis in range(len(extent))])
    return loudness


def noise(key, extent, deviation, bound, pieces=(), kind=jnp.bfloat16):
    array = deviation * jax.random.normal(key, extent, jnp.float32)
    if pieces:
        array = array * block_scale(key, extent, pieces, -0.22, 0.18)
    return jnp.clip(array, -bound, bound).astype(kind)


def setup_inputs(seed: int = 0) -> dict:
    key_of = jax.random.split(jax.random.key(seed), 12)
    return {
        "tokens": noise(key_of[0], (TOKEN_COUNT, MODEL_WIDTH), 1.0, 6.0, ((0, 32),)),
        "w_query": noise(key_of[1], (MODEL_WIDTH, QUERY_HEAD_COUNT * HEAD_WIDTH), MODEL_WIDTH ** -0.5, 0.15625, ((0, 8), (1, 4))),
        "key_weight_matrix": noise(key_of[2], (MODEL_WIDTH, KEY_VALUE_HEADS * HEAD_WIDTH), MODEL_WIDTH ** -0.5, 0.15625, ((0, 8), (1, 4))),
        "value_weight_matrix": noise(key_of[3], (MODEL_WIDTH, KEY_VALUE_HEADS * HEAD_WIDTH), MODEL_WIDTH ** -0.5, 0.15625, ((0, 8), (1, 4))),
        "w_out": noise(key_of[4], (QUERY_HEAD_COUNT * HEAD_WIDTH, MODEL_WIDTH), (QUERY_HEAD_COUNT * HEAD_WIDTH * 4 // SEQUENCE_LENGTH) ** -0.5, 6.0, ((0, 4), (1, 8))),
        "w_gate": noise(key_of[5], (MODEL_WIDTH, FF), MODEL_WIDTH ** -0.5, 0.15625, ((0, 8), (1, 4))),
        "w_up": noise(key_of[6], (MODEL_WIDTH, FF), MODEL_WIDTH ** -0.5, 0.15625, ((0, 8), (1, 4))),
        "w_down": noise(key_of[7], (FF, MODEL_WIDTH), (FF // 4) ** -0.5, 0.1875, ((0, 4), (1, 8))),
        "norm_attn": jnp.clip(1.0 + 0.1 * jax.random.normal(key_of[8], (MODEL_WIDTH,), jnp.float32), 0.5, 1.5).astype(jnp.bfloat16),
        "norm_ffn": jnp.clip(1.0 + 0.1 * jax.random.normal(key_of[9], (MODEL_WIDTH,), jnp.float32), 0.5, 1.5).astype(jnp.bfloat16),
        "grad_out": noise(key_of[10], (TOKEN_COUNT, MODEL_WIDTH), 1.0, 6.0, ((0, 32),)),
    }


EPSILON = 1e-05
ROPE_BASE = 100000.0
MASKED = -1e+30

@jax.custom_vjp
def reduced_precision(v):
    return lax.optimization_barrier(v.astype(jnp.bfloat16)).astype(jnp.float32)

@jax.custom_vjp
def reduced_backward(v):
    return v

def low_keep(v):
    return (reduced_precision(v), None)

def low_pass(kept, grad):
    return (grad,)

def back_keep(v):
    return (v, None)

def back_low(kept, grad):
    return (reduced_precision(grad),)
reduced_precision.defvjp(low_keep, low_pass)
reduced_backward.defvjp(back_keep, back_low)

def matrix_product(left, right):
    return jnp.dot(left, right, precision=lax.Precision.HIGHEST, preferred_element_type=jnp.float32)

def rms_norm(values, gain):
    return values * lax.rsqrt(lax.optimization_barrier(jnp.mean(values * values, axis=-1, keepdims=True)) + EPSILON) * gain

def rope_tables(positions):
    half = HEAD_WIDTH // 2
    freq = ROPE_BASE ** (-(jnp.arange(half, dtype=jnp.float32) * 2.0) / HEAD_WIDTH)
    angle = positions.astype(jnp.float32)[:, None] * freq[None, :]
    return (jnp.cos(angle)[:, None, :], jnp.sin(angle)[:, None, :])

def rotate(values, cosine, sine):
    half = values.shape[-1] // 2
    first = values[..., :half]
    second = values[..., half:]
    return jnp.concatenate([first * cosine - second * sine, second * cosine + first * sine], axis=-1)

def attend_block(query_block, query_pos, keys, values):
    scores = jnp.einsum('qgrd,kgd->grqk', query_block, keys, precision=lax.Precision.HIGHEST) * HEAD_WIDTH ** (-0.5)
    scores = reduced_backward(scores)
    key_pos = jnp.arange(keys.shape[0], dtype=jnp.int32)
    valid = key_pos[None, :] <= query_pos[:, None]
    scores = jnp.where(valid, scores, MASKED)
    top = lax.optimization_barrier(jnp.max(scores, axis=-1, keepdims=True))
    expo = jnp.exp(scores - top)
    denom = lax.optimization_barrier(jnp.sum(expo, axis=-1, keepdims=True))
    weighted = reduced_backward(jnp.einsum('grqk,kgd->qgrd', reduced_precision(expo), values, precision=lax.Precision.HIGHEST))
    return weighted / jnp.transpose(denom, (2, 0, 1, 3))

def attend_one_sequence(inputs):
    query_sequence, key_seq, value_seq = inputs
    block_index = min(512, SEQUENCE_LENGTH)
    query_block_list = query_sequence.reshape(SEQUENCE_LENGTH // block_index, block_index, KEY_VALUE_HEADS, QUERY_HEAD_COUNT // KEY_VALUE_HEADS, HEAD_WIDTH)
    positions = jnp.arange(SEQUENCE_LENGTH, dtype=jnp.int32).reshape(SEQUENCE_LENGTH // block_index, block_index)
    saved_block = jax.checkpoint(attend_block)
    result = lax.map(lambda pair: saved_block(pair[0], pair[1], key_seq, value_seq), (query_block_list, positions))
    return result.reshape(SEQUENCE_LENGTH, QUERY_HEAD_COUNT * HEAD_WIDTH)

def forward(tokens, w_query, key_weight_matrix, value_weight_matrix, w_out, w_gate, w_up, w_down, norm_attn, norm_ffn):
    first_normed_state = reduced_precision(rms_norm(tokens, norm_attn))
    query_proj = reduced_backward(matrix_product(first_normed_state, w_query)).reshape(TOKEN_COUNT, QUERY_HEAD_COUNT, HEAD_WIDTH)
    key_projected = reduced_backward(matrix_product(first_normed_state, key_weight_matrix)).reshape(TOKEN_COUNT, KEY_VALUE_HEADS, HEAD_WIDTH)
    value_reduced = reduced_precision(reduced_backward(matrix_product(first_normed_state, value_weight_matrix))).reshape(TOKEN_COUNT, KEY_VALUE_HEADS, HEAD_WIDTH)
    positions = jnp.arange(TOKEN_COUNT, dtype=jnp.int32) % SEQUENCE_LENGTH
    cosine, sine = rope_tables(positions)
    query_rotated = reduced_precision(rotate(query_proj, cosine, sine))
    key_rotated = reduced_precision(rotate(key_projected, cosine, sine))
    sequence_count = TOKEN_COUNT // SEQUENCE_LENGTH
    attention_output = lax.map(attend_one_sequence, (query_rotated.reshape(sequence_count, SEQUENCE_LENGTH, KEY_VALUE_HEADS, QUERY_HEAD_COUNT // KEY_VALUE_HEADS, HEAD_WIDTH), key_rotated.reshape(sequence_count, SEQUENCE_LENGTH, KEY_VALUE_HEADS, HEAD_WIDTH), value_reduced.reshape(sequence_count, SEQUENCE_LENGTH, KEY_VALUE_HEADS, HEAD_WIDTH)))
    attention_output = attention_output.reshape(TOKEN_COUNT, QUERY_HEAD_COUNT * HEAD_WIDTH)
    branch_attn = reduced_backward(matrix_product(reduced_precision(attention_output), w_out))
    hidden_state = tokens + branch_attn
    normed_two = reduced_precision(rms_norm(hidden_state, norm_ffn))
    gate = reduced_backward(matrix_product(normed_two, w_gate))
    up_val = reduced_backward(matrix_product(normed_two, w_up))
    hidden = reduced_precision(jax.nn.silu(gate) * up_val)
    branch_ffn = reduced_backward(matrix_product(hidden, w_down))
    result = hidden_state + branch_ffn
    squares = jnp.stack([jnp.sum(result * result), jnp.sum(branch_attn * branch_attn), jnp.sum(branch_ffn * branch_ffn)])
    return (result, squares)

def reference(tokens, w_query, key_weight_matrix, value_weight_matrix, w_out, w_gate, w_up, w_down, norm_attn, norm_ffn, grad_out):
    params = tuple((v.astype(jnp.float32) for v in (tokens, w_query, key_weight_matrix, value_weight_matrix, w_out, w_gate, w_up, w_down, norm_attn, norm_ffn)))
    result, pullback, squares = jax.vjp(forward, *params, has_aux=True)
    grads = pullback(grad_out.astype(jnp.float32))
    rms_stats = jnp.sqrt(squares / (TOKEN_COUNT * MODEL_WIDTH))
    return (result.astype(jnp.bfloat16), grads[0].astype(jnp.bfloat16), grads[1], grads[2], grads[3], grads[4], grads[5], grads[6], grads[7], grads[8], grads[9], rms_stats)
```

```python
import functools
import jax
import jax.numpy as jnp
from jax import lax
from jax.experimental import pallas as pl
from jax.experimental.pallas import tpu as pltpu
from jax.sharding import Mesh, PartitionSpec as P

HEAD = 96
LANES = 128
SEQUENCE_LENGTH = 4096
SPANS = 4
EPSILON = 1e-05
ROPE_BASE = 100000.0
MASKED = -1e30
LOG2E = 1.4426950408889634
NT = (((1,), (1,)), ((), ()))
NN = (((1,), (0,)), ((), ()))
TN = (((0,), (0,)), ((), ()))
F32 = jnp.float32
BF16 = jnp.bfloat16
VMEM_LIMIT = 60 * 1024 * 1024


def mm(left, right, dims):
    return lax.dot_general(left, right, dims, preferred_element_type=F32)


def widen(piece):
    return jnp.concatenate([piece, jnp.zeros((piece.shape[0], LANES - HEAD), piece.dtype)], axis=1)


def swapped(value):
    half = HEAD // 2
    return jnp.concatenate([value[:, half:HEAD], value[:, :half]], axis=1)


def attend_kernel(ids, own0, own1, own2, own3, other, out0, out1, out2, out3, q_s, kv_s, o_s, lse_s, acc_s, vt_s, *, block, tile):
    z, t = ids[0], ids[1]
    c = lax.rem(t, 2)
    spans = 4
    rows_all = q_s.shape[0]
    for j, own in enumerate((own0, own1, own2, own3)):
        zj = z ^ j
        for r in range(spans):
            at = pl.multiple_of(((t ^ r) * spans + zj) * block, block)
            at_other = pl.multiple_of(((t ^ 1 ^ r) * spans + zj) * block, block)
            q_s[pl.ds(at, block), :] = widen(own[:, r * HEAD : (r + 1) * HEAD])
            kv_s[c, pl.ds(at, block), :] = widen(own[:, (spans + r) * HEAD : (spans + r + 1) * HEAD])
            kv_s[1 - c, pl.ds(at_other, block), :] = widen(other[j, :, r * HEAD : (r + 1) * HEAD])
    factor = HEAD ** (-0.5) * LOG2E
    is_count = lax.broadcasted_iota(jnp.int32, (tile, LANES), 1) == HEAD

    def values(i, _):
        rows = pl.ds(pl.multiple_of(i * tile, tile), tile)
        vals = kv_s[1, rows, :]
        vt_s[:, rows] = jnp.transpose(jnp.where(is_count, jnp.ones_like(vals), vals))
        return 0

    lax.fori_loop(0, rows_all // tile, values, 0)

    def step(query, j, before, mask):
        rows = pl.ds(pl.multiple_of(j * tile, tile), tile)
        scores = mm(kv_s[0, rows, :], query, NT) * factor
        if mask is not None:
            scores = jnp.where(mask, scores, MASKED)
        top = jnp.maximum(before, jnp.max(scores, axis=0, keepdims=True))
        expo = jnp.exp2(scores - top).astype(BF16)
        acc_s[...] = acc_s[...] * jnp.exp2(before - top) + mm(vt_s[:, rows], expo, NN)
        return top

    def row_block(i, _):
        at = pl.multiple_of(i * tile, tile)
        query = q_s[pl.ds(at, tile), :]
        acc_s[...] = jnp.zeros_like(acc_s)
        top = lax.fori_loop(0, i, lambda j, top: step(query, j, top, None), jnp.full((1, tile), MASKED, F32))
        mask = lax.broadcasted_iota(jnp.int32, (tile, tile), 0) <= lax.broadcasted_iota(jnp.int32, (tile, tile), 1)
        top = step(query, i, top, mask)
        acc = acc_s[...]
        denom = acc[HEAD : HEAD + 1, :]
        o_s[pl.ds(at, tile), :] = jnp.transpose(acc / denom).astype(BF16)
        lse_s[:, pl.ds(at, tile)] = jnp.broadcast_to(top + jnp.log2(denom), (8, tile))
        return 0

    lax.fori_loop(0, rows_all // tile, row_block, 0)
    for j, out in enumerate((out0, out1, out2, out3)):
        zj = z ^ j
        for r in range(spans):
            at = pl.multiple_of(((t ^ r) * spans + zj) * block, block)
            out[:, r * HEAD : (r + 1) * HEAD] = o_s[pl.ds(at, block), :HEAD]


VM = pl.BlockSpec(memory_space=pltpu.VMEM)
SM = pl.BlockSpec(memory_space=pltpu.SMEM)


def shape(dims, dtype=BF16):
    return jax.ShapeDtypeStruct(dims, dtype)


def params():
    return pltpu.CompilerParams(vmem_limit_bytes=VMEM_LIMIT)


def attend(ids, own, other, tile=1024):
    block = own[0].shape[0]
    rows = block * 16
    return pl.pallas_call(
        functools.partial(attend_kernel, block=block, tile=tile),
        out_shape=[shape((block, 4 * HEAD))] * 4
        + [shape((rows, LANES)), shape((2, rows, LANES)), shape((rows, LANES)), shape((8, rows), F32)],
        in_specs=[SM] + [VM] * 5,
        out_specs=[VM] * 8,
        scratch_shapes=[pltpu.VMEM((LANES, tile), F32), pltpu.VMEM((LANES, rows), BF16)],
        compiler_params=params(),
        cost_estimate=pl.CostEstimate(flops=int(8e9), bytes_accessed=int(8e6), transcendentals=int(9e6)),
        name="attend",
    )(ids, *own, other)


def attend_back_kernel(ids, q_s, kv_s, o_s, lse_s, cos_s, sin_s, g0, g1, g2, g3, dq0, dq1, dq2, dq3, dk_out, dv_out, g_s, qx_s, kx_s, delta_s, dq_s, dk_s, dv_s, *, block, tile):
    z, t = ids[0], ids[1]
    spans = 4
    rows_all = q_s.shape[0]
    tiles = rows_all // tile
    for j, piece in enumerate((g0, g1, g2, g3)):
        zj = z ^ j
        for r in range(spans):
            at = pl.multiple_of(((t ^ r) * spans + zj) * block, block)
            g_s[pl.ds(at, block), :] = widen(piece[:, r * HEAD : (r + 1) * HEAD])

    def prepare(i, _):
        at = pl.multiple_of(i * tile, tile)
        rows = pl.ds(at, tile)
        query = q_s[rows, :]
        keys = kv_s[0, rows, :]
        qx_s[rows, :LANES] = query
        qx_s[rows, LANES:] = widen(swapped(query))
        kx_s[rows, :LANES] = keys
        kx_s[rows, LANES:] = widen(swapped(keys))
        both = g_s[rows, :].astype(F32) * o_s[rows, :].astype(F32)
        delta = jnp.sum(both, axis=1, keepdims=True)
        delta_s[:, rows] = jnp.transpose(jnp.broadcast_to(delta, (tile, LANES)))[:8]
        dq_s[rows, :] = jnp.zeros((tile, 2 * LANES), F32)
        return 0

    lax.fori_loop(0, tiles, prepare, 0)
    factor = HEAD ** (-0.5) * LOG2E
    scale = HEAD ** (-0.5)

    def step(i, keys, vals, kx, mask):
        rows = pl.ds(pl.multiple_of(i * tile, tile), tile)
        query = qx_s[rows, :]
        grad = g_s[rows, :]
        scores = mm(keys, query[:, :LANES], NT) * factor - lse_s[:1, rows]
        if mask is not None:
            scores = jnp.where(mask, scores, MASKED)
        prob = jnp.exp2(scores)
        through = mm(vals, grad, NT)
        ds = (prob * (through - delta_s[:1, rows])).astype(BF16)
        dv_s[...] += mm(prob.astype(BF16), grad, NN)
        dk_s[...] += mm(ds, query, NN)
        dq_s[rows, :] += mm(ds, kx, TN)

    def column_block(j, _):
        rows = pl.ds(pl.multiple_of(j * tile, tile), tile)
        kx = kx_s[rows, :]
        keys = kx[:, :LANES]
        vals = kv_s[1, rows, :]
        dk_s[...] = jnp.zeros_like(dk_s)
        dv_s[...] = jnp.zeros_like(dv_s)
        mask = lax.broadcasted_iota(jnp.int32, (tile, tile), 0) <= lax.broadcasted_iota(jnp.int32, (tile, tile), 1)
        step(j, keys, vals, kx, mask)
        lax.fori_loop(j + 1, tiles, lambda i, _: (step(i, keys, vals, kx, None), 0)[1], 0)
        dk = dk_s[...] * scale
        dk_out[rows, :] = (dk[:, :LANES] * cos_s[rows, :] - dk[:, LANES:] * sin_s[rows, :]).astype(BF16)
        dv_out[rows, :] = dv_s[...].astype(BF16)
        return 0

    lax.fori_loop(0, tiles, column_block, 0)
    for j, out in enumerate((dq0, dq1, dq2, dq3)):
        zj = z ^ j
        for r in range(spans):
            rows = pl.ds(pl.multiple_of(((t ^ r) * spans + zj) * block, block), block)
            dq = dq_s[rows, :] * scale
            out[:, r * HEAD : (r + 1) * HEAD] = (
                dq[:, :LANES] * cos_s[rows, :] - dq[:, LANES:] * sin_s[rows, :]
            ).astype(BF16)[:, :HEAD]


def attend_back(ids, q, kv, o, lse, cosine, sine, grads, tile=1024):
    block = grads[0].shape[0]
    rows = block * 16
    return pl.pallas_call(
        functools.partial(attend_back_kernel, block=block, tile=tile),
        out_shape=[shape((block, 4 * HEAD))] * 4 + [shape((rows, LANES))] * 2,
        in_specs=[SM] + [VM] * 10,
        out_specs=[VM] * 6,
        scratch_shapes=[
            pltpu.VMEM((rows, LANES), BF16),
            pltpu.VMEM((rows, 2 * LANES), BF16),
            pltpu.VMEM((rows, 2 * LANES), BF16),
            pltpu.VMEM((8, rows), F32),
            pltpu.VMEM((rows, 2 * LANES), F32),
            pltpu.VMEM((tile, 2 * LANES), F32),
            pltpu.VMEM((tile, LANES), F32),
        ],
        compiler_params=params(),
        cost_estimate=pl.CostEstimate(flops=int(22e9), bytes_accessed=int(12e6), transcendentals=int(9e6)),
        name="attend_back",
    )(ids, q, kv, o, lse, cosine, sine, *grads)


def project_kernel(ids, x0, x1, x2, x3, a, cos_s, sin_s, *outs, block):
    z, t = ids[0], ids[1]
    is_value = lax.rem(t, 2) == 1
    for j, out in enumerate(outs):
        weights = a[z ^ j, : 2 * HEAD, :]
        for r, x in enumerate((x0, x1, x2, x3)):
            rows = pl.ds(pl.multiple_of(((t ^ r) * SPANS + z) * block, block), block)
            cosine, sine = cos_s[rows, :HEAD], sin_s[rows, :HEAD]
            made = mm(x[...], weights, NT)
            query, other = made[:, :HEAD], made[:, HEAD:]
            out[:, r * HEAD : (r + 1) * HEAD] = (query * cosine + swapped(query) * sine).astype(BF16)
            cosine = jnp.where(is_value, 1.0, cosine)
            sine = jnp.where(is_value, 0.0, sine)
            out[:, (SPANS + r) * HEAD : (SPANS + r + 1) * HEAD] = (
                other * cosine + swapped(other) * sine
            ).astype(BF16)


def project(ids, x, a, cosine, sine):
    block = x[0].shape[0]
    return pl.pallas_call(
        functools.partial(project_kernel, block=block),
        out_shape=[shape((block, 8 * HEAD))] * 4,
        in_specs=[SM] + [VM] * 7,
        out_specs=[VM] * 4,
        compiler_params=params(),
        cost_estimate=pl.CostEstimate(flops=int(3e9), bytes_accessed=int(10e6), transcendentals=0),
        name="project",
    )(ids, *x, a, cosine, sine)


def gathered_heads(pieces, att, block):
    for j, piece in enumerate(pieces):
        for r in range(SPANS):
            att[r * block : (r + 1) * block, j * HEAD : (j + 1) * HEAD] = piece[:, r * HEAD : (r + 1) * HEAD]


def out_kernel(ids, p0, p1, p2, p3, a, near, far, att, orel, *, block):
    z = ids[0]
    gathered_heads((p0, p1, p2, p3), att, block)
    for j in range(4):
        orel[j * HEAD : (j + 1) * HEAD, :] = a[z ^ j, 2 * HEAD :, :]
    for r in range(SPANS):
        made = mm(att[r * block : (r + 1) * block, :], orel[...], NN).astype(BF16)
        (far if r % 2 else near)[r // 2] = made


def out_project(ids, pieces, a):
    block, width = pieces[0].shape[0], a.shape[2]
    return pl.pallas_call(
        functools.partial(out_kernel, block=block),
        out_shape=[shape((2, block, width))] * 2 + [shape((4 * block, 4 * HEAD)), shape((4 * HEAD, width))],
        in_specs=[SM] + [VM] * 5,
        out_specs=[VM] * 4,
        compiler_params=params(),
        cost_estimate=pl.CostEstimate(flops=int(1.3e9), bytes_accessed=int(10e6), transcendentals=0),
        name="out_project",
    )(ids, *pieces, a)


def out_back_kernel(ids, g0, g1, g2, g3, att, orel, d0, d1, d2, d3, dout, *, block):
    z = ids[0]
    grads = (g0, g1, g2, g3)
    for r, grad in enumerate(grads):
        made = mm(grad[...], orel[...], NT).astype(BF16)
        for j, out in enumerate((d0, d1, d2, d3)):
            out[:, r * HEAD : (r + 1) * HEAD] = made[:, j * HEAD : (j + 1) * HEAD]
    total = None
    for r, grad in enumerate(grads):
        made = mm(att[r * block : (r + 1) * block, :], grad[...], TN)
        total = made if total is None else total + made
    for j in range(4):
        dout[z ^ j] = total[j * HEAD : (j + 1) * HEAD].astype(BF16)


def out_back(ids, grads, att, orel):
    block, width = grads[0].shape
    return pl.pallas_call(
        functools.partial(out_back_kernel, block=block),
        out_shape=[shape((block, 4 * HEAD))] * 4 + [shape((4, HEAD, width))],
        in_specs=[SM] + [VM] * 6,
        out_specs=[VM] * 5,
        compiler_params=params(),
        cost_estimate=pl.CostEstimate(flops=int(2.5e9), bytes_accessed=int(10e6), transcendentals=0),
        name="out_back",
    )(ids, *grads, att, orel)


def pack_kernel(ids, mine, theirs, k0, k1, k2, k3, *, block):
    z, t = ids[0], ids[1]
    for j, out in enumerate((k0, k1, k2, k3)):
        for r in range(SPANS):
            rows = pl.ds(pl.multiple_of(((t ^ r) * SPANS + (z ^ j)) * block, block), block)
            total = (mine[rows, :].astype(F32) + theirs[rows, :].astype(F32)).astype(BF16)
            out[:, r * HEAD : (r + 1) * HEAD] = total[:, :HEAD]


def pack(ids, mine, theirs):
    block = mine.shape[0] // 16
    return pl.pallas_call(
        functools.partial(pack_kernel, block=block),
        out_shape=[shape((block, 4 * HEAD))] * 4,
        in_specs=[SM] + [VM] * 2,
        out_specs=[VM] * 4,
        compiler_params=params(),
        cost_estimate=pl.CostEstimate(flops=int(1e6), bytes_accessed=int(3e6), transcendentals=0),
        name="pack",
    )(ids, mine, theirs)


def project_back_kernel(ids, q0, q1, q2, q3, k0, k1, k2, k3, x0, x1, x2, x3, a, near, far, da, d_s, a_s, *, block):
    z = ids[0]
    for j, (query, other) in enumerate(zip((q0, q1, q2, q3), (k0, k1, k2, k3))):
        for r in range(SPANS):
            rows = slice(r * block, (r + 1) * block)
            lanes = slice(r * HEAD, (r + 1) * HEAD)
            d_s[rows, 2 * j * HEAD : (2 * j + 1) * HEAD] = query[:, lanes]
            d_s[rows, (2 * j + 1) * HEAD : (2 * j + 2) * HEAD] = other[:, lanes]
        a_s[2 * j * HEAD : (2 * j + 2) * HEAD, :] = a[z ^ j, : 2 * HEAD, :]
    for r in range(SPANS):
        made = mm(d_s[r * block : (r + 1) * block, :], a_s[...], NN).astype(BF16)
        (far if r % 2 else near)[r // 2] = made
    total = None
    for r, x in enumerate((x0, x1, x2, x3)):
        made = mm(d_s[r * block : (r + 1) * block, :], x[...], TN)
        total = made if total is None else total + made
    for j in range(4):
        da[z ^ j] = total[2 * j * HEAD : (2 * j + 2) * HEAD].astype(BF16)


def project_back(ids, queries, others, x, a):
    block, width = x[0].shape
    return pl.pallas_call(
        functools.partial(project_back_kernel, block=block),
        out_shape=[shape((2, block, width))] * 2 + [shape((4, 2 * HEAD, width))],
        in_specs=[SM] + [VM] * 13,
        out_specs=[VM] * 3,
        scratch_shapes=[pltpu.VMEM((4 * block, 8 * HEAD), BF16), pltpu.VMEM((8 * HEAD, width), BF16)],
        compiler_params=params(),
        cost_estimate=pl.CostEstimate(flops=int(5e9), bytes_accessed=int(14e6), transcendentals=0),
        name="project_back",
    )(ids, *queries, *others, *x, a)


def swap(value, axis):
    return lax.ppermute(value, axis, [(0, 1), (1, 0)])


def gather_group(value):
    core = swap(value, "c")
    across = swap(value, "x")
    return value, core, across, swap(across, "c")


def scatter_group(near, far):
    total = near.astype(F32) + swap(far, "c").astype(F32)
    return total[0] + swap(total[1].astype(BF16), "x").astype(F32)


def exchange(pieces):
    count = lax.axis_size("z")
    return [pieces[0]] + [
        lax.ppermute(pieces[j], "z", [(i, i ^ j) for i in range(count)]) for j in range(1, count)
    ]


def unit(values):
    scale = lax.rsqrt(jnp.mean(values * values, axis=-1, keepdims=True) + EPSILON)
    return values * scale, scale


def unit_back(values, scale, grad):
    inner = jnp.mean(grad * values, axis=-1, keepdims=True)
    return scale * grad - values * (scale * scale * scale) * inner


def spread(payload):
    return lax.all_to_all(payload, ("x", "c"), split_axis=0, concat_axis=0, tiled=True)


def per_device(tokens, w_query, w_key, w_value, w_out, w_gate, w_up, w_down, norm_attn, norm_ffn, grad_out):
    sequences, count = lax.axis_size("y"), lax.axis_size("z")
    block, width = tokens.shape
    shard = w_query.shape[0]
    part = SPANS * shard
    z = lax.axis_index("z")
    t = lax.axis_index("x") * 2 + lax.axis_index("c")
    ids = jnp.stack([z, t]).astype(jnp.int32)
    rows_all = SEQUENCE_LENGTH
    units = w_gate.shape[1] // SPANS

    gain_attn = norm_attn.astype(F32)[:, None]
    gain_ffn = norm_ffn.astype(F32)[:, None]
    scaled_query = (w_query.astype(F32) * gain_attn).astype(BF16)
    scaled_key = (w_key.astype(F32) * gain_attn).astype(BF16)
    scaled_value = (w_value.astype(F32) * gain_attn).astype(BF16)
    scaled_gate = (w_gate.astype(F32) * gain_ffn).astype(BF16)
    scaled_up = (w_up.astype(F32) * gain_ffn).astype(BF16)

    by_query = scaled_query.T.reshape(SPANS, HEAD, shard)
    by_key = scaled_key.T.reshape(2, HEAD, shard)
    by_value = scaled_value.T.reshape(2, HEAD, shard)
    by_kv = jnp.stack([by_key[0], by_value[0], by_key[1], by_value[1]])
    payload = jnp.concatenate([by_query, by_kv, w_out.reshape(SPANS, HEAD, shard)], axis=1)
    payload = spread(payload).transpose(1, 0, 2).reshape(3 * HEAD, part)
    attn_weights = lax.all_gather(payload, ("y", "z"), axis=0, tiled=False)
    attn_weights = attn_weights.reshape(sequences, count, 3 * HEAD, part).transpose(1, 2, 0, 3)
    attn_weights = attn_weights.reshape(count, 3 * HEAD, width)

    resid = tokens.astype(F32)
    unit_one, scale_one = unit(resid)
    x_one = gather_group(unit_one.astype(BF16))

    payload = jnp.stack(
        [
            scaled_gate.reshape(shard, SPANS, units).transpose(1, 0, 2),
            scaled_up.reshape(shard, SPANS, units).transpose(1, 0, 2),
            w_down.T.reshape(shard, SPANS, units).transpose(1, 0, 2),
        ],
        axis=1,
    )
    payload = spread(payload).transpose(1, 0, 2, 3).reshape(3, part, units)
    ffn_weights = lax.all_gather(payload, ("y", "z"), axis=0, tiled=False)
    ffn_weights = ffn_weights.reshape(sequences, count, 3, part, units).transpose(2, 0, 3, 1, 4)
    ffn_weights = ffn_weights.reshape(3, width, count * units)
    grad_rows = jnp.concatenate(gather_group(grad_out), axis=0)

    lane = jnp.arange(LANES)
    angle = jnp.arange(rows_all, dtype=F32)[:, None] * (ROPE_BASE ** (-(lane % (HEAD // 2) * 2.0) / HEAD))[None, :]
    cosine = jnp.cos(angle)
    sine = jnp.sin(angle) * jnp.where(lane < HEAD // 2, -1.0, 1.0)

    made = project(ids, x_one, attn_weights, cosine, sine)
    made = exchange(made)
    other = swap(jnp.stack([piece[:, SPANS * HEAD :] for piece in made]), "c")
    *attended, q_seq, kv_seq, o_seq, lse = attend(ids, made, other)
    near, far, att, orel = out_project(ids, exchange(attended), attn_weights)
    branch_attn = scatter_group(near, far)
    state = resid + branch_attn
    unit_two, scale_two = unit(state)
    x_two = jnp.concatenate(gather_group(unit_two.astype(BF16)), axis=0)

    full_gate, full_up, full_down = ffn_weights
    gate = jnp.dot(x_two, full_gate, preferred_element_type=F32)
    up = jnp.dot(x_two, full_up, preferred_element_type=F32)
    sigma = jax.nn.sigmoid(gate)
    swish = gate * sigma
    hidden = (swish * up).astype(BF16)
    ffn_part = mm(hidden, full_down, NT).astype(BF16).reshape(SPANS, block, width)
    branch_ffn = scatter_group(ffn_part[0::2], ffn_part[1::2])
    result = state + branch_ffn

    grad_hidden = jnp.dot(grad_rows, full_down, preferred_element_type=F32)
    grad_gate_pre = (grad_hidden * up * (sigma * (1.0 + gate * (1.0 - sigma)))).astype(BF16)
    grad_up_pre = (grad_hidden * swish).astype(BF16)
    two_part = (mm(grad_gate_pre, full_gate, NT) + mm(grad_up_pre, full_up, NT)).astype(BF16)
    two_part = two_part.reshape(SPANS, block, width)
    grad_unit_two = scatter_group(two_part[0::2], two_part[1::2])
    grad_state = grad_out.astype(F32) + unit_back(state, scale_two, grad_unit_two)

    def settle(grads):
        grads = grads.reshape(3, sequences, part, count, units).transpose(1, 3, 0, 2, 4)
        grads = grads.reshape(sequences * count, 3, part, units)
        total = lax.psum_scatter(grads, ("y", "z"), scatter_dimension=0, tiled=False)
        total = spread(total.reshape(3, SPANS, shard, units).transpose(1, 0, 2, 3))
        return total.transpose(1, 2, 0, 3).reshape(3, shard, SPANS * units).astype(F32)

    grad_ffn = settle(
        jnp.stack(
            [
                mm(x_two, grad_gate_pre, TN).astype(BF16),
                mm(x_two, grad_up_pre, TN).astype(BF16),
                mm(grad_rows, hidden, TN).astype(BF16),
            ]
        )
    )

    g_state = gather_group(grad_state.astype(BF16))
    *grad_att, grad_out_w = out_back(ids, g_state, att, orel)
    *dq, dk, dv = attend_back(ids, q_seq, kv_seq, o_seq, lse, cosine, sine, exchange(grad_att))
    dq = exchange(dq)
    first = lax.axis_index("c") == 0
    keep, give = jnp.where(first, dk, dv), jnp.where(first, dv, dk)
    dkv = exchange(pack(ids, keep, swap(give, "c")))
    near, far, grad_qkv = project_back(ids, dq, dkv, x_one, attn_weights)
    grad_unit_one = scatter_group(near, far)
    grad_tokens = (grad_state + unit_back(resid, scale_one, grad_unit_one)).astype(BF16)

    grads = jnp.concatenate([grad_qkv, grad_out_w], axis=1)
    grads = grads.reshape(count, 3 * HEAD, sequences, part).transpose(2, 0, 1, 3)
    grads = grads.reshape(sequences * count, 3 * HEAD, part)
    total = lax.psum_scatter(grads, ("y", "z"), scatter_dimension=0, tiled=False)
    total = spread(total.reshape(3 * HEAD, SPANS, shard).transpose(1, 0, 2)).astype(F32)
    grad_query = total[:, :HEAD].reshape(SPANS * HEAD, shard).T
    grad_key = total[0::2, HEAD : 2 * HEAD].reshape(2 * HEAD, shard).T
    grad_value = total[1::2, HEAD : 2 * HEAD].reshape(2 * HEAD, shard).T
    grad_outproj = total[:, 2 * HEAD :].reshape(SPANS * HEAD, shard)

    gain_one = (
        jnp.sum(w_query.astype(F32) * grad_query, axis=1)
        + jnp.sum(w_key.astype(F32) * grad_key, axis=1)
        + jnp.sum(w_value.astype(F32) * grad_value, axis=1)
    )
    gain_two = jnp.sum(w_gate.astype(F32) * grad_ffn[0], axis=1) + jnp.sum(w_up.astype(F32) * grad_ffn[1], axis=1)
    gain_one, gain_two = lax.psum((gain_one, gain_two), "z")

    squares = jnp.stack([jnp.sum(result * result), jnp.sum(branch_attn * branch_attn), jnp.sum(branch_ffn * branch_ffn)])
    squares = lax.psum(squares, ("y", "x", "c", "z"))
    entries = block * width * sequences * SPANS * count
    return (
        result.astype(BF16),
        grad_tokens,
        grad_query * gain_attn,
        grad_key * gain_attn,
        grad_value * gain_attn,
        grad_outproj,
        grad_ffn[0] * gain_ffn,
        grad_ffn[1] * gain_ffn,
        grad_ffn[2].T,
        gain_one,
        gain_two,
        jnp.sqrt(squares / entries),
    )


def solution(mesh):
    fsdp, tensor = mesh.shape["fsdp"], mesh.shape["tensor"]
    split = Mesh(mesh.devices.reshape(fsdp // SPANS, 2, 2, tensor), ("y", "x", "c", "z"))
    rows = ("y", "x", "c")
    tok = P(("y", "x", "c", "z"), None)
    col, row, vec = P(rows, "z"), P("z", rows), P(rows)
    return jax.shard_map(
        per_device,
        mesh=split,
        in_specs=(tok, col, col, col, row, col, col, row, vec, vec, tok),
        out_specs=(tok, tok, col, col, col, row, col, col, row, vec, vec, P()),
        check_vma=False,
    )
```

```python
import functools
import jax
import jax.numpy as jnp
from jax import lax
from jax.experimental import pallas as pl
from jax.experimental.pallas import tpu as pltpu
from jax.sharding import Mesh, PartitionSpec as P

HEAD = 96
LANES = 128
SEQUENCE_LENGTH = 4096
SPANS = 4
EPSILON = 1e-05
ROPE_BASE = 100000.0
MASKED = -1e30
LOG2E = 1.4426950408889634
NT = (((1,), (1,)), ((), ()))
NN = (((1,), (0,)), ((), ()))
TN = (((0,), (0,)), ((), ()))
F32 = jnp.float32
BF16 = jnp.bfloat16
VMEM_LIMIT = 60 * 1024 * 1024


def mm(left, right, dims):
    return lax.dot_general(left, right, dims, preferred_element_type=F32)


def widen(piece):
    return jnp.concatenate([piece, jnp.zeros((piece.shape[0], LANES - HEAD), piece.dtype)], axis=1)


def swapped(value):
    half = HEAD // 2
    return jnp.concatenate([value[:, half:HEAD], value[:, :half]], axis=1)


def attend_kernel(ids, own, other, out, q_s, kv_s, o_s, lse_s, acc_s, vt_s, *, block, tile):
    z, t = ids[0], ids[1]
    c = lax.rem(t, 2)
    spans = 4
    rows_all = q_s.shape[0]
    for zj in range(4):
        for r in range(spans):
            at = pl.multiple_of(((t ^ r) * spans + zj) * block, block)
            at_other = pl.multiple_of(((t ^ 1 ^ r) * spans + zj) * block, block)
            q_s[pl.ds(at, block), :] = widen(own[zj, :, r * HEAD : (r + 1) * HEAD])
            kv_s[c, pl.ds(at, block), :] = widen(own[zj, :, (spans + r) * HEAD : (spans + r + 1) * HEAD])
            kv_s[1 - c, pl.ds(at_other, block), :] = widen(other[zj, :, r * HEAD : (r + 1) * HEAD])
    factor = HEAD ** (-0.5) * LOG2E
    is_count = lax.broadcasted_iota(jnp.int32, (tile, LANES), 1) == HEAD

    def values(i, _):
        rows = pl.ds(pl.multiple_of(i * tile, tile), tile)
        vals = kv_s[1, rows, :]
        vt_s[:, rows] = jnp.transpose(jnp.where(is_count, jnp.ones_like(vals), vals))
        return 0

    lax.fori_loop(0, rows_all // tile, values, 0)

    def step(query, j, before, mask):
        rows = pl.ds(pl.multiple_of(j * tile, tile), tile)
        scores = mm(kv_s[0, rows, :], query, NT) * factor
        if mask is not None:
            scores = jnp.where(mask, scores, MASKED)
        top = jnp.maximum(before, jnp.max(scores, axis=0, keepdims=True))
        expo = jnp.exp2(scores - top).astype(BF16)
        acc_s[...] = acc_s[...] * jnp.exp2(before - top) + mm(vt_s[:, rows], expo, NN)
        return top

    def row_block(i, _):
        at = pl.multiple_of(i * tile, tile)
        query = q_s[pl.ds(at, tile), :]
        acc_s[...] = jnp.zeros_like(acc_s)
        top = lax.fori_loop(0, i, lambda j, top: step(query, j, top, None), jnp.full((1, tile), MASKED, F32))
        mask = lax.broadcasted_iota(jnp.int32, (tile, tile), 0) <= lax.broadcasted_iota(jnp.int32, (tile, tile), 1)
        top = step(query, i, top, mask)
        acc = acc_s[...]
        denom = acc[HEAD : HEAD + 1, :]
        o_s[pl.ds(at, tile), :] = jnp.transpose(acc / denom).astype(BF16)
        lse_s[:, pl.ds(at, tile)] = jnp.broadcast_to(top + jnp.log2(denom), (8, tile))
        return 0

    lax.fori_loop(0, rows_all // tile, row_block, 0)
    for zj in range(4):
        for r in range(spans):
            at = pl.multiple_of(((t ^ r) * spans + zj) * block, block)
            out[zj, :, r * HEAD : (r + 1) * HEAD] = o_s[pl.ds(at, block), :HEAD]


VM = pl.BlockSpec(memory_space=pltpu.VMEM)
SM = pl.BlockSpec(memory_space=pltpu.SMEM)


def shape(dims, dtype=BF16):
    return jax.ShapeDtypeStruct(dims, dtype)


def params():
    return pltpu.CompilerParams(vmem_limit_bytes=VMEM_LIMIT)


def attend(ids, own, other, tile=1024):
    block = own.shape[1]
    rows = block * 16
    return pl.pallas_call(
        functools.partial(attend_kernel, block=block, tile=tile),
        out_shape=[shape((4, block, 4 * HEAD)), shape((rows, LANES)), shape((2, rows, LANES)), shape((rows, LANES)), shape((8, rows), F32)],
        in_specs=[SM] + [VM] * 2,
        out_specs=[VM] * 5,
        scratch_shapes=[pltpu.VMEM((LANES, tile), F32), pltpu.VMEM((LANES, rows), BF16)],
        compiler_params=params(),
        cost_estimate=pl.CostEstimate(flops=int(21e9), bytes_accessed=1, transcendentals=0),
        name="attend",
    )(ids, own, other)


def attend_back_kernel(ids, q_s, kv_s, o_s, lse_s, cos_s, sin_s, g, dq_out, keep_out, give_out, g_s, qx_s, kx_s, delta_s, dq_s, dk_s, dv_s, *, block, tile):
    z, t = ids[0], ids[1]
    spans = 4
    rows_all = q_s.shape[0]
    tiles = rows_all // tile
    for zj in range(4):
        for r in range(spans):
            at = pl.multiple_of(((t ^ r) * spans + zj) * block, block)
            g_s[pl.ds(at, block), :] = widen(g[zj, :, r * HEAD : (r + 1) * HEAD])

    def prepare(i, _):
        at = pl.multiple_of(i * tile, tile)
        rows = pl.ds(at, tile)
        query = q_s[rows, :]
        keys = kv_s[0, rows, :]
        qx_s[rows, :LANES] = query
        qx_s[rows, LANES:] = widen(swapped(query))
        kx_s[rows, :LANES] = keys
        kx_s[rows, LANES:] = widen(swapped(keys))
        both = g_s[rows, :].astype(F32) * o_s[rows, :].astype(F32)
        delta = jnp.sum(both, axis=1, keepdims=True)
        delta_s[:, rows] = jnp.transpose(jnp.broadcast_to(delta, (tile, LANES)))[:8]
        dq_s[rows, :] = jnp.zeros((tile, 2 * LANES), F32)
        return 0

    lax.fori_loop(0, tiles, prepare, 0)
    factor = HEAD ** (-0.5) * LOG2E
    scale = HEAD ** (-0.5)

    def step(i, keys, vals, kx, mask):
        rows = pl.ds(pl.multiple_of(i * tile, tile), tile)
        query = qx_s[rows, :]
        grad = g_s[rows, :]
        scores = mm(keys, query[:, :LANES], NT) * factor - lse_s[:1, rows]
        if mask is not None:
            scores = jnp.where(mask, scores, MASKED)
        prob = jnp.exp2(scores)
        through = mm(vals, grad, NT)
        ds = (prob * (through - delta_s[:1, rows])).astype(BF16)
        dv_s[...] += mm(prob.astype(BF16), grad, NN)
        dk_s[...] += mm(ds, query, NN)
        dq_s[rows, :] += mm(ds, kx, TN)

    def column_block(j, _):
        rows = pl.ds(pl.multiple_of(j * tile, tile), tile)
        kx = kx_s[rows, :]
        keys = kx[:, :LANES]
        vals = kv_s[1, rows, :]
        dk_s[...] = jnp.zeros_like(dk_s)
        dv_s[...] = jnp.zeros_like(dv_s)
        mask = lax.broadcasted_iota(jnp.int32, (tile, tile), 0) <= lax.broadcasted_iota(jnp.int32, (tile, tile), 1)
        step(j, keys, vals, kx, mask)
        lax.fori_loop(j + 1, tiles, lambda i, _: (step(i, keys, vals, kx, None), 0)[1], 0)
        dk = dk_s[...] * scale
        dk = dk[:, :LANES] * cos_s[rows, :] - dk[:, LANES:] * sin_s[rows, :]
        dv = dv_s[...]
        first = lax.rem(t, 2) == 0
        keep_out[rows, :] = jnp.where(first, dk, dv).astype(BF16)
        give_out[rows, :] = jnp.where(first, dv, dk).astype(BF16)
        return 0

    lax.fori_loop(0, tiles, column_block, 0)
    for zj in range(4):
        for r in range(spans):
            rows = pl.ds(pl.multiple_of(((t ^ r) * spans + zj) * block, block), block)
            dq = dq_s[rows, :] * scale
            dq_out[zj, :, r * HEAD : (r + 1) * HEAD] = (
                dq[:, :LANES] * cos_s[rows, :] - dq[:, LANES:] * sin_s[rows, :]
            ).astype(BF16)[:, :HEAD]


def attend_back(ids, q, kv, o, lse, cosine, sine, grads, tile=1024):
    block = grads.shape[1]
    rows = block * 16
    return pl.pallas_call(
        functools.partial(attend_back_kernel, block=block, tile=tile),
        out_shape=[shape((4, block, 4 * HEAD))] + [shape((rows, LANES))] * 2,
        in_specs=[SM] + [VM] * 7,
        out_specs=[VM] * 3,
        scratch_shapes=[
            pltpu.VMEM((rows, LANES), BF16),
            pltpu.VMEM((rows, 2 * LANES), BF16),
            pltpu.VMEM((rows, 2 * LANES), BF16),
            pltpu.VMEM((8, rows), F32),
            pltpu.VMEM((rows, 2 * LANES), F32),
            pltpu.VMEM((tile, 2 * LANES), F32),
            pltpu.VMEM((tile, LANES), F32),
        ],
        compiler_params=params(),
        cost_estimate=pl.CostEstimate(flops=int(39e9), bytes_accessed=1, transcendentals=0),
        name="attend_back",
    )(ids, q, kv, o, lse, cosine, sine, grads)


def offsets(ids, count, part):
    if count == 1:
        return [0]
    return [pl.multiple_of(ids[2] * part, LANES), pl.multiple_of((1 - ids[2]) * part, LANES)]


def call(kernel, outs, name, scratch=(), micros=0):
    def run(ids, *args):
        return pl.pallas_call(
            kernel,
            out_shape=[shape(*o) if isinstance(o[0], tuple) else shape(o) for o in outs],
            in_specs=[SM] + [VM] * len(args),
            out_specs=[VM] * len(outs),
            scratch_shapes=[pltpu.VMEM(*item) for item in scratch],
            compiler_params=params(),
            cost_estimate=pl.CostEstimate(flops=int(micros * 1e9) + 1, bytes_accessed=1, transcendentals=0),
            name=name,
        )(ids, *args)

    return run


def split(refs, *counts):
    refs = list(refs)
    groups = []
    for count in counts:
        groups.append(refs[:count])
        refs = refs[count:]
    return groups


def prepare_attn(ids, w_query, w_key, w_value, w_out, gain):
    shard = w_query.shape[0]

    def kernel(ids, query, key, value, out, gain, *refs):
        pieces, made = split(refs, SPANS, 1)
        made = made[0]
        scale = gain[...]

        def turned(ref, at):
            return jnp.transpose(ref[:, at * HEAD : (at + 1) * HEAD].astype(F32) * scale).astype(BF16)

        for place in range(SPANS):
            made[place, :HEAD] = turned(query, place)
            made[place, HEAD : 2 * HEAD] = turned(value if place % 2 else key, place // 2)
            made[place, 2 * HEAD :] = jnp.transpose(out[:, place * HEAD : (place + 1) * HEAD].astype(F32)).astype(BF16)
        for r in range(SPANS):
            pieces[r][...] = made[ids[1] ^ r]

    scratch = [((SPANS, 3 * HEAD, shard), BF16)]
    return call(kernel, [(3 * HEAD, shard)] * SPANS, "prepare_attn", scratch)(
        ids, w_query, w_key, w_value, w_out.T, gain
    )


def prepare_ffn(ids, w_gate, w_up, w_down, gain):
    shard = w_gate.shape[0]
    units = w_gate.shape[1] // SPANS

    def kernel(ids, gate, up, down, gain, *pieces):
        scale = gain[...]
        for r in range(SPANS):
            at = pl.multiple_of((ids[1] ^ r) * units, LANES)
            pieces[r][0] = (gate[:, pl.ds(at, units)].astype(F32) * scale).astype(BF16)
            pieces[r][1] = (up[:, pl.ds(at, units)].astype(F32) * scale).astype(BF16)
            pieces[r][2] = down[:, pl.ds(at, units)]

    return call(kernel, [(3, shard, units)] * SPANS, "prepare_ffn")(ids, w_gate, w_up, w_down.T, gain)


def distinct(items):
    arrays = list({id(item[0]): item[0] for item in items}.values())
    index = {id(array): i for i, array in enumerate(arrays)}

    def rows_of(refs, item, rows):
        return refs[index[id(item[0])]][(*item[1], rows)]

    return arrays, rows_of


def project(ids, x, weights, cosine, sine):
    block = x[0].shape[0]
    parts = len(weights[0])
    part = weights[0][0][0].shape[-1]
    arrays, rows_of = distinct([item for items in weights for item in items])
    first = slice(0, 2 * HEAD)

    def kernel(ids, *refs):
        xs, ws, (cos_s, sin_s), (out,) = split(refs, SPANS, len(arrays), 2, 1)
        z, t = ids[0], ids[1]
        at = offsets(ids, parts, part)
        is_value = lax.rem(t, 2) == 1
        for r, x in enumerate(xs):
            rows = pl.ds(pl.multiple_of(((t ^ r) * SPANS + z) * block, block), block)
            cosine, sine = cos_s[rows, :HEAD], sin_s[rows, :HEAD]
            cos_kv = jnp.where(is_value, 1.0, cosine)
            sin_kv = jnp.where(is_value, 0.0, sine)
            for k in range(4):
                made = sum(mm(x[:, pl.ds(at[p], part)], rows_of(ws, weights[k][p], first), NT) for p in range(parts))
                query, other = made[:, :HEAD], made[:, HEAD:]
                out[z ^ k, :, r * HEAD : (r + 1) * HEAD] = (query * cosine + swapped(query) * sine).astype(BF16)
                out[z ^ k, :, (SPANS + r) * HEAD : (SPANS + r + 1) * HEAD] = (
                    other * cos_kv + swapped(other) * sin_kv
                ).astype(BF16)

    return call(kernel, [(4, block, 8 * HEAD)], "project")(ids, *x, *arrays, cosine, sine)[0]


def out_project(ids, pieces, weights):
    block = pieces.shape[1]
    parts = len(weights[0])
    part = weights[0][0][0].shape[-1]
    width = parts * part
    arrays, rows_of = distinct([item for items in weights for item in items])

    def kernel(ids, *refs):
        (pieces,), ws, (near, far, att, orel) = split(refs, 1, len(arrays), 4)
        at = offsets(ids, parts, part)
        for j in range(4):
            for r in range(SPANS):
                att[r * block : (r + 1) * block, j * HEAD : (j + 1) * HEAD] = pieces[ids[0] ^ j, :, r * HEAD : (r + 1) * HEAD]
            for p in range(parts):
                orel[j * HEAD : (j + 1) * HEAD, pl.ds(at[p], part)] = rows_of(ws, weights[j][p], slice(2 * HEAD, 3 * HEAD))
        for r in (1, 3, 2, 0):
            made = mm(att[r * block : (r + 1) * block, :], orel[...], NN).astype(BF16)
            (far if r % 2 else near)[r // 2] = made

    outs = [(2, block, width)] * 2 + [(4 * block, 4 * HEAD), (4 * HEAD, width)]
    return call(kernel, outs, "out_project")(ids, pieces, *arrays)


def out_back(ids, grads, att, orel, parts):
    block, width = grads[0].shape
    part = width // parts

    def kernel(ids, *refs):
        gs, (att, orel), (ds,), douts, (g_s,) = split(refs, SPANS, 2, 1, parts, 1)
        at = offsets(ids, parts, part)
        for r, grad in enumerate(gs):
            g_s[r * block : (r + 1) * block, :] = grad[...]
        made = mm(g_s[...], orel[...], NT).astype(BF16)
        for r in range(SPANS):
            for j in range(4):
                ds[ids[0] ^ j, :, r * HEAD : (r + 1) * HEAD] = made[r * block : (r + 1) * block, j * HEAD : (j + 1) * HEAD]
        for p in range(parts):
            total = mm(att[...], g_s[:, pl.ds(at[p], part)], TN)
            for k in range(4):
                douts[p][k] = total[k * HEAD : (k + 1) * HEAD].astype(BF16)

    outs = [(4, block, 4 * HEAD)] + [(4, HEAD, part)] * parts
    made = call(kernel, outs, "out_back", [((4 * block, width), BF16)])(ids, *grads, att, orel)
    return made[0], made[1:]


def pack(ids, queries, mine, theirs):
    _, block, wide = queries.shape

    def kernel(ids, queries, mine, theirs, out):
        t = ids[1]
        for zj in range(4):
            out[zj, :, :wide] = queries[zj]
            for r in range(SPANS):
                rows = pl.ds(pl.multiple_of(((t ^ r) * SPANS + zj) * block, block), block)
                total = (mine[rows, :].astype(F32) + theirs[rows, :].astype(F32)).astype(BF16)
                out[zj, :, wide + r * HEAD : wide + (r + 1) * HEAD] = total[:, :HEAD]

    return call(kernel, [(4, block, 2 * wide)], "pack")(ids, queries, mine, theirs)[0]


def project_weights(ids, grads, x, parts):
    block, width = x[0].shape
    part = width // parts

    def kernel(ids, *refs):
        (grads,), xs, (d_out,), das, (x_s,) = split(refs, 1, SPANS, 1, 2 * parts, 1)
        at = offsets(ids, parts, part)
        for j in range(4):
            for r in range(SPANS):
                for half in range(2):
                    lanes = slice((half * SPANS + r) * HEAD, (half * SPANS + r + 1) * HEAD)
                    d_out[r * block : (r + 1) * block, (2 * j + half) * HEAD : (2 * j + half + 1) * HEAD] = grads[
                        ids[0] ^ j, :, lanes
                    ]
        for r, x in enumerate(xs):
            x_s[r * block : (r + 1) * block, :] = x[...]
        for p in reversed(range(parts)):
            total = mm(d_out[...], x_s[:, pl.ds(at[p], part)], TN)
            for k in range(4):
                das[2 * p + (k < 2)][k % 2] = total[2 * k * HEAD : (2 * k + 2) * HEAD].astype(BF16)

    outs = [(4 * block, 8 * HEAD)] + [(2, 2 * HEAD, part)] * (2 * parts)
    made = call(kernel, outs, "project_weights", [((4 * block, width), BF16)])(ids, grads, *x)
    return made[0], made[1:]


def project_tokens(ids, grads, weights):
    rows = grads.shape[0]
    block = rows // SPANS
    parts = len(weights[0])
    part = weights[0][0][0].shape[-1]
    width = parts * part
    arrays, rows_of = distinct([item for items in weights for item in items])

    def kernel(ids, *refs):
        (d_s,), ws, (near, far), (a_s,) = split(refs, 1, len(arrays), 2, 1)
        at = offsets(ids, parts, part)
        for j in range(4):
            for p in range(parts):
                a_s[2 * j * HEAD : (2 * j + 2) * HEAD, pl.ds(at[p], part)] = rows_of(ws, weights[j][p], slice(0, 2 * HEAD))
        for r in (1, 3, 2, 0):
            made = mm(d_s[r * block : (r + 1) * block, :], a_s[...], NN).astype(BF16)
            (far if r % 2 else near)[r // 2] = made

    scratch = [((8 * HEAD, width), BF16)]
    return call(kernel, [(2, block, width)] * 2, "project_tokens", scratch)(ids, grads, *arrays)


def feed(ids, x, grads, weights):
    block, width = x[0].shape
    part, units = weights[0][0].shape[-2:]
    parts = width // part
    rows, every = 2 * block, 4 * units
    arrays = list({id(item[0]): item[0] for item in weights}.values())
    index = {id(array): i for i, array in enumerate(arrays)}

    def kernel(ids, *refs):
        xs, gs, ws, ffn, two, (hid, dgate, dup), (x_s, g_s, w_s) = split(refs, 2, 2, len(arrays), 2, 2, 3, 3)
        at = [pl.multiple_of(place, LANES) for place in offsets(ids, parts, part)]
        for r in range(2):
            x_s[r * block : (r + 1) * block, :] = xs[r][...]
            g_s[r * block : (r + 1) * block, :] = gs[r][...]
        for array, where, m, k, p in weights:
            w_s[m, pl.ds(at[p], part), k * units : (k + 1) * units] = ws[index[id(array)]][where]

        def pair(i, _):
            lanes = pl.ds(pl.multiple_of(i * units, LANES), units)
            gate = mm(x_s[...], w_s[0, :, lanes], NN)
            up = mm(x_s[...], w_s[1, :, lanes], NN)
            back = mm(g_s[...], w_s[2, :, lanes], NN)
            sigma = 1.0 / (1.0 + jnp.exp(-gate))
            swish = gate * sigma
            hid[:, lanes] = (swish * up).astype(BF16)
            dup[:, lanes] = (back * swish).astype(BF16)
            dgate[:, lanes] = (back * up * (sigma * (1.0 + gate * (1.0 - sigma)))).astype(BF16)
            return 0

        lax.fori_loop(0, 4, pair, 0)
        cut = width // 2
        for p in range(2):
            lanes = slice(p * cut, (p + 1) * cut)
            made = mm(dgate[...], w_s[0, lanes], NT) + mm(dup[...], w_s[1, lanes], NT)
            for r in range(2):
                two[r][:, lanes] = made[r * block : (r + 1) * block].astype(BF16)
        for p in range(2):
            lanes = slice(p * cut, (p + 1) * cut)
            made = mm(hid[...], w_s[2, lanes], NT)
            for r in range(2):
                ffn[r][:, lanes] = made[r * block : (r + 1) * block].astype(BF16)

    outs = [(block, width)] * 4 + [(rows, every)] * 3
    scratch = [((rows, width), BF16), ((rows, width), BF16), ((3, width, every), BF16)]
    made = call(kernel, outs, "feed", scratch, 18)(ids, *x, *grads, *arrays)
    return made[:2], made[2:4], made[4:]


def feed_weights(ids, x, grads, near, far, parts):
    block, width = x[0].shape
    part = width // parts
    half, every = near[0].shape
    units = every // 4

    def kernel(ids, *refs):
        xs, gs, ns, fs, outs, (x_s, g_s, h_s) = split(refs, SPANS, SPANS, 3, 3, 4 * parts, 3)
        at = offsets(ids, parts, part)
        for slot, r in enumerate((0, 1, 2, 3)):
            x_s[slot * block : (slot + 1) * block, :] = xs[r][...]
            g_s[slot * block : (slot + 1) * block, :] = gs[r][...]
        for m in range(3):
            h_s[m, :half] = ns[m][...]
            h_s[m, half:] = fs[m][...]
        for p in reversed(range(parts)):
            for m, left in ((2, g_s), (0, x_s), (1, x_s)):
                side = h_s[{0: 1, 1: 2, 2: 0}[m]]
                total = mm(left[:, pl.ds(at[p], part)], side, TN)
                for k in range(4):
                    outs[k * parts + p][m] = total[:, k * units : (k + 1) * units].astype(BF16)

    outs = [(3, part, units)] * (4 * parts)
    scratch = [((4 * block, width), BF16), ((4 * block, width), BF16), ((3, 4 * block, every), BF16)]
    return call(kernel, outs, "feed_weights", scratch, 17)(ids, *x, *grads, *near, *far)


def finish_ffn(ids, pieces, w_gate, w_up, gain):
    _, shard, units = pieces[0].shape
    every = SPANS * units

    def kernel(ids, *refs):
        pieces, (w_gate, w_up, gain), (gate, up, down, sums) = split(refs, SPANS, 3, 4)
        scale = gain[...]
        total = jnp.zeros((shard, 1), F32)
        for r, piece in enumerate(pieces):
            lanes = pl.ds(pl.multiple_of((ids[1] ^ r) * units, LANES), units)
            for m, (out, weight) in enumerate(((gate, w_gate), (up, w_up))):
                grad = piece[m].astype(F32)
                out[:, lanes] = grad * scale
                total += jnp.sum(grad * weight[:, lanes].astype(F32), axis=1, keepdims=True)
            down[:, lanes] = piece[2].astype(F32)
        sums[...] = jnp.transpose(jnp.broadcast_to(total, (shard, LANES)))[:8]

    outs = [((shard, every), F32)] * 3 + [((8, shard), F32)]
    return call(kernel, outs, "finish_ffn")(ids, *pieces, w_gate, w_up, gain)


def finish_attn(ids, pieces, w_query, w_key, w_value, gain):
    shard = pieces[0].shape[1]

    def kernel(ids, *refs):
        pieces, (w_query, w_key, w_value, gain), (query, key, value, out_w, sums), (made,) = split(refs, SPANS, 4, 5, 1)
        scale = gain[...]
        for r, piece in enumerate(pieces):
            made[ids[1] ^ r] = piece[...].astype(F32)
        total = jnp.zeros((shard, 1), F32)
        for place in range(SPANS):
            out_w[:, place * HEAD : (place + 1) * HEAD] = jnp.transpose(made[place, 2 * HEAD :])
            for out, weight, at, rows in (
                (query, w_query, place, 0),
                (value if place % 2 else key, w_value if place % 2 else w_key, place // 2, HEAD),
            ):
                grad = jnp.transpose(made[place, rows : rows + HEAD])
                lanes = slice(at * HEAD, (at + 1) * HEAD)
                out[:, lanes] = grad * scale
                total += jnp.sum(grad * weight[:, lanes].astype(F32), axis=1, keepdims=True)
        sums[...] = jnp.transpose(jnp.broadcast_to(total, (shard, LANES)))[:8]

    outs = [((shard, 4 * HEAD), F32), ((shard, 2 * HEAD), F32), ((shard, 2 * HEAD), F32)]
    outs += [((shard, 4 * HEAD), F32), ((8, shard), F32)]
    scratch = [((SPANS, 3 * HEAD, shard), F32)]
    return call(kernel, outs, "finish_attn", scratch)(ids, *pieces, w_query, w_key, w_value, gain)


def swap(value, axis):
    return lax.ppermute(value, axis, [(0, 1), (1, 0)])


def sent(value, axis, bits):
    return lax.ppermute(value, axis, [(i, i ^ bits) for i in range(lax.axis_size(axis))])


def gather_group(value):
    core = swap(value, "c")
    across = swap(value, "x")
    return value, core, across, swap(across, "c")


def scatter_group(near, far):
    total = near.astype(F32) + swap(far, "c").astype(F32)
    return total[0] + swap(total[1].astype(BF16), "x").astype(F32)


def scatter_halves(near, far):
    far_total = far[0].astype(F32) + swap(far[1], "c").astype(F32)
    crossing = swap(far_total.astype(BF16), "x")
    return near[0].astype(F32) + swap(near[1], "c").astype(F32) + crossing.astype(F32)


def exchange(pieces):
    return lax.all_to_all(pieces, "z", split_axis=0, concat_axis=0, tiled=True)


def spread(pieces):
    return [
        pieces[0],
        swap(pieces[1], "c"),
        swap(pieces[2], "x"),
        lax.ppermute(pieces[3], ("x", "c"), [(i, 3 - i) for i in range(SPANS)]),
    ]


def by_place(pieces, t):
    stacked = jnp.stack(pieces)
    return jnp.stack([lax.dynamic_index_in_dim(stacked, t ^ place, 0, keepdims=False) for place in range(SPANS)])


def beside(mine, dim):
    if lax.axis_size("y") == 2:
        return [mine, swap(mine, "y")]
    return [lax.all_gather(mine, "y", axis=dim, tiled=True)]


def along_z(mine):
    if lax.axis_size("z") != 4:
        return [mine] + [sent(mine, "z", k) for k in range(1, lax.axis_size("z"))]
    far = sent(mine, "z", 3)
    return [mine, sent(mine, "z", 1), sent(far, "z", 1), far]


def onto_z(pieces):
    far = pieces[3].astype(F32) + sent(pieces[2], "z", 1).astype(F32)
    near = pieces[0].astype(F32) + sent(pieces[1], "z", 1).astype(F32)
    return (near + sent(far.astype(BF16), "z", 3).astype(F32)).astype(BF16)


def settled(pieces, parts, dim):
    if parts == 2:
        sums = [
            (pieces[2 * k].astype(F32) + swap(pieces[2 * k + 1], "y").astype(F32)).astype(BF16) for k in range(4)
        ]
    else:
        sums = [lax.psum_scatter(piece, "y", scatter_dimension=dim, tiled=True) for piece in pieces]
    return onto_z(sums)


def over_z(value):
    return value + sum(sent(value, "z", k) for k in range(1, lax.axis_size("z")))


def unit(values):
    scale = lax.rsqrt(jnp.mean(values * values, axis=-1, keepdims=True) + EPSILON)
    return values * scale, scale


def unit_back(values, scale, grad):
    inner = jnp.mean(grad * values, axis=-1, keepdims=True)
    return scale * grad - values * (scale * scale * scale) * inner


def per_device(tokens, w_query, w_key, w_value, w_out, w_gate, w_up, w_down, norm_attn, norm_ffn, grad_out):
    sequences, count = lax.axis_size("y"), lax.axis_size("z")
    parts = 2 if sequences == 2 else 1
    block, width = tokens.shape
    shard = w_query.shape[0]
    t = lax.axis_index("x") * 2 + lax.axis_index("c")
    ids = jnp.stack([lax.axis_index("z"), t, lax.axis_index("y")]).astype(jnp.int32)
    gain_attn = norm_attn.astype(F32)[:, None]
    gain_ffn = norm_ffn.astype(F32)[:, None]

    fence = lax.optimization_barrier

    resid = tokens.astype(F32)
    unit_one, scale_one = unit(resid)
    attn_pieces, low_one = fence((prepare_attn(ids, w_query, w_key, w_value, w_out, gain_attn), unit_one.astype(BF16)))
    attn_mine = by_place(spread(attn_pieces), t).transpose(1, 0, 2).reshape(3 * HEAD, SPANS * shard)
    lane = jnp.arange(LANES)
    freq = ROPE_BASE ** (-(lane % (HEAD // 2) * 2.0) / HEAD)
    inner = jnp.arange(block, dtype=F32)[:, None] * freq
    outer = (jnp.arange(SEQUENCE_LENGTH // block, dtype=F32) * block)[:, None] * freq
    cos_in, sin_in, cos_out, sin_out = jnp.cos(inner), jnp.sin(inner), jnp.cos(outer)[:, None], jnp.sin(outer)[:, None]
    cosine = (cos_out * cos_in - sin_out * sin_in).reshape(SEQUENCE_LENGTH, LANES)
    sine = (sin_out * cos_in + cos_out * sin_in).reshape(SEQUENCE_LENGTH, LANES)
    sine = sine * jnp.where(lane < HEAD // 2, -1.0, 1.0)
    attn_mine, ffn_pieces, cosine, sine, low_one = fence(
        (attn_mine, prepare_ffn(ids, w_gate, w_up, w_down, gain_ffn), cosine, sine, low_one)
    )

    attn_three, attn_one = sent(attn_mine, "z", 3), sent(attn_mine, "z", 1)
    own = beside(attn_mine, 1)
    ffn_mine = by_place(spread(ffn_pieces), t).transpose(1, 0, 2, 3).reshape(3, SPANS * shard, -1)
    core, across = swap(low_one, "c"), swap(low_one, "x")
    ffn_mine, attn_three, attn_one, own = fence((ffn_mine, attn_three, attn_one, own))
    attn_two = sent(attn_three, "z", 1)
    three_one = beside(jnp.stack([attn_three, attn_one]), 2)
    gate_three = sent(ffn_mine[0], "z", 3)
    attn_two, three_one, gate_three, ffn_mine, core, across = fence(
        (attn_two, three_one, gate_three, ffn_mine, core, across)
    )
    x_one = (low_one, core, across, swap(across, "c"))
    two = beside(attn_two, 1)
    attn_weights = [
        [(array, ()) for array in own],
        [(array, (1,)) for array in three_one],
        [(array, ()) for array in two],
        [(array, (0,)) for array in three_one],
    ]
    gate_one, up_three = sent(ffn_mine[0], "z", 1), sent(ffn_mine[1], "z", 3)
    made = project(ids, x_one, attn_weights, cosine, sine)
    made, gate_one, up_three, gate_three, ffn_mine, grad_in = fence(
        (made, gate_one, up_three, gate_three, ffn_mine, grad_out)
    )

    made = exchange(made)
    ffn_own = beside(ffn_mine, 1)
    g_rows = gather_group(grad_in)
    by_one = jnp.stack([ffn_mine[1], gate_three])
    gate_three_one = jnp.stack([gate_three, gate_one])
    made, ffn_own, g_rows, by_one, gate_three_one, down_mine = fence(
        (made, ffn_own, g_rows, by_one, gate_three_one, ffn_mine[2])
    )
    down_three, by_one = sent(down_mine, "z", 3), sent(by_one, "z", 1)
    gate_three_one = beside(gate_three_one, 1)
    other = swap(made[:, :, SPANS * HEAD :], "c")
    attended, q_seq, kv_seq, o_seq, lse = attend(ids, made, other)
    attended, down_three, by_one, gate_three_one, up_three = fence(
        (attended, down_three, by_one, gate_three_one, up_three)
    )
    attended = exchange(attended)
    up_three_one = beside(jnp.stack([up_three, by_one[0]]), 1)
    last_one = jnp.stack([down_mine, up_three, down_three])
    down_three_gate_two = jnp.stack([down_three, by_one[1]])
    attended, up_three_one, last_one, down_three_gate_two = fence(
        (attended, up_three_one, last_one, down_three_gate_two)
    )
    last_one = sent(last_one, "z", 1)
    down_three_gate_two = beside(down_three_gate_two, 1)
    near, far, att, orel = out_project(ids, attended, attn_weights)
    branch_attn = scatter_group(near, far)
    state = resid + branch_attn
    unit_two, scale_two = unit(state)
    low_two, last_one, down_three_gate_two = fence((unit_two.astype(BF16), last_one, down_three_gate_two))
    x_two = gather_group(low_two)
    last_one = beside(last_one, 1)
    x_two, last_one = fence((x_two, last_one))

    ffn_weights = []
    for p in range(parts):
        ffn_weights += [(ffn_own[p], (m,), m, 0, p) for m in range(3)]
        ffn_weights += [(gate_three_one[p], (0,), 0, 3, p), (gate_three_one[p], (1,), 0, 1, p)]
        ffn_weights += [(up_three_one[p], (0,), 1, 3, p), (up_three_one[p], (1,), 1, 1, p)]
        ffn_weights += [(down_three_gate_two[p], (0,), 2, 3, p), (down_three_gate_two[p], (1,), 0, 2, p)]
        ffn_weights += [(last_one[p], (i,), *place, p) for i, place in enumerate(((2, 1), (1, 2), (2, 2)))]
    ffn_far, two_far, kept_far = feed(ids, x_two[2:], g_rows[2:], ffn_weights)
    crossing = (two_far[0].astype(F32) + swap(two_far[1], "c").astype(F32)).astype(BF16)
    crossing, x_near = fence((crossing, x_two[:2]))
    crossing = swap(crossing, "x")
    ffn_near, two_near, kept_near = feed(ids, x_near, g_rows[:2], ffn_weights)
    two_near, crossing = fence((two_near, crossing))
    grad_unit_two = two_near[0].astype(F32) + swap(two_near[1], "c").astype(F32) + crossing.astype(F32)
    grad_state = grad_out.astype(F32) + unit_back(state, scale_two, grad_unit_two)
    state_low, kept_near, ffn_near, ffn_far = fence((grad_state.astype(BF16), kept_near, ffn_near, ffn_far))
    across, core = swap(state_low, "x"), swap(state_low, "c")
    feed_grads = feed_weights(ids, x_two, g_rows, kept_near, kept_far, parts)
    across, core, feed_grads = fence((across, core, feed_grads))
    g_state = (state_low, core, across, swap(across, "c"))

    def home(total):
        pieces = total.reshape(*total.shape[:-2], SPANS, shard, total.shape[-1])
        return spread([lax.dynamic_index_in_dim(pieces, t ^ r, pieces.ndim - 3, keepdims=False) for r in range(SPANS)])

    def home_lanes(total):
        pieces = total.reshape(total.shape[0], SPANS, shard)
        return spread([lax.dynamic_index_in_dim(pieces, t ^ r, 1, keepdims=False) for r in range(SPANS)])

    def crossed(grads, k):
        if parts == 1:
            return lax.psum_scatter(grads[k], "y", scatter_dimension=1, tiled=True)
        return swap(grads[2 * k + 1], "y")

    def added(grads, k, came):
        return came if parts == 1 else (grads[2 * k].astype(F32) + came.astype(F32)).astype(BF16)

    two_came = crossed(feed_grads, 2)
    grad_att, out_grads = out_back(ids, g_state, att, orel, parts)
    grad_att = exchange(grad_att)
    grad_att, two_came, feed_grads, out_grads = fence((grad_att, two_came, feed_grads, out_grads))
    onward = sent(added(feed_grads, 2, two_came), "z", 1)
    three_came = crossed(feed_grads, 3)
    if parts == 2:
        out_sums = out_grads[0].astype(F32) + swap(out_grads[1], "y").astype(F32)
    else:
        out_sums = lax.psum_scatter(out_grads[0], "y", scatter_dimension=2, tiled=True)
    dq, keep, give = attend_back(ids, q_seq, kv_seq, o_seq, lse, cosine, sine, grad_att)
    dq, keep, give, onward, three_came, feed_grads, ffn_near, ffn_far, out_sums = fence(
        (dq, keep, give, onward, three_came, feed_grads, ffn_near, ffn_far, out_sums.astype(BF16))
    )
    one_came = crossed(feed_grads, 1)
    grads_heads = exchange(pack(ids, dq, keep, swap(give, "c")))
    branch_ffn = scatter_halves(ffn_near, ffn_far)
    result = state + branch_ffn
    squares = jnp.stack([jnp.sum(result * result), jnp.sum(branch_attn * branch_attn), jnp.sum(branch_ffn * branch_ffn)])
    squares = squares + swap(squares, "c")
    squares = squares + swap(squares, "x")
    onward = (added(feed_grads, 3, three_came).astype(F32) + onward.astype(F32)).astype(BF16)
    onward, onward_down = onward[:2], onward[2:]
    one_sum = added(feed_grads, 1, one_came)
    grads_heads, result, squares, onward, onward_down, one_sum, feed_grads = fence(
        (grads_heads, result, squares, onward, onward_down, one_sum, feed_grads)
    )
    onward = sent(onward, "z", 3)
    grads_qkv, qkv_grads = project_weights(ids, grads_heads, x_one, parts)
    grads_qkv, qkv_grads = fence((grads_qkv, qkv_grads))
    near, far = project_tokens(ids, grads_qkv, attn_weights)
    if parts == 2:
        late, early = (kept.astype(F32) + swap(gone, "y").astype(F32) for kept, gone in zip(qkv_grads[:2], qkv_grads[2:]))
    else:
        late, early = (lax.psum_scatter(piece, "y", scatter_dimension=2, tiled=True) for piece in qkv_grads)
    sums = [early[0], early[1], late[0], late[1]]
    sums = [jnp.concatenate([sums[k].astype(BF16), out_sums[k]], axis=0) for k in range(4)]
    sums, feed_grads, onward, onward_down = fence((sums, feed_grads, onward, onward_down))
    onward_down = sent(onward_down, "z", 3)
    own_came = crossed(feed_grads, 0)
    onto_three = (sums[3].astype(F32) + sent(sums[2], "z", 1).astype(F32)).astype(BF16)
    onto_one = sent(sums[1], "z", 1)
    total = near.astype(F32) + swap(far, "c").astype(F32)
    onto_three, onto_one, total, onward_down, one_sum = fence((onto_three, onto_one, total, onward_down, one_sum))
    onto_three = sent(onto_three, "z", 3)
    feed_one = sent(one_sum, "z", 1)
    crossing = swap(total[1].astype(BF16), "x")
    feed_total = added(feed_grads, 0, own_came).astype(F32) + jnp.concatenate([onward, onward_down]).astype(F32)
    feed_total = feed_total + feed_one.astype(F32)
    squares = squares + swap(squares, "y") if parts == 2 else lax.psum(squares, "y")
    onto_three, crossing, feed_total = fence((onto_three, crossing, feed_total.astype(BF16)))
    attn_total = sums[0].astype(F32) + onto_one.astype(F32) + onto_three.astype(F32)
    grad_unit_one = total[0] + crossing.astype(F32)
    grad_tokens = (grad_state + unit_back(resid, scale_one, grad_unit_one)).astype(BF16)
    grad_gate, grad_up, grad_down, gain_two = finish_ffn(ids, home(feed_total), w_gate, w_up, gain_ffn)
    grad_query, grad_key, grad_value, grad_outproj, gain_one = finish_attn(
        ids, home_lanes(attn_total.astype(BF16)), w_query, w_key, w_value, gain_attn
    )
    sums = over_z(jnp.concatenate([gain_one[0], gain_two[0], squares]))
    entries = block * width * sequences * SPANS * count
    return (
        result.astype(BF16),
        grad_tokens,
        grad_query,
        grad_key,
        grad_value,
        grad_outproj.T,
        grad_gate,
        grad_up,
        grad_down.T,
        sums[:shard],
        sums[shard : 2 * shard],
        jnp.sqrt(sums[2 * shard :] / entries),
    )


def solution(mesh):
    fsdp, tensor = mesh.shape["fsdp"], mesh.shape["tensor"]
    split = Mesh(mesh.devices.reshape(fsdp // SPANS, 2, 2, tensor), ("y", "x", "c", "z"))
    rows = ("y", "x", "c")
    tok = P(("y", "x", "c", "z"), None)
    col, row, vec = P(rows, "z"), P("z", rows), P(rows)
    return jax.shard_map(
        per_device,
        mesh=split,
        in_specs=(tok, col, col, col, row, col, col, row, vec, vec, tok),
        out_specs=(tok, tok, col, col, col, row, col, col, row, vec, vec, P()),
        check_vma=False,
    )
```

```python
import functools
import jax
import jax.numpy as jnp
from jax import lax
from jax.experimental import pallas as pl
from jax.experimental.pallas import tpu as pltpu
from jax.sharding import Mesh, PartitionSpec as P

HEAD = 96
LANES = 128
SEQUENCE_LENGTH = 4096
SPANS = 4
EPSILON = 1e-05
ROPE_BASE = 100000.0
MASKED = -1e30
LOG2E = 1.4426950408889634
NT = (((1,), (1,)), ((), ()))
NN = (((1,), (0,)), ((), ()))
TN = (((0,), (0,)), ((), ()))
F32 = jnp.float32
BF16 = jnp.bfloat16


def mm(left, right, dims):
    return lax.dot_general(left, right, dims, preferred_element_type=F32)


def widen(piece):
    return jnp.concatenate([piece, jnp.zeros((piece.shape[0], LANES - HEAD), piece.dtype)], axis=1)


def swapped(value):
    half = HEAD // 2
    return jnp.concatenate([value[:, half:HEAD], value[:, :half]], axis=1)


def attend_kernel(ids, own, other, out, q_s, kv_s, o_s, lse_s, acc_s, vt_s, *, block, tile):
    z, t = ids[0], ids[1]
    c = lax.rem(t, 2)
    spans = 4
    rows_all = q_s.shape[0]
    for zj in range(4):
        for r in range(spans):
            at = pl.multiple_of(((t ^ r) * spans + zj) * block, block)
            at_other = pl.multiple_of(((t ^ 1 ^ r) * spans + zj) * block, block)
            q_s[pl.ds(at, block), :] = widen(own[zj, :, r * HEAD : (r + 1) * HEAD])
            kv_s[c, pl.ds(at, block), :] = widen(own[zj, :, (spans + r) * HEAD : (spans + r + 1) * HEAD])
            kv_s[1 - c, pl.ds(at_other, block), :] = widen(other[zj, :, r * HEAD : (r + 1) * HEAD])
    factor = HEAD ** (-0.5) * LOG2E
    is_count = lax.broadcasted_iota(jnp.int32, (tile, LANES), 1) == HEAD

    def values(i, _):
        rows = pl.ds(pl.multiple_of(i * tile, tile), tile)
        vals = kv_s[1, rows, :]
        vt_s[:, rows] = jnp.transpose(jnp.where(is_count, jnp.ones_like(vals), vals))
        return 0

    lax.fori_loop(0, rows_all // tile, values, 0)

    def step(query, j, before, mask):
        rows = pl.ds(pl.multiple_of(j * tile, tile), tile)
        scores = mm(kv_s[0, rows, :], query, NT) * factor
        if mask is not None:
            scores = jnp.where(mask, scores, MASKED)
        top = jnp.maximum(before, jnp.max(scores, axis=0, keepdims=True))
        expo = jnp.exp2(scores - top).astype(BF16)
        acc_s[...] = acc_s[...] * jnp.exp2(before - top) + mm(vt_s[:, rows], expo, NN)
        return top

    def row_block(i, _):
        at = pl.multiple_of(i * tile, tile)
        query = q_s[pl.ds(at, tile), :]
        acc_s[...] = jnp.zeros_like(acc_s)
        top = lax.fori_loop(0, i, lambda j, top: step(query, j, top, None), jnp.full((1, tile), MASKED, F32))
        mask = lax.broadcasted_iota(jnp.int32, (tile, tile), 0) <= lax.broadcasted_iota(jnp.int32, (tile, tile), 1)
        top = step(query, i, top, mask)
        acc = acc_s[...]
        denom = acc[HEAD : HEAD + 1, :]
        o_s[pl.ds(at, tile), :] = jnp.transpose(acc / denom).astype(BF16)
        lse_s[:, pl.ds(at, tile)] = jnp.broadcast_to(top + jnp.log2(denom), (8, tile))
        return 0

    lax.fori_loop(0, rows_all // tile, row_block, 0)
    for zj in range(4):
        for r in range(spans):
            at = pl.multiple_of(((t ^ r) * spans + zj) * block, block)
            out[zj, :, r * HEAD : (r + 1) * HEAD] = o_s[pl.ds(at, block), :HEAD]


VM = pl.BlockSpec(memory_space=pltpu.VMEM)
SM = pl.BlockSpec(memory_space=pltpu.SMEM)


def shape(dims, dtype=BF16):
    return jax.ShapeDtypeStruct(dims, dtype)


def params(room):
    return pltpu.CompilerParams(vmem_limit_bytes=room * 1024 * 1024)


def attend(ids, own, other, tile=1024):
    block = own.shape[1]
    rows = block * 16
    return pl.pallas_call(
        functools.partial(attend_kernel, block=block, tile=tile),
        out_shape=[shape((4, block, 4 * HEAD)), shape((rows, LANES)), shape((2, rows, LANES)), shape((rows, LANES)), shape((8, rows), F32)],
        in_specs=[SM] + [VM] * 2,
        out_specs=[VM] * 5,
        scratch_shapes=[pltpu.VMEM((LANES, tile), F32), pltpu.VMEM((LANES, rows), BF16)],
        compiler_params=params(30),
        cost_estimate=pl.CostEstimate(flops=int(21e9), bytes_accessed=1, transcendentals=0),
        name="attend",
    )(ids, own, other)


def attend_back_kernel(ids, q_s, kv_s, o_s, lse_s, cos_s, sin_s, g, dq_out, keep_out, give_out, g_s, qx_s, kx_s, delta_s, dq_s, dk_s, dv_s, *, block, tile):
    z, t = ids[0], ids[1]
    spans = 4
    rows_all = q_s.shape[0]
    tiles = rows_all // tile
    for zj in range(4):
        for r in range(spans):
            at = pl.multiple_of(((t ^ r) * spans + zj) * block, block)
            g_s[pl.ds(at, block), :] = widen(g[zj, :, r * HEAD : (r + 1) * HEAD])

    def prepare(i, _):
        at = pl.multiple_of(i * tile, tile)
        rows = pl.ds(at, tile)
        query = q_s[rows, :]
        keys = kv_s[0, rows, :]
        qx_s[rows, :LANES] = query
        qx_s[rows, LANES:] = widen(swapped(query))
        kx_s[rows, :LANES] = keys
        kx_s[rows, LANES:] = widen(swapped(keys))
        both = g_s[rows, :].astype(F32) * o_s[rows, :].astype(F32)
        delta = jnp.sum(both, axis=1, keepdims=True)
        delta_s[:, rows] = jnp.transpose(jnp.broadcast_to(delta, (tile, LANES)))[:8]
        dq_s[rows, :] = jnp.zeros((tile, 2 * LANES), F32)
        return 0

    lax.fori_loop(0, tiles, prepare, 0)
    factor = HEAD ** (-0.5) * LOG2E
    scale = HEAD ** (-0.5)

    def step(i, keys, vals, kx, mask):
        rows = pl.ds(pl.multiple_of(i * tile, tile), tile)
        query = qx_s[rows, :]
        grad = g_s[rows, :]
        scores = mm(keys, query[:, :LANES], NT) * factor - lse_s[:1, rows]
        if mask is not None:
            scores = jnp.where(mask, scores, MASKED)
        prob = jnp.exp2(scores)
        through = mm(vals, grad, NT)
        ds = (prob * (through - delta_s[:1, rows])).astype(BF16)
        dv_s[...] += mm(prob.astype(BF16), grad, NN)
        dk_s[...] += mm(ds, query, NN)
        dq_s[rows, :] += mm(ds, kx, TN)

    def column_block(j, _):
        rows = pl.ds(pl.multiple_of(j * tile, tile), tile)
        kx = kx_s[rows, :]
        keys = kx[:, :LANES]
        vals = kv_s[1, rows, :]
        dk_s[...] = jnp.zeros_like(dk_s)
        dv_s[...] = jnp.zeros_like(dv_s)
        mask = lax.broadcasted_iota(jnp.int32, (tile, tile), 0) <= lax.broadcasted_iota(jnp.int32, (tile, tile), 1)
        step(j, keys, vals, kx, mask)
        lax.fori_loop(j + 1, tiles, lambda i, _: (step(i, keys, vals, kx, None), 0)[1], 0)
        dk = dk_s[...] * scale
        dk = dk[:, :LANES] * cos_s[rows, :] - dk[:, LANES:] * sin_s[rows, :]
        dv = dv_s[...]
        first = lax.rem(t, 2) == 0
        keep_out[rows, :] = jnp.where(first, dk, dv).astype(BF16)
        give_out[rows, :] = jnp.where(first, dv, dk).astype(BF16)
        return 0

    lax.fori_loop(0, tiles, column_block, 0)
    for zj in range(4):
        for r in range(spans):
            rows = pl.ds(pl.multiple_of(((t ^ r) * spans + zj) * block, block), block)
            dq = dq_s[rows, :] * scale
            dq_out[zj, :, r * HEAD : (r + 1) * HEAD] = (
                dq[:, :LANES] * cos_s[rows, :] - dq[:, LANES:] * sin_s[rows, :]
            ).astype(BF16)[:, :HEAD]


def attend_back(ids, q, kv, o, lse, cosine, sine, grads, tile=1024):
    block = grads.shape[1]
    rows = block * 16
    return pl.pallas_call(
        functools.partial(attend_back_kernel, block=block, tile=tile),
        out_shape=[shape((4, block, 4 * HEAD))] + [shape((rows, LANES))] * 2,
        in_specs=[SM] + [VM] * 7,
        out_specs=[VM] * 3,
        scratch_shapes=[
            pltpu.VMEM((rows, LANES), BF16),
            pltpu.VMEM((rows, 2 * LANES), BF16),
            pltpu.VMEM((rows, 2 * LANES), BF16),
            pltpu.VMEM((8, rows), F32),
            pltpu.VMEM((rows, 2 * LANES), F32),
            pltpu.VMEM((tile, 2 * LANES), F32),
            pltpu.VMEM((tile, LANES), F32),
        ],
        compiler_params=params(48),
        cost_estimate=pl.CostEstimate(flops=int(39e9), bytes_accessed=1, transcendentals=0),
        name="attend_back",
    )(ids, q, kv, o, lse, cosine, sine, grads)


def offsets(ids, count, part):
    if count == 1:
        return [0]
    return [pl.multiple_of(ids[2] * part, LANES), pl.multiple_of((1 - ids[2]) * part, LANES)]


def call(kernel, outs, name, scratch=(), micros=0, room=20):
    def run(ids, *args):
        return pl.pallas_call(
            kernel,
            out_shape=[shape(*o) if isinstance(o[0], tuple) else shape(o) for o in outs],
            in_specs=[SM] + [VM] * len(args),
            out_specs=[VM] * len(outs),
            scratch_shapes=[pltpu.VMEM(*item) for item in scratch],
            compiler_params=params(room),
            cost_estimate=pl.CostEstimate(flops=int(micros * 1e9) + 1, bytes_accessed=1, transcendentals=0),
            name=name,
        )(ids, *args)

    return run


def split(refs, *counts):
    refs = list(refs)
    groups = []
    for count in counts:
        groups.append(refs[:count])
        refs = refs[count:]
    return groups


def prepare_attn(ids, w_query, w_key, w_value, w_out, gain):
    shard = w_query.shape[0]

    def kernel(ids, query, key, value, out, gain, *refs):
        pieces, made = split(refs, SPANS, 1)
        made = made[0]
        scale = gain[...]

        def turned(ref, at):
            return jnp.transpose(ref[:, at * HEAD : (at + 1) * HEAD].astype(F32) * scale).astype(BF16)

        for place in range(SPANS):
            made[place, :HEAD] = turned(query, place)
            made[place, HEAD : 2 * HEAD] = turned(value if place % 2 else key, place // 2)
            made[place, 2 * HEAD :] = jnp.transpose(out[:, place * HEAD : (place + 1) * HEAD].astype(F32)).astype(BF16)
        for r in range(SPANS):
            pieces[r][...] = made[ids[1] ^ r]

    scratch = [((SPANS, 3 * HEAD, shard), BF16)]
    return call(kernel, [(3 * HEAD, shard)] * SPANS, "prepare_attn", scratch)(
        ids, w_query, w_key, w_value, w_out.T, gain
    )


def prepare_ffn(ids, w_gate, w_up, w_down, gain):
    shard = w_gate.shape[0]
    units = w_gate.shape[1] // SPANS

    def kernel(ids, gate, up, down, gain, *pieces):
        scale = gain[...]
        for r in range(SPANS):
            at = pl.multiple_of((ids[1] ^ r) * units, LANES)
            pieces[r][0] = (gate[:, pl.ds(at, units)].astype(F32) * scale).astype(BF16)
            pieces[r][1] = (up[:, pl.ds(at, units)].astype(F32) * scale).astype(BF16)
            pieces[r][2] = down[:, pl.ds(at, units)]

    return call(kernel, [(3, shard, units)] * SPANS, "prepare_ffn")(ids, w_gate, w_up, w_down.T, gain)


def join_attn(ids, pieces):
    rows, shard = pieces[0].shape

    def kernel(ids, *refs):
        pieces, (out,), (made,) = split(refs, SPANS, 1, 1)
        for r, piece in enumerate(pieces):
            made[ids[1] ^ r] = piece[...]
        for place in range(SPANS):
            out[:, place * shard : (place + 1) * shard] = made[place]

    return call(kernel, [(rows, SPANS * shard)], "join_attn", [((SPANS, rows, shard), BF16)])(ids, *pieces)[0]


def join_ffn(ids, pieces):
    _, shard, units = pieces[0].shape

    def kernel(ids, *refs):
        pieces, (out,) = split(refs, SPANS, 1)
        for r, piece in enumerate(pieces):
            out[:, pl.ds(pl.multiple_of((ids[1] ^ r) * shard, 16), shard), :] = piece[...]

    return call(kernel, [(3, SPANS * shard, units)], "join_ffn")(ids, *pieces)[0]


def part_attn(ids, own, one, three):
    rows, part = own.shape
    shard = part // SPANS

    def kernel(ids, own, one, three, *refs):
        pieces, (made,) = split(refs, SPANS, 1)
        total = (own[...].astype(F32) + one[...].astype(F32) + three[...].astype(F32)).astype(BF16)
        for place in range(SPANS):
            made[place] = total[:, place * shard : (place + 1) * shard]
        for r, piece in enumerate(pieces):
            piece[...] = made[ids[1] ^ r]

    return call(kernel, [(rows, shard)] * SPANS, "part_attn", [((SPANS, rows, shard), BF16)])(ids, own, one, three)


def distinct(items):
    arrays = list({id(item[0]): item[0] for item in items}.values())
    index = {id(array): i for i, array in enumerate(arrays)}

    def rows_of(refs, item, rows):
        return refs[index[id(item[0])]][(*item[1], rows)]

    return arrays, rows_of


def project(ids, x, weights, cosine, sine):
    block = x[0].shape[0]
    parts = len(weights[0])
    part = weights[0][0][0].shape[-1]
    arrays, rows_of = distinct([item for items in weights for item in items])
    first = slice(0, 2 * HEAD)

    def kernel(ids, *refs):
        xs, ws, (cos_s, sin_s), (out,) = split(refs, SPANS, len(arrays), 2, 1)
        z, t = ids[0], ids[1]
        at = offsets(ids, parts, part)
        is_value = lax.rem(t, 2) == 1
        for r, x in enumerate(xs):
            rows = pl.ds(pl.multiple_of(((t ^ r) * SPANS + z) * block, block), block)
            cosine, sine = cos_s[rows, :HEAD], sin_s[rows, :HEAD]
            cos_kv = jnp.where(is_value, 1.0, cosine)
            sin_kv = jnp.where(is_value, 0.0, sine)
            for k in range(4):
                made = sum(mm(x[:, pl.ds(at[p], part)], rows_of(ws, weights[k][p], first), NT) for p in range(parts))
                query, other = made[:, :HEAD], made[:, HEAD:]
                out[z ^ k, :, r * HEAD : (r + 1) * HEAD] = (query * cosine + swapped(query) * sine).astype(BF16)
                out[z ^ k, :, (SPANS + r) * HEAD : (SPANS + r + 1) * HEAD] = (
                    other * cos_kv + swapped(other) * sin_kv
                ).astype(BF16)

    return call(kernel, [(4, block, 8 * HEAD)], "project")(ids, *x, *arrays, cosine, sine)[0]


def out_project(ids, pieces, weights):
    block = pieces.shape[1]
    parts = len(weights[0])
    part = weights[0][0][0].shape[-1]
    width = parts * part
    arrays, rows_of = distinct([item for items in weights for item in items])

    def kernel(ids, *refs):
        (pieces,), ws, (near, far, att, orel) = split(refs, 1, len(arrays), 4)
        at = offsets(ids, parts, part)
        for j in range(4):
            for r in range(SPANS):
                att[r * block : (r + 1) * block, j * HEAD : (j + 1) * HEAD] = pieces[ids[0] ^ j, :, r * HEAD : (r + 1) * HEAD]
            for p in range(parts):
                orel[j * HEAD : (j + 1) * HEAD, pl.ds(at[p], part)] = rows_of(ws, weights[j][p], slice(2 * HEAD, 3 * HEAD))
        for r in (1, 3, 2, 0):
            made = mm(att[r * block : (r + 1) * block, :], orel[...], NN).astype(BF16)
            (far if r % 2 else near)[r // 2] = made

    outs = [(2, block, width)] * 2 + [(4 * block, 4 * HEAD), (4 * HEAD, width)]
    return call(kernel, outs, "out_project")(ids, pieces, *arrays)


def out_back(ids, grads, att, orel, parts):
    block, width = grads[0].shape
    part = width // parts

    def kernel(ids, *refs):
        gs, (att, orel), (ds,), douts, (g_s,) = split(refs, SPANS, 2, 1, parts, 1)
        at = offsets(ids, parts, part)
        for r, grad in enumerate(gs):
            g_s[r * block : (r + 1) * block, :] = grad[...]
        made = mm(g_s[...], orel[...], NT).astype(BF16)
        for r in range(SPANS):
            for j in range(4):
                ds[ids[0] ^ j, :, r * HEAD : (r + 1) * HEAD] = made[r * block : (r + 1) * block, j * HEAD : (j + 1) * HEAD]
        for p in range(parts):
            total = mm(att[...], g_s[:, pl.ds(at[p], part)], TN)
            for k in range(4):
                douts[p][k] = total[k * HEAD : (k + 1) * HEAD].astype(BF16)

    outs = [(4, block, 4 * HEAD)] + [(4, HEAD, part)] * parts
    made = call(kernel, outs, "out_back", [((4 * block, width), BF16)])(ids, *grads, att, orel)
    return made[0], made[1:]


def pack(ids, queries, mine, theirs):
    _, block, wide = queries.shape

    def kernel(ids, queries, mine, theirs, out):
        t = ids[1]
        for zj in range(4):
            out[zj, :, :wide] = queries[zj]
            for r in range(SPANS):
                rows = pl.ds(pl.multiple_of(((t ^ r) * SPANS + zj) * block, block), block)
                total = (mine[rows, :].astype(F32) + theirs[rows, :].astype(F32)).astype(BF16)
                out[zj, :, wide + r * HEAD : wide + (r + 1) * HEAD] = total[:, :HEAD]

    return call(kernel, [(4, block, 2 * wide)], "pack")(ids, queries, mine, theirs)[0]


def project_weights(ids, grads, x, parts):
    block, width = x[0].shape
    part = width // parts

    def kernel(ids, *refs):
        (grads,), xs, (d_out,), das, (x_s,) = split(refs, 1, SPANS, 1, 2 * parts, 1)
        at = offsets(ids, parts, part)
        for j in range(4):
            for r in range(SPANS):
                for half in range(2):
                    lanes = slice((half * SPANS + r) * HEAD, (half * SPANS + r + 1) * HEAD)
                    d_out[r * block : (r + 1) * block, (2 * j + half) * HEAD : (2 * j + half + 1) * HEAD] = grads[
                        ids[0] ^ j, :, lanes
                    ]
        for r, x in enumerate(xs):
            x_s[r * block : (r + 1) * block, :] = x[...]
        for p in reversed(range(parts)):
            total = mm(d_out[...], x_s[:, pl.ds(at[p], part)], TN)
            for k in range(4):
                das[2 * p + (k < 2)][k % 2] = total[2 * k * HEAD : (2 * k + 2) * HEAD].astype(BF16)

    outs = [(4 * block, 8 * HEAD)] + [(2, 2 * HEAD, part)] * (2 * parts)
    made = call(kernel, outs, "project_weights", [((4 * block, width), BF16)], 100)(ids, grads, *x)
    return made[0], made[1:]


def project_tokens(ids, grads, weights):
    rows = grads.shape[0]
    block = rows // SPANS
    parts = len(weights[0])
    part = weights[0][0][0].shape[-1]
    width = parts * part
    arrays, rows_of = distinct([item for items in weights for item in items])

    def kernel(ids, *refs):
        (d_s,), ws, (near, far), (a_s,) = split(refs, 1, len(arrays), 2, 1)
        at = offsets(ids, parts, part)
        for j in range(4):
            for p in range(parts):
                a_s[2 * j * HEAD : (2 * j + 2) * HEAD, pl.ds(at[p], part)] = rows_of(ws, weights[j][p], slice(0, 2 * HEAD))
        for r in (1, 3, 2, 0):
            made = mm(d_s[r * block : (r + 1) * block, :], a_s[...], NN).astype(BF16)
            (far if r % 2 else near)[r // 2] = made

    scratch = [((8 * HEAD, width), BF16)]
    return call(kernel, [(2, block, width)] * 2, "project_tokens", scratch, 100)(ids, grads, *arrays)


def feed(ids, x, grads, weights):
    block, width = x[0].shape
    part, units = weights[0][0].shape[-2:]
    parts = width // part
    rows, every = 2 * block, 4 * units
    arrays = list({id(item[0]): item[0] for item in weights}.values())
    index = {id(array): i for i, array in enumerate(arrays)}

    def kernel(ids, *refs):
        xs, gs, ws, ffn, two, (hid, dgate, dup), (x_s, g_s, w_s) = split(refs, 2, 2, len(arrays), 2, 2, 3, 3)
        at = [pl.multiple_of(place, LANES) for place in offsets(ids, parts, part)]
        for r in range(2):
            x_s[r * block : (r + 1) * block, :] = xs[r][...]
            g_s[r * block : (r + 1) * block, :] = gs[r][...]
        for array, where, m, k, p in weights:
            w_s[m, pl.ds(at[p], part), k * units : (k + 1) * units] = ws[index[id(array)]][where]

        def quarter(k, _):
            lanes = pl.ds(pl.multiple_of(k * units, LANES), units)
            gate = mm(x_s[...], w_s[0, :, lanes], NN)
            up = mm(x_s[...], w_s[1, :, lanes], NN)
            back = mm(g_s[...], w_s[2, :, lanes], NN)
            sigma = 0.5 * jnp.tanh(0.5 * gate) + 0.5
            swish = gate * sigma
            hid[:, lanes] = (swish * up).astype(BF16)
            dup[:, lanes] = (back * swish).astype(BF16)
            dgate[:, lanes] = (back * up * (sigma + swish * (1.0 - sigma))).astype(BF16)
            return 0

        lax.fori_loop(0, 4, quarter, 0)
        cut = width // 2
        for p in range(2):
            lanes = slice(p * cut, (p + 1) * cut)
            made = mm(dgate[...], w_s[0, lanes], NT) + mm(dup[...], w_s[1, lanes], NT)
            for r in range(2):
                two[r][:, lanes] = made[r * block : (r + 1) * block].astype(BF16)
        for p in range(2):
            lanes = slice(p * cut, (p + 1) * cut)
            made = mm(hid[...], w_s[2, lanes], NT)
            for r in range(2):
                ffn[r][:, lanes] = made[r * block : (r + 1) * block].astype(BF16)

    outs = [(block, width)] * 4 + [(rows, every)] * 3
    scratch = [((rows, width), BF16), ((rows, width), BF16), ((3, width, every), BF16)]
    made = call(kernel, outs, "feed", scratch, 18, 42)(ids, *x, *grads, *arrays)
    return made[:2], made[2:4], made[4:]


def feed_weights(ids, x, grads, near, far, parts):
    block, width = x[0].shape
    part = width // parts
    half, every = near[0].shape
    units = every // 4

    def kernel(ids, *refs):
        xs, gs, ns, fs, outs, (x_s, g_s, h_s) = split(refs, SPANS, SPANS, 3, 3, 4 * parts, 3)
        at = offsets(ids, parts, part)
        for slot, r in enumerate((0, 1, 2, 3)):
            x_s[slot * block : (slot + 1) * block, :] = xs[r][...]
            g_s[slot * block : (slot + 1) * block, :] = gs[r][...]
        for m in range(3):
            h_s[m, :half] = ns[m][...]
            h_s[m, half:] = fs[m][...]
        for p in reversed(range(parts)):
            for m, left in ((2, g_s), (0, x_s), (1, x_s)):
                side = h_s[{0: 1, 1: 2, 2: 0}[m]]
                total = mm(left[:, pl.ds(at[p], part)], side, TN)
                for k in range(4):
                    outs[k * parts + p][m] = total[:, k * units : (k + 1) * units].astype(BF16)

    outs = [(3, part, units)] * (4 * parts)
    scratch = [((4 * block, width), BF16), ((4 * block, width), BF16), ((3, 4 * block, every), BF16)]
    return call(kernel, outs, "feed_weights", scratch, 17, 48)(ids, *x, *grads, *near, *far)


def finish_ffn(ids, pieces, gain):
    _, shard, units = pieces[0].shape
    every = SPANS * units

    def kernel(ids, *refs):
        pieces, (gain,), (gate, up, down) = split(refs, SPANS, 1, 3)
        scale = gain[...]
        for r, piece in enumerate(pieces):
            lanes = pl.ds(pl.multiple_of((ids[1] ^ r) * units, LANES), units)
            gate[:, lanes] = piece[0].astype(F32) * scale
            up[:, lanes] = piece[1].astype(F32) * scale
            down[:, lanes] = piece[2].astype(F32)

    return call(kernel, [((shard, every), F32)] * 3, "finish_ffn")(ids, *pieces, gain)


def finish_attn(ids, pieces, gain):
    shard = pieces[0].shape[1]

    def kernel(ids, *refs):
        pieces, (gain,), (query, key, value, out_w), (made,) = split(refs, SPANS, 1, 4, 1)
        scale = gain[...]
        for r, piece in enumerate(pieces):
            made[ids[1] ^ r] = piece[...].astype(F32)
        for place in range(SPANS):
            lanes = slice(place * HEAD, (place + 1) * HEAD)
            half = slice(place // 2 * HEAD, (place // 2 + 1) * HEAD)
            out_w[:, lanes] = jnp.transpose(made[place, 2 * HEAD :])
            query[:, lanes] = jnp.transpose(made[place, :HEAD]) * scale
            (value if place % 2 else key)[:, half] = jnp.transpose(made[place, HEAD : 2 * HEAD]) * scale

    outs = [((shard, wide * HEAD), F32) for wide in (4, 2, 2, 4)]
    scratch = [((SPANS, 3 * HEAD, shard), F32)]
    return call(kernel, outs, "finish_attn", scratch)(ids, *pieces, gain)


def swap(value, axis):
    return lax.ppermute(value, axis, [(0, 1), (1, 0)])


def sent(value, axis, bits):
    return lax.ppermute(value, axis, [(i, i ^ bits) for i in range(lax.axis_size(axis))])


def gather_group(value):
    core = swap(value, "c")
    across = swap(value, "x")
    return value, core, across, swap(across, "c")


def scatter_group(near, far):
    total = near.astype(F32) + swap(far, "c").astype(F32)
    return total[0] + swap(total[1].astype(BF16), "x").astype(F32)


def scatter_halves(near, far):
    far_total = far[0].astype(F32) + swap(far[1], "c").astype(F32)
    crossing = swap(far_total.astype(BF16), "x")
    return near[0].astype(F32) + swap(near[1], "c").astype(F32) + crossing.astype(F32)


def exchange(pieces):
    return lax.all_to_all(pieces, "z", split_axis=0, concat_axis=0, tiled=True)


def spread(pieces):
    return [
        pieces[0],
        swap(pieces[1], "c"),
        swap(pieces[2], "x"),
        lax.ppermute(pieces[3], ("x", "c"), [(i, 3 - i) for i in range(SPANS)]),
    ]


def beside(mine, dim):
    if lax.axis_size("y") == 2:
        return [mine, swap(mine, "y")]
    return [lax.all_gather(mine, "y", axis=dim, tiled=True)]


def along_z(mine):
    if lax.axis_size("z") != 4:
        return [mine] + [sent(mine, "z", k) for k in range(1, lax.axis_size("z"))]
    far = sent(mine, "z", 3)
    return [mine, sent(mine, "z", 1), sent(far, "z", 1), far]


def onto_z(pieces):
    far = pieces[3].astype(F32) + sent(pieces[2], "z", 1).astype(F32)
    near = pieces[0].astype(F32) + sent(pieces[1], "z", 1).astype(F32)
    return (near + sent(far.astype(BF16), "z", 3).astype(F32)).astype(BF16)


def settled(pieces, parts, dim):
    if parts == 2:
        sums = [
            (pieces[2 * k].astype(F32) + swap(pieces[2 * k + 1], "y").astype(F32)).astype(BF16) for k in range(4)
        ]
    else:
        sums = [lax.psum_scatter(piece, "y", scatter_dimension=dim, tiled=True) for piece in pieces]
    return onto_z(sums)


def halved(values, rest, axis, dim):
    if lax.axis_size(axis) != 2:
        values, rest = lax.psum((values, rest), axis)
        return lax.dynamic_index_in_dim(values, lax.axis_index(axis), dim, keepdims=False), rest
    here = lax.axis_index(axis)
    kept = lax.dynamic_index_in_dim(values, here, dim, keepdims=False)
    gone = lax.dynamic_index_in_dim(values, 1 - here, dim, keepdims=False)
    came = swap(jnp.concatenate([gone.reshape(-1), rest]), axis)
    return kept + came[: kept.size].reshape(kept.shape), rest + came[kept.size :]


def over_z(value):
    return value + sum(sent(value, "z", k) for k in range(1, lax.axis_size("z")))


def unit(values):
    scale = lax.rsqrt(jnp.mean(values * values, axis=-1, keepdims=True) + EPSILON)
    return values * scale, scale


def unit_back(values, scale, grad):
    inner = jnp.mean(grad * values, axis=-1, keepdims=True)
    return scale * grad - values * (scale * scale * scale) * inner


def per_device(tokens, w_query, w_key, w_value, w_out, w_gate, w_up, w_down, norm_attn, norm_ffn, grad_out):
    sequences, count = lax.axis_size("y"), lax.axis_size("z")
    parts = 2 if sequences == 2 else 1
    block, width = tokens.shape
    shard = w_query.shape[0]
    t = lax.axis_index("x") * 2 + lax.axis_index("c")
    ids = jnp.stack([lax.axis_index("z"), t, lax.axis_index("y")]).astype(jnp.int32)
    gain_attn = norm_attn.astype(F32)[:, None]
    gain_ffn = norm_ffn.astype(F32)[:, None]

    fence = lax.optimization_barrier

    resid = tokens.astype(F32)
    unit_one, scale_one = unit(resid)
    attn_pieces, low_one = fence((prepare_attn(ids, w_query, w_key, w_value, w_out, gain_attn), unit_one.astype(BF16)))
    attn_mine = join_attn(ids, spread(attn_pieces))
    lane = jnp.arange(LANES)
    freq = ROPE_BASE ** (-(lane % (HEAD // 2) * 2.0) / HEAD)
    inner = jnp.arange(block, dtype=F32)[:, None] * freq
    outer = (jnp.arange(SEQUENCE_LENGTH // block, dtype=F32) * block)[:, None] * freq
    cos_in, sin_in, cos_out, sin_out = jnp.cos(inner), jnp.sin(inner), jnp.cos(outer)[:, None], jnp.sin(outer)[:, None]
    cosine = (cos_out * cos_in - sin_out * sin_in).reshape(SEQUENCE_LENGTH, LANES)
    sine = (sin_out * cos_in + cos_out * sin_in).reshape(SEQUENCE_LENGTH, LANES)
    sine = sine * jnp.where(lane < HEAD // 2, -1.0, 1.0)
    attn_mine, ffn_pieces, cosine, sine, low_one = fence(
        (attn_mine, prepare_ffn(ids, w_gate, w_up, w_down, gain_ffn), cosine, sine, low_one)
    )

    attn_three, attn_one = sent(attn_mine, "z", 3), sent(attn_mine, "z", 1)
    own = beside(attn_mine, 1)
    ffn_mine = join_ffn(ids, spread(ffn_pieces))
    core, across = swap(low_one, "c"), swap(low_one, "x")
    ffn_mine, attn_three, attn_one, own = fence((ffn_mine, attn_three, attn_one, own))
    attn_two = sent(attn_three, "z", 1)
    three_one = beside(jnp.stack([attn_three, attn_one]), 2)
    gate_three = sent(ffn_mine[0], "z", 3)
    attn_two, three_one, gate_three, ffn_mine, core, across = fence(
        (attn_two, three_one, gate_three, ffn_mine, core, across)
    )
    x_one = (low_one, core, across, swap(across, "c"))
    two = beside(attn_two, 1)
    attn_weights = [
        [(array, ()) for array in own],
        [(array, (1,)) for array in three_one],
        [(array, ()) for array in two],
        [(array, (0,)) for array in three_one],
    ]
    gate_one, up_three = sent(ffn_mine[0], "z", 1), sent(ffn_mine[1], "z", 3)
    made = project(ids, x_one, attn_weights, cosine, sine)
    made, gate_one, up_three, gate_three, ffn_mine, grad_in = fence(
        (made, gate_one, up_three, gate_three, ffn_mine, grad_out)
    )

    made = exchange(made)
    ffn_own = beside(ffn_mine, 1)
    g_rows = gather_group(grad_in)
    by_one = jnp.stack([ffn_mine[1], gate_three])
    first = jnp.stack([gate_three, gate_one, up_three])
    made, ffn_own, g_rows, by_one, first, down_mine = fence((made, ffn_own, g_rows, by_one, first, ffn_mine[2]))
    by_one, down_three = sent(by_one, "z", 1), sent(down_mine, "z", 3)
    first = beside(first, 1)
    other = swap(made[:, :, SPANS * HEAD :], "c")
    attended, q_seq, kv_seq, o_seq, lse = attend(ids, made, other)
    attended, down_three, by_one, first, up_three, down_mine = fence(
        (attended, down_three, by_one, first, up_three, down_mine)
    )
    attended = exchange(attended)
    by_one = beside(by_one, 1)
    down_one = sent(down_mine, "z", 1)
    both_two = jnp.stack([up_three, down_three])
    attended, by_one, down_one, down_three, both_two = fence((attended, by_one, down_one, down_three, both_two))
    both_two = sent(both_two, "z", 1)
    down_three, down_one = beside(down_three, 0), beside(down_one, 0)
    near, far, att, orel = out_project(ids, attended, attn_weights)
    branch_attn = scatter_group(near, far)
    state = resid + branch_attn
    unit_two, scale_two = unit(state)
    low_two, both_two, down_three, down_one = fence((unit_two.astype(BF16), both_two, down_three, down_one))
    x_two = gather_group(low_two)
    both_two = beside(both_two, 1)
    x_two, both_two = fence((x_two, both_two))

    ffn_weights = []
    for p in range(parts):
        ffn_weights += [(ffn_own[p], (m,), m, 0, p) for m in range(3)]
        ffn_weights += [(first[p], (i,), *place, p) for i, place in enumerate(((0, 3), (0, 1), (1, 3)))]
        ffn_weights += [(by_one[p], (i,), *place, p) for i, place in enumerate(((1, 1), (0, 2)))]
        ffn_weights += [(down_three[p], (Ellipsis,), 2, 3, p), (down_one[p], (Ellipsis,), 2, 1, p)]
        ffn_weights += [(both_two[p], (0,), 1, 2, p), (both_two[p], (1,), 2, 2, p)]
    ffn_far, two_far, kept_far = feed(ids, x_two[2:], g_rows[2:], ffn_weights)
    crossing = (two_far[0].astype(F32) + swap(two_far[1], "c").astype(F32)).astype(BF16)
    crossing, x_near = fence((crossing, x_two[:2]))
    crossing = swap(crossing, "x")
    ffn_near, two_near, kept_near = feed(ids, x_near, g_rows[:2], ffn_weights)
    two_near, crossing = fence((two_near, crossing))
    grad_unit_two = two_near[0].astype(F32) + swap(two_near[1], "c").astype(F32) + crossing.astype(F32)
    grad_state = grad_out.astype(F32) + unit_back(state, scale_two, grad_unit_two)
    state_low, kept_near, ffn_near, ffn_far, grad_unit_two = fence(
        (grad_state.astype(BF16), kept_near, ffn_near, ffn_far, grad_unit_two)
    )
    across, core = swap(state_low, "x"), swap(state_low, "c")
    feed_grads = feed_weights(ids, x_two, g_rows, kept_near, kept_far, parts)
    across, core, feed_grads = fence((across, core, feed_grads))
    g_state = (state_low, core, across, swap(across, "c"))

    def home(total):
        pieces = total.reshape(*total.shape[:-2], SPANS, shard, total.shape[-1])
        return spread([lax.dynamic_index_in_dim(pieces, t ^ r, pieces.ndim - 3, keepdims=False) for r in range(SPANS)])

    def crossed(grads, k):
        if parts == 1:
            return lax.psum_scatter(grads[k], "y", scatter_dimension=1, tiled=True)
        return swap(grads[2 * k + 1], "y")

    def added(grads, k, came):
        return came if parts == 1 else (grads[2 * k].astype(F32) + came.astype(F32)).astype(BF16)

    two_came = crossed(feed_grads, 2)
    grad_att, out_grads = out_back(ids, g_state, att, orel, parts)
    grad_att = exchange(grad_att)
    onward = added(feed_grads, 2, two_came)
    grad_att, onward, feed_grads, out_grads = fence((grad_att, onward, feed_grads, out_grads))
    onward = sent(onward, "z", 1)
    three_came = crossed(feed_grads, 3)
    if parts == 2:
        out_sums = out_grads[0].astype(F32) + swap(out_grads[1], "y").astype(F32)
    else:
        out_sums = lax.psum_scatter(out_grads[0], "y", scatter_dimension=2, tiled=True)
    dq, keep, give = attend_back(ids, q_seq, kv_seq, o_seq, lse, cosine, sine, grad_att)
    dq, keep, give, onward, three_came, feed_grads, ffn_near, ffn_far, out_sums = fence(
        (dq, keep, give, onward, three_came, feed_grads, ffn_near, ffn_far, out_sums.astype(BF16))
    )
    one_came = crossed(feed_grads, 1)
    grads_heads = exchange(pack(ids, dq, keep, swap(give, "c")))
    branch_ffn = scatter_halves(ffn_near, ffn_far)
    result = state + branch_ffn
    gain_two = jnp.sum(grad_unit_two * unit_two, axis=0)
    squares = jnp.stack([jnp.sum(result * result), jnp.sum(branch_attn * branch_attn), jnp.sum(branch_ffn * branch_ffn)])
    onward = (added(feed_grads, 3, three_came).astype(F32) + onward.astype(F32)).astype(BF16)
    onward, onward_down = onward[:2], onward[2:]
    one_sum = added(feed_grads, 1, one_came)
    grads_heads, result, squares, gain_two, onward, onward_down, one_sum, feed_grads = fence(
        (grads_heads, result, squares, gain_two, onward, onward_down, one_sum, feed_grads)
    )
    onward = sent(onward, "z", 3)
    feed_one = sent(one_sum, "z", 1)
    grads_qkv, qkv_grads = project_weights(ids, grads_heads, x_one, parts)
    grads_qkv, qkv_grads = fence((grads_qkv, qkv_grads))
    near, far = project_tokens(ids, grads_qkv, attn_weights)
    if parts == 2:
        gone = [swap(piece, "y") for piece in qkv_grads[2:]]
    else:
        gone = [lax.psum_scatter(piece, "y", scatter_dimension=2, tiled=True) for piece in qkv_grads]
    own_came = crossed(feed_grads, 0)
    gone, feed_grads, onward, onward_down, feed_one, near, far, own_came = fence(
        (gone, feed_grads, onward, onward_down, feed_one, near, far, own_came)
    )
    late, early = (
        [came.astype(F32) if parts == 1 else kept.astype(F32) + came.astype(F32) for kept, came in zip(qkv_grads, gone)]
    )
    sums = [early[0], early[1], late[0], late[1]]
    sums = [jnp.concatenate([sums[k].astype(BF16), out_sums[k]], axis=0) for k in range(4)]
    onto_three = (sums[3].astype(F32) + sent(sums[2], "z", 1).astype(F32)).astype(BF16)
    onto_one = sent(sums[1], "z", 1)
    onward_down = sent(onward_down, "z", 3)
    total = near.astype(F32) + swap(far, "c").astype(F32)
    crossing = swap(total[1].astype(BF16), "x")
    feed_total = added(feed_grads, 0, own_came).astype(F32) + jnp.concatenate([onward, onward_down]).astype(F32)
    feed_total = (feed_total + feed_one.astype(F32)).astype(BF16)
    onto_three, onto_one, crossing, feed_total = fence((onto_three, onto_one, crossing, feed_total))
    onto_three = sent(onto_three, "z", 3)
    feed_home = home(feed_total)
    grad_unit_one = total[0] + crossing.astype(F32)
    grad_tokens = (grad_state + unit_back(resid, scale_one, grad_unit_one)).astype(BF16)
    gains = jnp.stack([jnp.sum(grad_unit_one * unit_one, axis=0), gain_two])
    gains, squares = halved(gains.reshape(2, sequences, 2, 2, shard), squares, "c", 3)
    gains, squares = halved(gains, squares, "y", 1)
    gains, squares = halved(gains, squares, "x", 1)
    totals = over_z(jnp.concatenate([gains.reshape(-1), squares]))
    onto_three, onto_one, feed_home, totals, grad_tokens = fence((onto_three, onto_one, feed_home, totals, grad_tokens))
    attn_home = spread(part_attn(ids, sums[0], onto_one, onto_three))
    grad_gate, grad_up, grad_down = finish_ffn(ids, feed_home, gain_ffn)
    grad_query, grad_key, grad_value, grad_outproj = finish_attn(ids, attn_home, gain_attn)
    entries = block * width * sequences * SPANS * count
    return (
        result.astype(BF16),
        grad_tokens,
        grad_query,
        grad_key,
        grad_value,
        grad_outproj.T,
        grad_gate,
        grad_up,
        grad_down.T,
        totals[:shard] / gain_attn[:, 0],
        totals[shard : 2 * shard] / gain_ffn[:, 0],
        jnp.sqrt(totals[2 * shard :] / entries),
    )


def solution(mesh):
    fsdp, tensor = mesh.shape["fsdp"], mesh.shape["tensor"]
    split = Mesh(mesh.devices.reshape(fsdp // SPANS, 2, 2, tensor), ("y", "x", "c", "z"))
    rows = ("y", "x", "c")
    tok = P(("y", "x", "c", "z"), None)
    col, row, vec = P(rows, "z"), P("z", rows), P(rows)
    return jax.shard_map(
        per_device,
        mesh=split,
        in_specs=(tok, col, col, col, row, col, col, row, vec, vec, tok),
        out_specs=(tok, tok, col, col, col, row, col, col, row, vec, vec, P()),
        check_vma=False,
    )
```

```python
import functools
import jax
import jax.numpy as jnp
from jax import lax
from jax.experimental import pallas as pl
from jax.experimental.pallas import tpu as pltpu
from jax.sharding import Mesh, PartitionSpec as P

HEAD = 96
LANES = 128
SEQUENCE_LENGTH = 4096
SPANS = 4
EPSILON = 1e-05
ROPE_BASE = 100000.0
MASKED = -1e30
LOG2E = 1.4426950408889634
NT = (((1,), (1,)), ((), ()))
NN = (((1,), (0,)), ((), ()))
TN = (((0,), (0,)), ((), ()))
F32 = jnp.float32
BF16 = jnp.bfloat16


def mm(left, right, dims):
    return lax.dot_general(left, right, dims, preferred_element_type=F32)


def widen(piece):
    return jnp.concatenate([piece, jnp.zeros((piece.shape[0], LANES - HEAD), piece.dtype)], axis=1)


def swapped(value):
    half = HEAD // 2
    return jnp.concatenate([value[:, half:HEAD], value[:, :half]], axis=1)


def rotary(tables, place):
    cos_in, sin_in, cos_out, sin_out = tables
    at = pl.ds(place, 1)
    cosine = cos_out[at, :] * cos_in[...] - sin_out[at, :] * sin_in[...]
    return cosine, sin_out[at, :] * cos_in[...] + cos_out[at, :] * sin_in[...]


def attend_kernel(ids, own, other, out, q_s, kv_s, o_s, lse_s, acc_s, vt_s, *, block, tile):
    z, t = ids[0], ids[1]
    c = lax.rem(t, 2)
    spans = 4
    rows_all = q_s.shape[0]
    for zj in range(4):
        for r in range(spans):
            at = pl.multiple_of(((t ^ r) * spans + zj) * block, block)
            at_other = pl.multiple_of(((t ^ 1 ^ r) * spans + zj) * block, block)
            q_s[pl.ds(at, block), :] = widen(own[zj, :, r * HEAD : (r + 1) * HEAD])
            kv_s[c, pl.ds(at, block), :] = widen(own[zj, :, (spans + r) * HEAD : (spans + r + 1) * HEAD])
            kv_s[1 - c, pl.ds(at_other, block), :] = widen(other[zj, :, r * HEAD : (r + 1) * HEAD])
    factor = HEAD ** (-0.5) * LOG2E
    is_count = lax.broadcasted_iota(jnp.int32, (tile, LANES), 1) == HEAD

    def values(i, _):
        rows = pl.ds(pl.multiple_of(i * tile, tile), tile)
        vals = kv_s[1, rows, :]
        vt_s[:, rows] = jnp.transpose(jnp.where(is_count, jnp.ones_like(vals), vals))
        return 0

    lax.fori_loop(0, rows_all // tile, values, 0)

    def step(query, j, before, mask):
        rows = pl.ds(pl.multiple_of(j * tile, tile), tile)
        scores = mm(kv_s[0, rows, :], query, NT) * factor
        if mask is not None:
            scores = jnp.where(mask, scores, MASKED)
        top = jnp.maximum(before, jnp.max(scores, axis=0, keepdims=True))
        expo = jnp.exp2(scores - top).astype(BF16)
        acc_s[...] = acc_s[...] * jnp.exp2(before - top) + mm(vt_s[:, rows], expo, NN)
        return top

    def row_block(i, _):
        at = pl.multiple_of(i * tile, tile)
        query = q_s[pl.ds(at, tile), :]
        acc_s[...] = jnp.zeros_like(acc_s)
        top = lax.fori_loop(0, i, lambda j, top: step(query, j, top, None), jnp.full((1, tile), MASKED, F32))
        mask = lax.broadcasted_iota(jnp.int32, (tile, tile), 0) <= lax.broadcasted_iota(jnp.int32, (tile, tile), 1)
        top = step(query, i, top, mask)
        acc = acc_s[...]
        denom = acc[HEAD : HEAD + 1, :]
        o_s[pl.ds(at, tile), :] = jnp.transpose(acc / denom).astype(BF16)
        lse_s[:, pl.ds(at, tile)] = jnp.broadcast_to(top + jnp.log2(denom), (8, tile))
        return 0

    lax.fori_loop(0, rows_all // tile, row_block, 0)
    for zj in range(4):
        for r in range(spans):
            at = pl.multiple_of(((t ^ r) * spans + zj) * block, block)
            out[zj, :, r * HEAD : (r + 1) * HEAD] = o_s[pl.ds(at, block), :HEAD]


VM = pl.BlockSpec(memory_space=pltpu.VMEM)
SM = pl.BlockSpec(memory_space=pltpu.SMEM)


def shape(dims, dtype=BF16):
    return jax.ShapeDtypeStruct(dims, dtype)


def params(room):
    return pltpu.CompilerParams(vmem_limit_bytes=room * 1024 * 1024)


def attend(ids, own, other, tile=1024):
    block = own.shape[1]
    rows = block * 16
    return pl.pallas_call(
        functools.partial(attend_kernel, block=block, tile=tile),
        out_shape=[shape((4, block, 4 * HEAD)), shape((rows, LANES)), shape((2, rows, LANES)), shape((rows, LANES)), shape((8, rows), F32)],
        in_specs=[SM] + [VM] * 2,
        out_specs=[VM] * 5,
        scratch_shapes=[pltpu.VMEM((LANES, tile), F32), pltpu.VMEM((LANES, rows), BF16)],
        compiler_params=params(22),
        cost_estimate=pl.CostEstimate(flops=int(21e9), bytes_accessed=1, transcendentals=0),
        name="attend",
    )(ids, own, other)


def attend_back_kernel(ids, q_s, kv_s, o_s, lse_s, cos_in, sin_in, cos_out, sin_out, g, dq_out, keep_out, give_out, g_s, qx_s, kx_s, delta_s, dq_s, dk_s, dv_s, *, block, tile):
    z, t = ids[0], ids[1]
    spans = 4
    rows_all = q_s.shape[0]
    tiles = rows_all // tile
    for zj in range(4):
        for r in range(spans):
            at = pl.multiple_of(((t ^ r) * spans + zj) * block, block)
            g_s[pl.ds(at, block), :] = widen(g[zj, :, r * HEAD : (r + 1) * HEAD])

    def prepare(i, _):
        at = pl.multiple_of(i * tile, tile)
        rows = pl.ds(at, tile)
        query = q_s[rows, :]
        keys = kv_s[0, rows, :]
        qx_s[rows, :LANES] = query
        qx_s[rows, LANES:] = widen(swapped(query))
        kx_s[rows, :LANES] = keys
        kx_s[rows, LANES:] = widen(swapped(keys))
        both = g_s[rows, :].astype(F32) * o_s[rows, :].astype(F32)
        delta = jnp.sum(both, axis=1, keepdims=True)
        delta_s[:, rows] = jnp.transpose(jnp.broadcast_to(delta, (tile, LANES)))[:8]
        dq_s[rows, :] = jnp.zeros((tile, 2 * LANES), F32)
        return 0

    lax.fori_loop(0, tiles, prepare, 0)
    factor = HEAD ** (-0.5) * LOG2E
    scale = HEAD ** (-0.5)

    def step(i, keys, vals, kx, mask):
        rows = pl.ds(pl.multiple_of(i * tile, tile), tile)
        query = qx_s[rows, :]
        grad = g_s[rows, :]
        scores = mm(keys, query[:, :LANES], NT) * factor - lse_s[:1, rows]
        if mask is not None:
            scores = jnp.where(mask, scores, MASKED)
        prob = jnp.exp2(scores)
        through = mm(vals, grad, NT)
        ds = (prob * (through - delta_s[:1, rows])).astype(BF16)
        dv_s[...] += mm(prob.astype(BF16), grad, NN)
        dk_s[...] += mm(ds, query, NN)
        dq_s[rows, :] += mm(ds, kx, TN)

    def column_block(j, _):
        rows = pl.ds(pl.multiple_of(j * tile, tile), tile)
        kx = kx_s[rows, :]
        keys = kx[:, :LANES]
        vals = kv_s[1, rows, :]
        dk_s[...] = jnp.zeros_like(dk_s)
        dv_s[...] = jnp.zeros_like(dv_s)
        mask = lax.broadcasted_iota(jnp.int32, (tile, tile), 0) <= lax.broadcasted_iota(jnp.int32, (tile, tile), 1)
        step(j, keys, vals, kx, mask)
        lax.fori_loop(j + 1, tiles, lambda i, _: (step(i, keys, vals, kx, None), 0)[1], 0)
        dk = dk_s[...] * scale
        turns = [rotary((cos_in, sin_in, cos_out, sin_out), j * (tile // block) + b) for b in range(tile // block)]
        cosine, sine = (jnp.concatenate(parts, axis=0) for parts in zip(*turns))
        dk = dk[:, :LANES] * cosine - dk[:, LANES:] * sine
        dv = dv_s[...]
        first = lax.rem(t, 2) == 0
        keep_out[rows, :] = jnp.where(first, dk, dv).astype(BF16)
        give_out[rows, :] = jnp.where(first, dv, dk).astype(BF16)
        return 0

    lax.fori_loop(0, tiles, column_block, 0)
    for zj in range(4):
        for r in range(spans):
            rows = pl.ds(pl.multiple_of(((t ^ r) * spans + zj) * block, block), block)
            cosine, sine = rotary((cos_in, sin_in, cos_out, sin_out), (t ^ r) * spans + zj)
            dq = dq_s[rows, :] * scale
            dq_out[zj, :, r * HEAD : (r + 1) * HEAD] = (
                dq[:, :LANES] * cosine - dq[:, LANES:] * sine
            ).astype(BF16)[:, :HEAD]


def attend_back(ids, q, kv, o, lse, tables, grads, tile=1024):
    block = grads.shape[1]
    rows = block * 16
    return pl.pallas_call(
        functools.partial(attend_back_kernel, block=block, tile=tile),
        out_shape=[shape((4, block, 4 * HEAD))] + [shape((rows, LANES))] * 2,
        in_specs=[SM] + [VM] * 9,
        out_specs=[VM] * 3,
        scratch_shapes=[
            pltpu.VMEM((rows, LANES), BF16),
            pltpu.VMEM((rows, 2 * LANES), BF16),
            pltpu.VMEM((rows, 2 * LANES), BF16),
            pltpu.VMEM((8, rows), F32),
            pltpu.VMEM((rows, 2 * LANES), F32),
            pltpu.VMEM((tile, 2 * LANES), F32),
            pltpu.VMEM((tile, LANES), F32),
        ],
        compiler_params=params(36),
        cost_estimate=pl.CostEstimate(flops=int(39e9), bytes_accessed=1, transcendentals=0),
        name="attend_back",
    )(ids, q, kv, o, lse, *tables, grads)


def offsets(ids, count, part):
    if count == 1:
        return [0]
    return [pl.multiple_of(ids[2] * part, LANES), pl.multiple_of((1 - ids[2]) * part, LANES)]


def call(kernel, outs, name, scratch=(), micros=0, room=14):
    def run(ids, *args):
        return pl.pallas_call(
            kernel,
            out_shape=[shape(*o) if isinstance(o[0], tuple) else shape(o) for o in outs],
            in_specs=[SM] + [VM] * len(args),
            out_specs=[VM] * len(outs),
            scratch_shapes=[pltpu.VMEM(*item) for item in scratch],
            compiler_params=params(room),
            cost_estimate=pl.CostEstimate(flops=int(micros * 1e9) + 1, bytes_accessed=1, transcendentals=0),
            name=name,
        )(ids, *args)

    return run


def split(refs, *counts):
    refs = list(refs)
    groups = []
    for count in counts:
        groups.append(refs[:count])
        refs = refs[count:]
    return groups


def prepare_attn(ids, w_query, w_key, w_value, w_out, gain):
    shard = w_query.shape[0]

    def kernel(ids, query, key, value, out, gain, *refs):
        pieces, made = split(refs, SPANS, 1)
        made = made[0]
        scale = gain[...]

        def turned(ref, at):
            return jnp.transpose(ref[:, at * HEAD : (at + 1) * HEAD].astype(F32) * scale).astype(BF16)

        for place in range(SPANS):
            made[place, :HEAD] = turned(query, place)
            made[place, HEAD : 2 * HEAD] = turned(value if place % 2 else key, place // 2)
            made[place, 2 * HEAD :] = jnp.transpose(out[:, place * HEAD : (place + 1) * HEAD].astype(F32)).astype(BF16)
        for r in range(SPANS):
            pieces[r][...] = made[ids[1] ^ r]

    scratch = [((SPANS, 3 * HEAD, shard), BF16)]
    return call(kernel, [(3 * HEAD, shard)] * SPANS, "prepare_attn", scratch)(
        ids, w_query, w_key, w_value, w_out.T, gain
    )


def prepare_ffn(ids, w_gate, w_up, w_down, gain):
    shard = w_gate.shape[0]
    units = w_gate.shape[1] // SPANS

    def kernel(ids, gate, up, down, gain, *pieces):
        scale = gain[...]
        for r in range(SPANS):
            at = pl.multiple_of((ids[1] ^ r) * units, LANES)
            pieces[r][0] = (gate[:, pl.ds(at, units)].astype(F32) * scale).astype(BF16)
            pieces[r][1] = (up[:, pl.ds(at, units)].astype(F32) * scale).astype(BF16)
            pieces[r][2] = down[:, pl.ds(at, units)]

    return call(kernel, [(3, shard, units)] * SPANS, "prepare_ffn")(ids, w_gate, w_up, w_down.T, gain)


def join_attn(ids, pieces):
    rows, shard = pieces[0].shape

    def kernel(ids, *refs):
        pieces, (out,), (made,) = split(refs, SPANS, 1, 1)
        for r, piece in enumerate(pieces):
            made[ids[1] ^ r] = piece[...]
        for place in range(SPANS):
            out[:, place * shard : (place + 1) * shard] = made[place]

    return call(kernel, [(rows, SPANS * shard)], "join_attn", [((SPANS, rows, shard), BF16)])(ids, *pieces)[0]


def join_ffn(ids, pieces):
    _, shard, units = pieces[0].shape

    def kernel(ids, *refs):
        pieces, (out,) = split(refs, SPANS, 1)
        for r, piece in enumerate(pieces):
            out[:, pl.ds(pl.multiple_of((ids[1] ^ r) * shard, 16), shard), :] = piece[...]

    return call(kernel, [(3, SPANS * shard, units)], "join_ffn")(ids, *pieces)[0]


def part_attn(ids, own, one, three):
    rows, part = own.shape
    shard = part // SPANS

    def kernel(ids, own, one, three, *refs):
        pieces, (made,) = split(refs, SPANS, 1)
        total = (own[...].astype(F32) + one[...].astype(F32) + three[...].astype(F32)).astype(BF16)
        for place in range(SPANS):
            made[place] = total[:, place * shard : (place + 1) * shard]
        for r, piece in enumerate(pieces):
            piece[...] = made[ids[1] ^ r]

    return call(kernel, [(rows, shard)] * SPANS, "part_attn", [((SPANS, rows, shard), BF16)])(ids, own, one, three)


def distinct(items):
    arrays = list({id(item[0]): item[0] for item in items}.values())
    index = {id(array): i for i, array in enumerate(arrays)}

    def rows_of(refs, item, rows):
        return refs[index[id(item[0])]][(*item[1], rows)]

    return arrays, rows_of


def project(ids, x, weights, tables):
    block = x[0].shape[0]
    parts = len(weights[0])
    part = weights[0][0][0].shape[-1]
    arrays, rows_of = distinct([item for items in weights for item in items])
    first = slice(0, 2 * HEAD)

    def kernel(ids, *refs):
        xs, ws, tables, (out,) = split(refs, SPANS, len(arrays), 4, 1)
        z, t = ids[0], ids[1]
        at = offsets(ids, parts, part)
        is_value = lax.rem(t, 2) == 1
        for r, x in enumerate(xs):
            cosine, sine = rotary(tables, (t ^ r) * SPANS + z)
            cosine, sine = cosine[:, :HEAD], sine[:, :HEAD]
            cos_kv = jnp.where(is_value, 1.0, cosine)
            sin_kv = jnp.where(is_value, 0.0, sine)
            for k in range(4):
                made = sum(mm(x[:, pl.ds(at[p], part)], rows_of(ws, weights[k][p], first), NT) for p in range(parts))
                query, other = made[:, :HEAD], made[:, HEAD:]
                out[z ^ k, :, r * HEAD : (r + 1) * HEAD] = (query * cosine + swapped(query) * sine).astype(BF16)
                out[z ^ k, :, (SPANS + r) * HEAD : (SPANS + r + 1) * HEAD] = (
                    other * cos_kv + swapped(other) * sin_kv
                ).astype(BF16)

    return call(kernel, [(4, block, 8 * HEAD)], "project")(ids, *x, *arrays, *tables)[0]


def out_weights(ids, weights):
    parts = len(weights[0])
    part = weights[0][0][0].shape[-1]
    arrays, rows_of = distinct([item for items in weights for item in items])

    def kernel(ids, *refs):
        ws, (orel,) = split(refs, len(arrays), 1)
        at = offsets(ids, parts, part)
        for j in range(4):
            for p in range(parts):
                orel[j * HEAD : (j + 1) * HEAD, pl.ds(at[p], part)] = rows_of(ws, weights[j][p], slice(2 * HEAD, 3 * HEAD))

    return call(kernel, [(4 * HEAD, parts * part)], "out_weights")(ids, *arrays)[0]


def out_project(ids, pieces, orel):
    block, width = pieces.shape[1], orel.shape[1]

    def kernel(ids, pieces, orel, near, far, att):
        for j in range(4):
            for r in range(SPANS):
                att[r * block : (r + 1) * block, j * HEAD : (j + 1) * HEAD] = pieces[ids[0] ^ j, :, r * HEAD : (r + 1) * HEAD]
        for r in (1, 3, 2, 0):
            made = mm(att[r * block : (r + 1) * block, :], orel[...], NN).astype(BF16)
            (far if r % 2 else near)[r // 2] = made

    outs = [(2, block, width)] * 2 + [(4 * block, 4 * HEAD)]
    return call(kernel, outs, "out_project")(ids, pieces, orel)


def out_back(ids, grads, att, orel, parts):
    block, width = grads[0].shape
    part = width // parts

    def kernel(ids, *refs):
        gs, (att, orel), (ds,), douts, (g_s,) = split(refs, SPANS, 2, 1, parts, 1)
        at = offsets(ids, parts, part)
        for r, grad in enumerate(gs):
            g_s[r * block : (r + 1) * block, :] = grad[...]
        made = mm(g_s[...], orel[...], NT).astype(BF16)
        for r in range(SPANS):
            for j in range(4):
                ds[ids[0] ^ j, :, r * HEAD : (r + 1) * HEAD] = made[r * block : (r + 1) * block, j * HEAD : (j + 1) * HEAD]
        for p in range(parts):
            total = mm(att[...], g_s[:, pl.ds(at[p], part)], TN)
            for k in range(4):
                douts[p][k] = total[k * HEAD : (k + 1) * HEAD].astype(BF16)

    outs = [(4, block, 4 * HEAD)] + [(4, HEAD, part)] * parts
    made = call(kernel, outs, "out_back", [((4 * block, width), BF16)])(ids, *grads, att, orel)
    return made[0], made[1:]


def pack(ids, queries, mine, theirs):
    _, block, wide = queries.shape

    def kernel(ids, queries, mine, theirs, out):
        t = ids[1]
        for zj in range(4):
            out[zj, :, :wide] = queries[zj]
            for r in range(SPANS):
                rows = pl.ds(pl.multiple_of(((t ^ r) * SPANS + zj) * block, block), block)
                total = (mine[rows, :].astype(F32) + theirs[rows, :].astype(F32)).astype(BF16)
                out[zj, :, wide + r * HEAD : wide + (r + 1) * HEAD] = total[:, :HEAD]

    return call(kernel, [(4, block, 2 * wide)], "pack")(ids, queries, mine, theirs)[0]


def project_weights(ids, grads, x, parts):
    block, width = x[0].shape
    part = width // parts

    def kernel(ids, *refs):
        (grads,), xs, (d_out,), das, (x_s,) = split(refs, 1, SPANS, 1, 2 * parts, 1)
        at = offsets(ids, parts, part)
        for j in range(4):
            for r in range(SPANS):
                for half in range(2):
                    lanes = slice((half * SPANS + r) * HEAD, (half * SPANS + r + 1) * HEAD)
                    d_out[r * block : (r + 1) * block, (2 * j + half) * HEAD : (2 * j + half + 1) * HEAD] = grads[
                        ids[0] ^ j, :, lanes
                    ]
        for r, x in enumerate(xs):
            x_s[r * block : (r + 1) * block, :] = x[...]
        for p in reversed(range(parts)):
            total = mm(d_out[...], x_s[:, pl.ds(at[p], part)], TN)
            for k in range(4):
                das[2 * p + (k < 2)][k % 2] = total[2 * k * HEAD : (2 * k + 2) * HEAD].astype(BF16)

    outs = [(4 * block, 8 * HEAD)] + [(2, 2 * HEAD, part)] * (2 * parts)
    made = call(kernel, outs, "project_weights", [((4 * block, width), BF16)], 100)(ids, grads, *x)
    return made[0], made[1:]


def project_tokens(ids, grads, x, weights):
    rows = grads.shape[0]
    block = rows // SPANS
    parts = len(weights[0])
    part = weights[0][0][0].shape[-1]
    width = parts * part
    arrays, rows_of = distinct([item for items in weights for item in items])

    def kernel(ids, *refs):
        (d_s,), xs, ws, (near, far, sums), (a_s,) = split(refs, 1, SPANS, len(arrays), 3, 1)
        at = offsets(ids, parts, part)
        for j in range(4):
            for p in range(parts):
                a_s[2 * j * HEAD : (2 * j + 2) * HEAD, pl.ds(at[p], part)] = rows_of(ws, weights[j][p], slice(0, 2 * HEAD))
        total = None
        for r in (1, 3, 2, 0):
            made = mm(d_s[r * block : (r + 1) * block, :], a_s[...], NN)
            term = jnp.sum(made * xs[r][...].astype(F32), axis=0, keepdims=True)
            total = term if total is None else total + term
            (far if r % 2 else near)[r // 2] = made.astype(BF16)
        sums[...] = jnp.broadcast_to(total, (8, width))

    outs = [((2, block, width), BF16)] * 2 + [((8, width), F32)]
    return call(kernel, outs, "project_tokens", [((8 * HEAD, width), BF16)], 100)(ids, grads, *x, *arrays)


def settle_attn(ids, grads, out_sums):
    flat = [array for pair in grads for array in pair]
    each = len(grads[0])
    _, high, part = flat[0].shape
    low = out_sums.shape[1]

    def kernel(ids, *refs):
        late, early, (out_s,), outs = split(refs, each, each, 1, 4)
        for k, out in enumerate(outs):
            pair = early if k < 2 else late
            total = pair[0][k % 2]
            if each == 2:
                total = (total.astype(F32) + pair[1][k % 2].astype(F32)).astype(BF16)
            out[:high, :] = total
            out[high:, :] = out_s[k]

    return call(kernel, [(high + low, part)] * 4, "settle_attn")(ids, *flat, out_sums)


def feed(ids, x, grads, weights):
    block, width = x[0].shape
    part, units = weights[0][0].shape[-2:]
    parts = width // part
    rows, every = 2 * block, 4 * units
    arrays = list({id(item[0]): item[0] for item in weights}.values())
    index = {id(array): i for i, array in enumerate(arrays)}

    def kernel(ids, *refs):
        xs, gs, ws, ffn, two, (hid, dgate, dup), (x_s, g_s, w_s) = split(refs, 2, 2, len(arrays), 2, 2, 3, 3)
        at = [pl.multiple_of(place, LANES) for place in offsets(ids, parts, part)]
        for r in range(2):
            x_s[r * block : (r + 1) * block, :] = xs[r][...]
            g_s[r * block : (r + 1) * block, :] = gs[r][...]
        for array, where, m, k, p in weights:
            w_s[m, pl.ds(at[p], part), k * units : (k + 1) * units] = ws[index[id(array)]][where]

        def eighth(i, _):
            lanes = pl.ds(pl.multiple_of(i // 2 * units, LANES), units)
            at = pl.ds(pl.multiple_of(lax.rem(i, 2) * block, block), block)
            gate = mm(x_s[at, :], w_s[0, :, lanes], NN)
            up = mm(x_s[at, :], w_s[1, :, lanes], NN)
            back = mm(g_s[at, :], w_s[2, :, lanes], NN)
            sigma = 0.5 * jnp.tanh(0.5 * gate) + 0.5
            swish = gate * sigma
            hid[at, lanes] = (swish * up).astype(BF16)
            dup[at, lanes] = (back * swish).astype(BF16)
            dgate[at, lanes] = (back * up * (sigma + swish * (1.0 - sigma))).astype(BF16)
            return 0

        lax.fori_loop(0, 8, eighth, 0)
        cut = width // 3

        def third(p, _):
            lanes = pl.ds(pl.multiple_of(p * cut, LANES), cut)
            made = mm(dgate[...], w_s[0, lanes, :], NT) + mm(dup[...], w_s[1, lanes, :], NT)
            for r in range(2):
                two[r][:, lanes] = made[r * block : (r + 1) * block].astype(BF16)
            made = mm(hid[...], w_s[2, lanes, :], NT)
            for r in range(2):
                ffn[r][:, lanes] = made[r * block : (r + 1) * block].astype(BF16)
            return 0

        lax.fori_loop(0, 3, third, 0)

    outs = [(block, width)] * 4 + [(rows, every)] * 3
    scratch = [((rows, width), BF16), ((rows, width), BF16), ((3, width, every), BF16)]
    made = call(kernel, outs, "feed", scratch, 18, 34)(ids, *x, *grads, *arrays)
    return made[:2], made[2:4], made[4:]


def feed_weights(ids, x, grads, near, far, parts):
    block, width = x[0].shape
    part = width // parts
    half, every = near[0].shape
    units = every // 4

    def kernel(ids, *refs):
        xs, gs, ns, fs, outs, (rows_s, h_s) = split(refs, SPANS, SPANS, 3, 3, 4 * parts, 2)
        at = offsets(ids, parts, part)
        for r in range(SPANS):
            rows_s[0, r * block : (r + 1) * block, :] = xs[r][...]
            rows_s[1, r * block : (r + 1) * block, :] = gs[r][...]
        for m in range(3):
            h_s[m, :half] = ns[m][...]
            h_s[m, half:] = fs[m][...]

        def one(m, _):
            side = lax.rem(m + 1, 3)
            left = m // 2
            for p in reversed(range(parts)):
                total = mm(rows_s[left, :, pl.ds(at[p], part)], h_s[side], TN)
                for k in range(4):
                    outs[k * parts + p][m] = total[:, k * units : (k + 1) * units].astype(BF16)
            return 0

        lax.fori_loop(0, 3, one, 0)

    outs = [(3, part, units)] * (4 * parts)
    scratch = [((2, 4 * block, width), BF16), ((3, 4 * block, every), BF16)]
    return call(kernel, outs, "feed_weights", scratch, 17, 40)(ids, *x, *grads, *near, *far)


def finish_ffn(ids, pieces, gain):
    _, shard, units = pieces[0].shape
    every = SPANS * units

    def kernel(ids, *refs):
        pieces, (gain,), (gate, up, down) = split(refs, SPANS, 1, 3)
        scale = gain[...]
        for r, piece in enumerate(pieces):
            lanes = pl.ds(pl.multiple_of((ids[1] ^ r) * units, LANES), units)
            gate[:, lanes] = piece[0].astype(F32) * scale
            up[:, lanes] = piece[1].astype(F32) * scale
            down[:, lanes] = piece[2].astype(F32)

    return call(kernel, [((shard, every), F32)] * 3, "finish_ffn")(ids, *pieces, gain)


def finish_attn(ids, pieces, gain):
    shard = pieces[0].shape[1]

    def kernel(ids, *refs):
        pieces, (gain,), (query, key, value, out_w), (made,) = split(refs, SPANS, 1, 4, 1)
        scale = gain[...]
        for r, piece in enumerate(pieces):
            made[ids[1] ^ r] = piece[...].astype(F32)
        for place in range(SPANS):
            lanes = slice(place * HEAD, (place + 1) * HEAD)
            half = slice(place // 2 * HEAD, (place // 2 + 1) * HEAD)
            out_w[:, lanes] = jnp.transpose(made[place, 2 * HEAD :])
            query[:, lanes] = jnp.transpose(made[place, :HEAD]) * scale
            (value if place % 2 else key)[:, half] = jnp.transpose(made[place, HEAD : 2 * HEAD]) * scale

    outs = [((shard, wide * HEAD), F32) for wide in (4, 2, 2, 4)]
    scratch = [((SPANS, 3 * HEAD, shard), F32)]
    return call(kernel, outs, "finish_attn", scratch)(ids, *pieces, gain)


def swap(value, axis):
    return lax.ppermute(value, axis, [(0, 1), (1, 0)])


def sent(value, axis, bits):
    return lax.ppermute(value, axis, [(i, i ^ bits) for i in range(lax.axis_size(axis))])


def gather_group(value):
    core = swap(value, "c")
    across = swap(value, "x")
    return value, core, across, swap(across, "c")


def scatter_group(near, far):
    total = near.astype(F32) + swap(far, "c").astype(F32)
    return total[0] + swap(total[1].astype(BF16), "x").astype(F32)


def scatter_halves(near, far):
    far_total = far[0].astype(F32) + swap(far[1], "c").astype(F32)
    crossing = swap(far_total.astype(BF16), "x")
    return near[0].astype(F32) + swap(near[1], "c").astype(F32) + crossing.astype(F32)


def exchange(pieces):
    return lax.all_to_all(pieces, "z", split_axis=0, concat_axis=0, tiled=True)


def spread(pieces):
    return [
        pieces[0],
        swap(pieces[1], "c"),
        swap(pieces[2], "x"),
        lax.ppermute(pieces[3], ("x", "c"), [(i, 3 - i) for i in range(SPANS)]),
    ]


def beside(mine, dim):
    if lax.axis_size("y") == 2:
        return [mine, swap(mine, "y")]
    return [lax.all_gather(mine, "y", axis=dim, tiled=True)]


def along_z(mine):
    if lax.axis_size("z") != 4:
        return [mine] + [sent(mine, "z", k) for k in range(1, lax.axis_size("z"))]
    far = sent(mine, "z", 3)
    return [mine, sent(mine, "z", 1), sent(far, "z", 1), far]


def onto_z(pieces):
    far = pieces[3].astype(F32) + sent(pieces[2], "z", 1).astype(F32)
    near = pieces[0].astype(F32) + sent(pieces[1], "z", 1).astype(F32)
    return (near + sent(far.astype(BF16), "z", 3).astype(F32)).astype(BF16)


def settled(pieces, parts, dim):
    if parts == 2:
        sums = [
            (pieces[2 * k].astype(F32) + swap(pieces[2 * k + 1], "y").astype(F32)).astype(BF16) for k in range(4)
        ]
    else:
        sums = [lax.psum_scatter(piece, "y", scatter_dimension=dim, tiled=True) for piece in pieces]
    return onto_z(sums)


def halved(values, rest, axis, dim):
    if lax.axis_size(axis) != 2:
        values, rest = lax.psum((values, rest), axis)
        return lax.dynamic_index_in_dim(values, lax.axis_index(axis), dim, keepdims=False), rest
    here = lax.axis_index(axis)
    kept = lax.dynamic_index_in_dim(values, here, dim, keepdims=False)
    gone = lax.dynamic_index_in_dim(values, 1 - here, dim, keepdims=False)
    came = swap(jnp.concatenate([gone.reshape(-1), rest]), axis)
    return kept + came[: kept.size].reshape(kept.shape), rest + came[kept.size :]


def over_z(value):
    return value + sum(sent(value, "z", k) for k in range(1, lax.axis_size("z")))


def unit(values):
    scale = lax.rsqrt(jnp.mean(values * values, axis=-1, keepdims=True) + EPSILON)
    return values * scale, scale


def unit_back(values, scale, grad):
    inner = jnp.mean(grad * values, axis=-1, keepdims=True)
    return scale * grad - values * (scale * scale * scale) * inner


def per_device(tokens, w_query, w_key, w_value, w_out, w_gate, w_up, w_down, norm_attn, norm_ffn, grad_out):
    sequences, count = lax.axis_size("y"), lax.axis_size("z")
    parts = 2 if sequences == 2 else 1
    block, width = tokens.shape
    shard = w_query.shape[0]
    t = lax.axis_index("x") * 2 + lax.axis_index("c")
    ids = jnp.stack([lax.axis_index("z"), t, lax.axis_index("y")]).astype(jnp.int32)
    gain_attn = norm_attn.astype(F32)[:, None]
    gain_ffn = norm_ffn.astype(F32)[:, None]

    fence = lax.optimization_barrier

    resid = tokens.astype(F32)
    unit_one, scale_one = unit(resid)
    attn_pieces, low_one = fence((prepare_attn(ids, w_query, w_key, w_value, w_out, gain_attn), unit_one.astype(BF16)))
    attn_mine = join_attn(ids, spread(attn_pieces))
    lane = jnp.arange(LANES)
    freq = ROPE_BASE ** (-(lane % (HEAD // 2) * 2.0) / HEAD)
    inner = jnp.arange(block, dtype=F32)[:, None] * freq
    outer = (jnp.arange(SEQUENCE_LENGTH // block, dtype=F32) * block)[:, None] * freq
    sign = jnp.where(lane < HEAD // 2, -1.0, 1.0)
    tables = (jnp.cos(inner), jnp.sin(inner) * sign, jnp.cos(outer), jnp.sin(outer) * sign)
    attn_mine, ffn_pieces, tables, low_one = fence(
        (attn_mine, prepare_ffn(ids, w_gate, w_up, w_down, gain_ffn), tables, low_one)
    )

    attn_three, attn_one = sent(attn_mine, "z", 3), sent(attn_mine, "z", 1)
    own = beside(attn_mine, 1)
    ffn_mine = join_ffn(ids, spread(ffn_pieces))
    core, across = swap(low_one, "c"), swap(low_one, "x")
    ffn_mine, attn_three, attn_one, own = fence((ffn_mine, attn_three, attn_one, own))
    attn_two = sent(attn_three, "z", 1)
    three_one = beside(jnp.stack([attn_three, attn_one]), 2)
    gate_three = sent(ffn_mine[0], "z", 3)
    attn_two, three_one, gate_three, ffn_mine, core, across = fence(
        (attn_two, three_one, gate_three, ffn_mine, core, across)
    )
    x_one = (low_one, core, across, swap(across, "c"))
    two = beside(attn_two, 1)
    attn_weights = [
        [(array, ()) for array in own],
        [(array, (1,)) for array in three_one],
        [(array, ()) for array in two],
        [(array, (0,)) for array in three_one],
    ]
    gate_one, up_three = sent(ffn_mine[0], "z", 1), sent(ffn_mine[1], "z", 3)
    made = project(ids, x_one, attn_weights, tables)
    made, gate_one, up_three, gate_three, ffn_mine, grad_in = fence(
        (made, gate_one, up_three, gate_three, ffn_mine, grad_out)
    )

    made = exchange(made)
    ffn_own = beside(ffn_mine, 1)
    g_rows = gather_group(grad_in)
    by_one = jnp.stack([ffn_mine[1], gate_three])
    first = jnp.stack([gate_three, gate_one, up_three])
    made, ffn_own, g_rows, by_one, first, down_mine, orel = fence(
        (made, ffn_own, g_rows, by_one, first, ffn_mine[2], out_weights(ids, attn_weights))
    )
    by_one, down_three = sent(by_one, "z", 1), sent(down_mine, "z", 3)
    first = beside(first, 1)
    other = swap(made[:, :, SPANS * HEAD :], "c")
    attended, q_seq, kv_seq, o_seq, lse = attend(ids, made, other)
    attended, down_three, by_one, first, up_three, down_mine = fence(
        (attended, down_three, by_one, first, up_three, down_mine)
    )
    attended = exchange(attended)
    by_one = beside(by_one, 1)
    down_one = sent(down_mine, "z", 1)
    both_two = jnp.stack([up_three, down_three])
    attended, by_one, down_one, down_three, both_two = fence((attended, by_one, down_one, down_three, both_two))
    both_two = sent(both_two, "z", 1)
    down_three, down_one = beside(down_three, 0), beside(down_one, 0)
    near, far, att = out_project(ids, attended, orel)
    branch_attn = scatter_group(near, far)
    state = resid + branch_attn
    unit_two, scale_two = unit(state)
    low_two, both_two, down_three, down_one = fence((unit_two.astype(BF16), both_two, down_three, down_one))
    x_two = gather_group(low_two)
    both_two = beside(both_two, 1)
    x_two, both_two = fence((x_two, both_two))

    ffn_weights = []
    for p in range(parts):
        ffn_weights += [(ffn_own[p], (m,), m, 0, p) for m in range(3)]
        ffn_weights += [(first[p], (i,), *place, p) for i, place in enumerate(((0, 3), (0, 1), (1, 3)))]
        ffn_weights += [(by_one[p], (i,), *place, p) for i, place in enumerate(((1, 1), (0, 2)))]
        ffn_weights += [(down_three[p], (Ellipsis,), 2, 3, p), (down_one[p], (Ellipsis,), 2, 1, p)]
        ffn_weights += [(both_two[p], (0,), 1, 2, p), (both_two[p], (1,), 2, 2, p)]
    ffn_far, two_far, kept_far = feed(ids, x_two[2:], g_rows[2:], ffn_weights)
    crossing = (two_far[0].astype(F32) + swap(two_far[1], "c").astype(F32)).astype(BF16)
    crossing, x_near = fence((crossing, x_two[:2]))
    crossing = swap(crossing, "x")
    ffn_near, two_near, kept_near = feed(ids, x_near, g_rows[:2], ffn_weights)
    two_near, crossing = fence((two_near, crossing))
    grad_unit_two = two_near[0].astype(F32) + swap(two_near[1], "c").astype(F32) + crossing.astype(F32)
    grad_state = grad_out.astype(F32) + unit_back(state, scale_two, grad_unit_two)
    state_low, kept_near, ffn_near, ffn_far, grad_unit_two = fence(
        (grad_state.astype(BF16), kept_near, ffn_near, ffn_far, grad_unit_two)
    )
    across, core = swap(state_low, "x"), swap(state_low, "c")
    feed_grads = feed_weights(ids, x_two, g_rows, kept_near, kept_far, parts)
    across, core, feed_grads = fence((across, core, feed_grads))
    g_state = (state_low, core, across, swap(across, "c"))

    def home(total):
        pieces = total.reshape(*total.shape[:-2], SPANS, shard, total.shape[-1])
        return spread([lax.dynamic_index_in_dim(pieces, t ^ r, pieces.ndim - 3, keepdims=False) for r in range(SPANS)])

    def crossed(grads, k):
        if parts == 1:
            return lax.psum_scatter(grads[k], "y", scatter_dimension=1, tiled=True)
        return swap(grads[2 * k + 1], "y")

    def added(grads, k, came):
        return came if parts == 1 else (grads[2 * k].astype(F32) + came.astype(F32)).astype(BF16)

    two_came = crossed(feed_grads, 2)
    grad_att, out_grads = out_back(ids, g_state, att, orel, parts)
    grad_att = exchange(grad_att)
    onward = added(feed_grads, 2, two_came)
    grad_att, onward, feed_grads, out_grads = fence((grad_att, onward, feed_grads, out_grads))
    onward = sent(onward, "z", 1)
    three_came = crossed(feed_grads, 3)
    if parts == 2:
        out_sums = out_grads[0].astype(F32) + swap(out_grads[1], "y").astype(F32)
    else:
        out_sums = lax.psum_scatter(out_grads[0], "y", scatter_dimension=2, tiled=True)
    dq, keep, give = attend_back(ids, q_seq, kv_seq, o_seq, lse, tables, grad_att)
    dq, keep, give, onward, three_came, feed_grads, ffn_near, ffn_far, out_sums = fence(
        (dq, keep, give, onward, three_came, feed_grads, ffn_near, ffn_far, out_sums.astype(BF16))
    )
    one_came = crossed(feed_grads, 1)
    grads_heads = exchange(pack(ids, dq, keep, swap(give, "c")))
    branch_ffn = scatter_halves(ffn_near, ffn_far)
    result = state + branch_ffn
    gain_two = jnp.sum(grad_unit_two * unit_two, axis=0)
    squares = jnp.stack([jnp.sum(result * result), jnp.sum(branch_attn * branch_attn), jnp.sum(branch_ffn * branch_ffn)])
    onward = (added(feed_grads, 3, three_came).astype(F32) + onward.astype(F32)).astype(BF16)
    onward, onward_down = onward[:2], onward[2:]
    one_sum = added(feed_grads, 1, one_came)
    grads_heads, result, squares, gain_two, onward, onward_down, one_sum, feed_grads = fence(
        (grads_heads, result, squares, gain_two, onward, onward_down, one_sum, feed_grads)
    )
    onward = sent(onward, "z", 3)
    feed_one = sent(one_sum, "z", 1)
    grads_qkv, qkv_grads = project_weights(ids, grads_heads, x_one, parts)
    grads_qkv, qkv_grads = fence((grads_qkv, qkv_grads))
    near, far, gain_one = project_tokens(ids, grads_qkv, x_one, attn_weights)
    if parts == 2:
        gone = [(kept, swap(piece, "y")) for kept, piece in zip(qkv_grads[:2], qkv_grads[2:])]
    else:
        gone = [(lax.psum_scatter(piece, "y", scatter_dimension=2, tiled=True),) for piece in qkv_grads]
    own_came = crossed(feed_grads, 0)
    gains = jnp.stack([gain_one[0], gain_two]).reshape(2, sequences, 2, 2, shard)
    sums = settle_attn(ids, gone, out_sums)
    sums, feed_grads, onward, onward_down, feed_one, near, far, own_came, gains = fence(
        (sums, feed_grads, onward, onward_down, feed_one, near, far, own_came, gains)
    )
    onto_three = (sums[3].astype(F32) + sent(sums[2], "z", 1).astype(F32)).astype(BF16)
    onto_one = sent(sums[1], "z", 1)
    onward_down = sent(onward_down, "z", 3)
    total = near.astype(F32) + swap(far, "c").astype(F32)
    gains, squares = halved(gains, squares, "c", 3)
    crossing = swap(total[1].astype(BF16), "x")
    gains, squares = halved(gains, squares, "y", 1)
    feed_total = added(feed_grads, 0, own_came).astype(F32) + jnp.concatenate([onward, onward_down]).astype(F32)
    feed_total = (feed_total + feed_one.astype(F32)).astype(BF16)
    onto_three, onto_one, crossing, feed_total, gains, squares = fence(
        (onto_three, onto_one, crossing, feed_total, gains, squares)
    )
    onto_three = sent(onto_three, "z", 3)
    feed_home = home(feed_total)
    grad_unit_one = total[0] + crossing.astype(F32)
    grad_tokens = (grad_state + unit_back(resid, scale_one, grad_unit_one)).astype(BF16)
    gains, squares = halved(gains, squares, "x", 1)
    onto_three, onto_one, feed_home, gains, squares, grad_tokens = fence(
        (onto_three, onto_one, feed_home, gains, squares, grad_tokens)
    )
    attn_home = spread(part_attn(ids, sums[0], onto_one, onto_three))
    attn_home, gains, squares = fence((attn_home, gains, squares))
    totals = over_z(jnp.concatenate([gains.reshape(-1), squares]))
    grad_gate, grad_up, grad_down = finish_ffn(ids, feed_home, gain_ffn)
    grad_query, grad_key, grad_value, grad_outproj = finish_attn(ids, attn_home, gain_attn)
    entries = block * width * sequences * SPANS * count
    return (
        result.astype(BF16),
        grad_tokens,
        grad_query,
        grad_key,
        grad_value,
        grad_outproj.T,
        grad_gate,
        grad_up,
        grad_down.T,
        totals[:shard] / gain_attn[:, 0],
        totals[shard : 2 * shard] / gain_ffn[:, 0],
        jnp.sqrt(totals[2 * shard :] / entries),
    )


def solution(mesh):
    fsdp, tensor = mesh.shape["fsdp"], mesh.shape["tensor"]
    split = Mesh(mesh.devices.reshape(fsdp // SPANS, 2, 2, tensor), ("y", "x", "c", "z"))
    rows = ("y", "x", "c")
    tok = P(("y", "x", "c", "z"), None)
    col, row, vec = P(rows, "z"), P("z", rows), P(rows)
    return jax.shard_map(
        per_device,
        mesh=split,
        in_specs=(tok, col, col, col, row, col, col, row, vec, vec, tok),
        out_specs=(tok, tok, col, col, col, row, col, col, row, vec, vec, P()),
        check_vma=False,
    )
```

```python
import functools
import jax
import jax.numpy as jnp
from jax import lax
from jax.experimental import pallas as pl
from jax.experimental.pallas import tpu as pltpu
from jax.sharding import Mesh, PartitionSpec as P

HEAD = 96
LANES = 128
SEQUENCE_LENGTH = 4096
SPANS = 4
EPSILON = 1e-05
ROPE_BASE = 100000.0
MASKED = -1e30
LOG2E = 1.4426950408889634
NT = (((1,), (1,)), ((), ()))
NN = (((1,), (0,)), ((), ()))
TN = (((0,), (0,)), ((), ()))
F32 = jnp.float32
BF16 = jnp.bfloat16


def mm(left, right, dims):
    return lax.dot_general(left, right, dims, preferred_element_type=F32)


def widen(piece):
    return jnp.concatenate([piece, jnp.zeros((piece.shape[0], LANES - HEAD), piece.dtype)], axis=1)


def swapped(value):
    half = HEAD // 2
    return jnp.concatenate([value[:, half:HEAD], value[:, :half]], axis=1)


def rotary(tables, place):
    cos_in, sin_in, cos_out, sin_out = tables
    at = pl.ds(place, 1)
    cosine = cos_out[at, :] * cos_in[...] - sin_out[at, :] * sin_in[...]
    return cosine, sin_out[at, :] * cos_in[...] + cos_out[at, :] * sin_in[...]


def attend_kernel(ids, own, other, out, q_s, kv_s, o_s, lse_s, acc_s, vt_s, *, block, tile):
    z, t = ids[0], ids[1]
    c = lax.rem(t, 2)
    spans = 4
    rows_all = q_s.shape[0]
    for zj in range(4):
        for r in range(spans):
            at = pl.multiple_of(((t ^ r) * spans + zj) * block, block)
            at_other = pl.multiple_of(((t ^ 1 ^ r) * spans + zj) * block, block)
            q_s[pl.ds(at, block), :] = widen(own[zj, :, r * HEAD : (r + 1) * HEAD])
            kv_s[c, pl.ds(at, block), :] = widen(own[zj, :, (spans + r) * HEAD : (spans + r + 1) * HEAD])
            kv_s[1 - c, pl.ds(at_other, block), :] = widen(other[zj, :, r * HEAD : (r + 1) * HEAD])
    factor = HEAD ** (-0.5) * LOG2E
    is_count = lax.broadcasted_iota(jnp.int32, (tile, LANES), 1) == HEAD

    def values(i, _):
        rows = pl.ds(pl.multiple_of(i * tile, tile), tile)
        vals = kv_s[1, rows, :]
        vt_s[:, rows] = jnp.transpose(jnp.where(is_count, jnp.ones_like(vals), vals))
        return 0

    lax.fori_loop(0, rows_all // tile, values, 0)

    def step(query, j, before, mask):
        rows = pl.ds(pl.multiple_of(j * tile, tile), tile)
        scores = mm(kv_s[0, rows, :], query, NT) * factor
        if mask is not None:
            scores = jnp.where(mask, scores, MASKED)
        top = jnp.maximum(before, jnp.max(scores, axis=0, keepdims=True))
        expo = jnp.exp2(scores - top).astype(BF16)
        acc_s[...] = acc_s[...] * jnp.exp2(before - top) + mm(vt_s[:, rows], expo, NN)
        return top

    def row_block(i, _):
        at = pl.multiple_of(i * tile, tile)
        query = q_s[pl.ds(at, tile), :]
        acc_s[...] = jnp.zeros_like(acc_s)
        top = lax.fori_loop(0, i, lambda j, top: step(query, j, top, None), jnp.full((1, tile), MASKED, F32))
        mask = lax.broadcasted_iota(jnp.int32, (tile, tile), 0) <= lax.broadcasted_iota(jnp.int32, (tile, tile), 1)
        top = step(query, i, top, mask)
        acc = acc_s[...]
        denom = acc[HEAD : HEAD + 1, :]
        o_s[pl.ds(at, tile), :] = jnp.transpose(acc / denom).astype(BF16)
        lse_s[:, pl.ds(at, tile)] = jnp.broadcast_to(top + jnp.log2(denom), (8, tile))
        return 0

    lax.fori_loop(0, rows_all // tile, row_block, 0)
    for zj in range(4):
        for r in range(spans):
            at = pl.multiple_of(((t ^ r) * spans + zj) * block, block)
            out[zj, :, r * HEAD : (r + 1) * HEAD] = o_s[pl.ds(at, block), :HEAD]


VM = pl.BlockSpec(memory_space=pltpu.VMEM)
SM = pl.BlockSpec(memory_space=pltpu.SMEM)


def shape(dims, dtype=BF16):
    return jax.ShapeDtypeStruct(dims, dtype)


def params(room):
    return pltpu.CompilerParams(vmem_limit_bytes=room * 1024 * 1024)


def attend(ids, own, other, tile=1024):
    block = own.shape[1]
    rows = block * 16
    return pl.pallas_call(
        functools.partial(attend_kernel, block=block, tile=tile),
        out_shape=[shape((4, block, 4 * HEAD)), shape((rows, LANES)), shape((2, rows, LANES)), shape((rows, LANES)), shape((8, rows), F32)],
        in_specs=[SM] + [VM] * 2,
        out_specs=[VM] * 5,
        scratch_shapes=[pltpu.VMEM((LANES, tile), F32), pltpu.VMEM((LANES, rows), BF16)],
        compiler_params=params(22),
        cost_estimate=pl.CostEstimate(flops=int(21e9), bytes_accessed=1, transcendentals=0),
        name="attend",
    )(ids, own, other)


def attend_back_kernel(ids, q_s, kv_s, o_s, lse_s, cos_in, sin_in, cos_out, sin_out, g, dq_out, keep_out, give_out, g_s, qx_s, kx_s, delta_s, dq_s, dk_s, dv_s, *, block, tile):
    z, t = ids[0], ids[1]
    spans = 4
    rows_all = q_s.shape[0]
    tiles = rows_all // tile
    for zj in range(4):
        for r in range(spans):
            at = pl.multiple_of(((t ^ r) * spans + zj) * block, block)
            g_s[pl.ds(at, block), :] = widen(g[zj, :, r * HEAD : (r + 1) * HEAD])

    def prepare(i, _):
        at = pl.multiple_of(i * tile, tile)
        rows = pl.ds(at, tile)
        query = q_s[rows, :]
        keys = kv_s[0, rows, :]
        qx_s[rows, :LANES] = query
        qx_s[rows, LANES:] = widen(swapped(query))
        kx_s[rows, :LANES] = keys
        kx_s[rows, LANES:] = widen(swapped(keys))
        both = g_s[rows, :].astype(F32) * o_s[rows, :].astype(F32)
        delta = jnp.sum(both, axis=1, keepdims=True)
        delta_s[:, rows] = jnp.transpose(jnp.broadcast_to(delta, (tile, LANES)))[:8]
        dq_s[rows, :] = jnp.zeros((tile, 2 * LANES), F32)
        return 0

    lax.fori_loop(0, tiles, prepare, 0)
    factor = HEAD ** (-0.5) * LOG2E
    scale = HEAD ** (-0.5)

    def step(i, keys, vals, kx, mask):
        rows = pl.ds(pl.multiple_of(i * tile, tile), tile)
        query = qx_s[rows, :]
        grad = g_s[rows, :]
        scores = mm(keys, query[:, :LANES], NT) * factor - lse_s[:1, rows]
        if mask is not None:
            scores = jnp.where(mask, scores, MASKED)
        prob = jnp.exp2(scores)
        through = mm(vals, grad, NT)
        ds = (prob * (through - delta_s[:1, rows])).astype(BF16)
        dv_s[...] += mm(prob.astype(BF16), grad, NN)
        dk_s[...] += mm(ds, query, NN)
        dq_s[rows, :] += mm(ds, kx, TN)

    def column_block(j, _):
        rows = pl.ds(pl.multiple_of(j * tile, tile), tile)
        kx = kx_s[rows, :]
        keys = kx[:, :LANES]
        vals = kv_s[1, rows, :]
        dk_s[...] = jnp.zeros_like(dk_s)
        dv_s[...] = jnp.zeros_like(dv_s)
        mask = lax.broadcasted_iota(jnp.int32, (tile, tile), 0) <= lax.broadcasted_iota(jnp.int32, (tile, tile), 1)
        step(j, keys, vals, kx, mask)
        lax.fori_loop(j + 1, tiles, lambda i, _: (step(i, keys, vals, kx, None), 0)[1], 0)
        dk = dk_s[...] * scale
        turns = [rotary((cos_in, sin_in, cos_out, sin_out), j * (tile // block) + b) for b in range(tile // block)]
        cosine, sine = (jnp.concatenate(parts, axis=0) for parts in zip(*turns))
        dk = dk[:, :LANES] * cosine - dk[:, LANES:] * sine
        dv = dv_s[...]
        first = lax.rem(t, 2) == 0
        keep_out[rows, :] = jnp.where(first, dk, dv).astype(BF16)
        give_out[rows, :] = jnp.where(first, dv, dk).astype(BF16)
        return 0

    lax.fori_loop(0, tiles, column_block, 0)
    for zj in range(4):
        for r in range(spans):
            rows = pl.ds(pl.multiple_of(((t ^ r) * spans + zj) * block, block), block)
            cosine, sine = rotary((cos_in, sin_in, cos_out, sin_out), (t ^ r) * spans + zj)
            dq = dq_s[rows, :] * scale
            dq_out[zj, :, r * HEAD : (r + 1) * HEAD] = (
                dq[:, :LANES] * cosine - dq[:, LANES:] * sine
            ).astype(BF16)[:, :HEAD]


def attend_back(ids, q, kv, o, lse, tables, grads, tile=1024):
    block = grads.shape[1]
    rows = block * 16
    return pl.pallas_call(
        functools.partial(attend_back_kernel, block=block, tile=tile),
        out_shape=[shape((4, block, 4 * HEAD))] + [shape((rows, LANES))] * 2,
        in_specs=[SM] + [VM] * 9,
        out_specs=[VM] * 3,
        scratch_shapes=[
            pltpu.VMEM((rows, LANES), BF16),
            pltpu.VMEM((rows, 2 * LANES), BF16),
            pltpu.VMEM((rows, 2 * LANES), BF16),
            pltpu.VMEM((8, rows), F32),
            pltpu.VMEM((rows, 2 * LANES), F32),
            pltpu.VMEM((tile, 2 * LANES), F32),
            pltpu.VMEM((tile, LANES), F32),
        ],
        compiler_params=params(36),
        cost_estimate=pl.CostEstimate(flops=int(39e9), bytes_accessed=1, transcendentals=0),
        name="attend_back",
    )(ids, q, kv, o, lse, *tables, grads)


def offsets(ids, count, part):
    if count == 1:
        return [0]
    return [pl.multiple_of(ids[2] * part, LANES), pl.multiple_of((1 - ids[2]) * part, LANES)]


def call(kernel, outs, name, scratch=(), micros=0, room=14):
    def run(ids, *args):
        return pl.pallas_call(
            kernel,
            out_shape=[shape(*o) if isinstance(o[0], tuple) else shape(o) for o in outs],
            in_specs=[SM] + [VM] * len(args),
            out_specs=[VM] * len(outs),
            scratch_shapes=[pltpu.VMEM(*item) for item in scratch],
            compiler_params=params(room),
            cost_estimate=pl.CostEstimate(flops=int(micros * 1e9) + 1, bytes_accessed=1, transcendentals=0),
            name=name,
        )(ids, *args)

    return run


def split(refs, *counts):
    refs = list(refs)
    groups = []
    for count in counts:
        groups.append(refs[:count])
        refs = refs[count:]
    return groups


def prepare_attn(ids, w_query, w_key, w_value, w_out, gain):
    shard = w_query.shape[0]

    def kernel(ids, query, key, value, out, gain, *refs):
        pieces, made = split(refs, SPANS, 1)
        made = made[0]
        scale = gain[...]

        def turned(ref, at):
            return jnp.transpose(ref[:, at * HEAD : (at + 1) * HEAD].astype(F32) * scale).astype(BF16)

        for place in range(SPANS):
            made[place, :HEAD] = turned(query, place)
            made[place, HEAD : 2 * HEAD] = turned(value if place % 2 else key, place // 2)
            made[place, 2 * HEAD :] = jnp.transpose(out[:, place * HEAD : (place + 1) * HEAD].astype(F32)).astype(BF16)
        for r in range(SPANS):
            pieces[r][...] = made[ids[1] ^ r]

    scratch = [((SPANS, 3 * HEAD, shard), BF16)]
    return call(kernel, [(3 * HEAD, shard)] * SPANS, "prepare_attn", scratch)(
        ids, w_query, w_key, w_value, w_out.T, gain
    )


def prepare_ffn(ids, w_gate, w_up, w_down, gain):
    shard = w_gate.shape[0]
    units = w_gate.shape[1] // SPANS

    def kernel(ids, gate, up, down, gain, *pieces):
        scale = gain[...]
        for r in range(SPANS):
            at = pl.multiple_of((ids[1] ^ r) * units, LANES)
            pieces[r][0] = (gate[:, pl.ds(at, units)].astype(F32) * scale).astype(BF16)
            pieces[r][1] = (up[:, pl.ds(at, units)].astype(F32) * scale).astype(BF16)
            pieces[r][2] = down[:, pl.ds(at, units)]

    return call(kernel, [(3, shard, units)] * SPANS, "prepare_ffn")(ids, w_gate, w_up, w_down.T, gain)


def join_attn(ids, pieces):
    rows, shard = pieces[0].shape

    def kernel(ids, *refs):
        pieces, (out,), (made,) = split(refs, SPANS, 1, 1)
        for r, piece in enumerate(pieces):
            made[ids[1] ^ r] = piece[...]
        for place in range(SPANS):
            out[:, place * shard : (place + 1) * shard] = made[place]

    return call(kernel, [(rows, SPANS * shard)], "join_attn", [((SPANS, rows, shard), BF16)])(ids, *pieces)[0]


def join_ffn(ids, pieces):
    _, shard, units = pieces[0].shape

    def kernel(ids, *refs):
        pieces, (out,) = split(refs, SPANS, 1)
        for r, piece in enumerate(pieces):
            out[:, pl.ds(pl.multiple_of((ids[1] ^ r) * shard, 16), shard), :] = piece[...]

    return call(kernel, [(3, SPANS * shard, units)], "join_ffn")(ids, *pieces)[0]


def part_attn(ids, own, one, three):
    rows, part = own.shape
    shard = part // SPANS

    def kernel(ids, own, one, three, *refs):
        pieces, (made,) = split(refs, SPANS, 1)
        total = (own[...].astype(F32) + one[...].astype(F32) + three[...].astype(F32)).astype(BF16)
        for place in range(SPANS):
            made[place] = total[:, place * shard : (place + 1) * shard]
        for r, piece in enumerate(pieces):
            piece[...] = made[ids[1] ^ r]

    return call(kernel, [(rows, shard)] * SPANS, "part_attn", [((SPANS, rows, shard), BF16)])(ids, own, one, three)


def distinct(items):
    arrays = list({id(item[0]): item[0] for item in items}.values())
    index = {id(array): i for i, array in enumerate(arrays)}

    def rows_of(refs, item, rows):
        return refs[index[id(item[0])]][(*item[1], rows)]

    return arrays, rows_of


def project(ids, x, weights, tables):
    block = x[0].shape[0]
    parts = len(weights[0])
    part = weights[0][0][0].shape[-1]
    arrays, rows_of = distinct([item for items in weights for item in items])
    first = slice(0, 2 * HEAD)

    def kernel(ids, *refs):
        xs, ws, tables, (out,) = split(refs, SPANS, len(arrays), 4, 1)
        z, t = ids[0], ids[1]
        at = offsets(ids, parts, part)
        is_value = lax.rem(t, 2) == 1
        for r, x in enumerate(xs):
            cosine, sine = rotary(tables, (t ^ r) * SPANS + z)
            cosine, sine = cosine[:, :HEAD], sine[:, :HEAD]
            cos_kv = jnp.where(is_value, 1.0, cosine)
            sin_kv = jnp.where(is_value, 0.0, sine)
            for k in range(4):
                made = sum(mm(x[:, pl.ds(at[p], part)], rows_of(ws, weights[k][p], first), NT) for p in range(parts))
                query, other = made[:, :HEAD], made[:, HEAD:]
                out[z ^ k, :, r * HEAD : (r + 1) * HEAD] = (query * cosine + swapped(query) * sine).astype(BF16)
                out[z ^ k, :, (SPANS + r) * HEAD : (SPANS + r + 1) * HEAD] = (
                    other * cos_kv + swapped(other) * sin_kv
                ).astype(BF16)

    return call(kernel, [(4, block, 8 * HEAD)], "project")(ids, *x, *arrays, *tables)[0]


def out_weights(ids, weights):
    parts = len(weights[0])
    part = weights[0][0][0].shape[-1]
    arrays, rows_of = distinct([item for items in weights for item in items])

    def kernel(ids, *refs):
        ws, (orel,) = split(refs, len(arrays), 1)
        at = offsets(ids, parts, part)
        for j in range(4):
            for p in range(parts):
                orel[j * HEAD : (j + 1) * HEAD, pl.ds(at[p], part)] = rows_of(ws, weights[j][p], slice(2 * HEAD, 3 * HEAD))

    return call(kernel, [(4 * HEAD, parts * part)], "out_weights")(ids, *arrays)[0]


def out_project(ids, pieces, orel):
    block, width = pieces.shape[1], orel.shape[1]

    def kernel(ids, pieces, orel, near, far, att):
        for j in range(4):
            for r in range(SPANS):
                att[r * block : (r + 1) * block, j * HEAD : (j + 1) * HEAD] = pieces[ids[0] ^ j, :, r * HEAD : (r + 1) * HEAD]
        for r in (1, 3, 2, 0):
            made = mm(att[r * block : (r + 1) * block, :], orel[...], NN).astype(BF16)
            (far if r % 2 else near)[r // 2] = made

    outs = [(2, block, width)] * 2 + [(4 * block, 4 * HEAD)]
    return call(kernel, outs, "out_project")(ids, pieces, orel)


def out_back(ids, grads, att, orel, parts):
    block, width = grads[0].shape
    part = width // parts

    def kernel(ids, *refs):
        gs, (att, orel), (ds,), douts, (g_s,) = split(refs, SPANS, 2, 1, parts, 1)
        at = offsets(ids, parts, part)
        for r, grad in enumerate(gs):
            g_s[r * block : (r + 1) * block, :] = grad[...]
        made = mm(g_s[...], orel[...], NT).astype(BF16)
        for r in range(SPANS):
            for j in range(4):
                ds[ids[0] ^ j, :, r * HEAD : (r + 1) * HEAD] = made[r * block : (r + 1) * block, j * HEAD : (j + 1) * HEAD]
        for p in range(parts):
            total = mm(att[...], g_s[:, pl.ds(at[p], part)], TN)
            for k in range(4):
                douts[p][k] = total[k * HEAD : (k + 1) * HEAD].astype(BF16)

    outs = [(4, block, 4 * HEAD)] + [(4, HEAD, part)] * parts
    made = call(kernel, outs, "out_back", [((4 * block, width), BF16)])(ids, *grads, att, orel)
    return made[0], made[1:]


def pack(ids, queries, mine, theirs):
    _, block, wide = queries.shape

    def kernel(ids, queries, mine, theirs, out):
        t = ids[1]
        for zj in range(4):
            out[zj, :, :wide] = queries[zj]
            for r in range(SPANS):
                rows = pl.ds(pl.multiple_of(((t ^ r) * SPANS + zj) * block, block), block)
                total = (mine[rows, :].astype(F32) + theirs[rows, :].astype(F32)).astype(BF16)
                out[zj, :, wide + r * HEAD : wide + (r + 1) * HEAD] = total[:, :HEAD]

    return call(kernel, [(4, block, 2 * wide)], "pack")(ids, queries, mine, theirs)[0]


def project_weights(ids, grads, x, parts):
    block, width = x[0].shape
    part = width // parts

    def kernel(ids, *refs):
        (grads,), xs, (d_out,), das, (x_s,) = split(refs, 1, SPANS, 1, 2 * parts, 1)
        at = offsets(ids, parts, part)
        for j in range(4):
            for r in range(SPANS):
                for half in range(2):
                    lanes = slice((half * SPANS + r) * HEAD, (half * SPANS + r + 1) * HEAD)
                    d_out[r * block : (r + 1) * block, (2 * j + half) * HEAD : (2 * j + half + 1) * HEAD] = grads[
                        ids[0] ^ j, :, lanes
                    ]
        for r, x in enumerate(xs):
            x_s[r * block : (r + 1) * block, :] = x[...]
        for p in reversed(range(parts)):
            total = mm(d_out[...], x_s[:, pl.ds(at[p], part)], TN)
            for k in range(4):
                das[2 * p + (k < 2)][k % 2] = total[2 * k * HEAD : (2 * k + 2) * HEAD].astype(BF16)

    outs = [(4 * block, 8 * HEAD)] + [(2, 2 * HEAD, part)] * (2 * parts)
    made = call(kernel, outs, "project_weights", [((4 * block, width), BF16)], 100)(ids, grads, *x)
    return made[0], made[1:]


def project_tokens(ids, grads, x, weights):
    rows = grads.shape[0]
    block = rows // SPANS
    parts = len(weights[0])
    part = weights[0][0][0].shape[-1]
    width = parts * part
    arrays, rows_of = distinct([item for items in weights for item in items])

    def kernel(ids, *refs):
        (d_s,), xs, ws, (near, far, sums), (a_s,) = split(refs, 1, SPANS, len(arrays), 3, 1)
        at = offsets(ids, parts, part)
        for j in range(4):
            for p in range(parts):
                a_s[2 * j * HEAD : (2 * j + 2) * HEAD, pl.ds(at[p], part)] = rows_of(ws, weights[j][p], slice(0, 2 * HEAD))
        total = None
        for r in (1, 3, 2, 0):
            made = mm(d_s[r * block : (r + 1) * block, :], a_s[...], NN)
            term = jnp.sum(made * xs[r][...].astype(F32), axis=0, keepdims=True)
            total = term if total is None else total + term
            (far if r % 2 else near)[r // 2] = made.astype(BF16)
        sums[...] = jnp.broadcast_to(total, (8, width))

    outs = [((2, block, width), BF16)] * 2 + [((8, width), F32)]
    return call(kernel, outs, "project_tokens", [((8 * HEAD, width), BF16)], 100)(ids, grads, *x, *arrays)


def settle_attn(ids, grads, out_sums):
    flat = [array for pair in grads for array in pair]
    each = len(grads[0])
    _, high, part = flat[0].shape
    low = out_sums.shape[1]

    def kernel(ids, *refs):
        late, early, (out_s,), outs = split(refs, each, each, 1, 4)
        for k, out in enumerate(outs):
            pair = early if k < 2 else late
            total = pair[0][k % 2]
            if each == 2:
                total = (total.astype(F32) + pair[1][k % 2].astype(F32)).astype(BF16)
            out[:high, :] = total
            out[high:, :] = out_s[k]

    return call(kernel, [(high + low, part)] * 4, "settle_attn")(ids, *flat, out_sums)


def feed(ids, x, grads, weights):
    block, width = x[0].shape
    part, units = weights[0][0].shape[-2:]
    parts = width // part
    rows, every = 2 * block, 4 * units
    arrays = list({id(item[0]): item[0] for item in weights}.values())
    index = {id(array): i for i, array in enumerate(arrays)}

    def kernel(ids, *refs):
        xs, gs, ws, ffn, two, (hid, dgate, dup), (x_s, g_s, w_s) = split(refs, 2, 2, len(arrays), 2, 2, 3, 3)
        at = [pl.multiple_of(place, LANES) for place in offsets(ids, parts, part)]
        for r in range(2):
            x_s[r * block : (r + 1) * block, :] = xs[r][...]
            g_s[r * block : (r + 1) * block, :] = gs[r][...]
        for array, where, m, k, p in weights:
            w_s[m, pl.ds(at[p], part), k * units : (k + 1) * units] = ws[index[id(array)]][where]

        def eighth(i, _):
            lanes = pl.ds(pl.multiple_of(i // 2 * units, LANES), units)
            at = pl.ds(pl.multiple_of(lax.rem(i, 2) * block, block), block)
            gate = mm(x_s[at, :], w_s[0, :, lanes], NN)
            up = mm(x_s[at, :], w_s[1, :, lanes], NN)
            back = mm(g_s[at, :], w_s[2, :, lanes], NN)
            sigma = 0.5 * jnp.tanh(0.5 * gate) + 0.5
            swish = gate * sigma
            hid[at, lanes] = (swish * up).astype(BF16)
            dup[at, lanes] = (back * swish).astype(BF16)
            dgate[at, lanes] = (back * up * (sigma + swish * (1.0 - sigma))).astype(BF16)
            return 0

        lax.fori_loop(0, 8, eighth, 0)
        cut = width // 3

        def third(p, _):
            lanes = pl.ds(pl.multiple_of(p * cut, LANES), cut)
            made = mm(dgate[...], w_s[0, lanes, :], NT) + mm(dup[...], w_s[1, lanes, :], NT)
            for r in range(2):
                two[r][:, lanes] = made[r * block : (r + 1) * block].astype(BF16)
            made = mm(hid[...], w_s[2, lanes, :], NT)
            for r in range(2):
                ffn[r][:, lanes] = made[r * block : (r + 1) * block].astype(BF16)
            return 0

        lax.fori_loop(0, 3, third, 0)

    outs = [(block, width)] * 4 + [(rows, every)] * 3
    scratch = [((rows, width), BF16), ((rows, width), BF16), ((3, width, every), BF16)]
    made = call(kernel, outs, "feed", scratch, 18, 34)(ids, *x, *grads, *arrays)
    return made[:2], made[2:4], made[4:]


def feed_weights(ids, x, grads, near, far, parts):
    block, width = x[0].shape
    part = width // parts
    half, every = near[0].shape
    units = every // 4

    def kernel(ids, *refs):
        xs, gs, ns, fs, outs, (rows_s, h_s) = split(refs, SPANS, SPANS, 3, 3, 4 * parts, 2)
        at = offsets(ids, parts, part)
        for r in range(SPANS):
            rows_s[0, r * block : (r + 1) * block, :] = xs[r][...]
            rows_s[1, r * block : (r + 1) * block, :] = gs[r][...]
        for m in range(3):
            h_s[m, :half] = ns[m][...]
            h_s[m, half:] = fs[m][...]

        def one(m, _):
            side = lax.rem(m + 1, 3)
            left = m // 2
            for p in reversed(range(parts)):
                total = mm(rows_s[left, :, pl.ds(at[p], part)], h_s[side], TN)
                for k in range(4):
                    outs[k * parts + p][m] = total[:, k * units : (k + 1) * units].astype(BF16)
            return 0

        lax.fori_loop(0, 3, one, 0)

    outs = [(3, part, units)] * (4 * parts)
    scratch = [((2, 4 * block, width), BF16), ((3, 4 * block, every), BF16)]
    return call(kernel, outs, "feed_weights", scratch, 17, 40)(ids, *x, *grads, *near, *far)


def finish_ffn(ids, pieces, gain):
    _, shard, units = pieces[0].shape
    every = SPANS * units

    def kernel(ids, *refs):
        pieces, (gain,), (gate, up, down) = split(refs, SPANS, 1, 3)
        scale = gain[...]
        for r, piece in enumerate(pieces):
            lanes = pl.ds(pl.multiple_of((ids[1] ^ r) * units, LANES), units)
            gate[:, lanes] = piece[0].astype(F32) * scale
            up[:, lanes] = piece[1].astype(F32) * scale
            down[:, lanes] = piece[2].astype(F32)

    return call(kernel, [((shard, every), F32)] * 3, "finish_ffn")(ids, *pieces, gain)


def finish_attn(ids, pieces, gain):
    shard = pieces[0].shape[1]

    def kernel(ids, *refs):
        pieces, (gain,), (query, key, value, out_w), (made,) = split(refs, SPANS, 1, 4, 1)
        scale = gain[...]
        for r, piece in enumerate(pieces):
            made[ids[1] ^ r] = piece[...].astype(F32)
        for place in range(SPANS):
            lanes = slice(place * HEAD, (place + 1) * HEAD)
            half = slice(place // 2 * HEAD, (place // 2 + 1) * HEAD)
            out_w[:, lanes] = jnp.transpose(made[place, 2 * HEAD :])
            query[:, lanes] = jnp.transpose(made[place, :HEAD]) * scale
            (value if place % 2 else key)[:, half] = jnp.transpose(made[place, HEAD : 2 * HEAD]) * scale

    outs = [((shard, wide * HEAD), F32) for wide in (4, 2, 2, 4)]
    scratch = [((SPANS, 3 * HEAD, shard), F32)]
    return call(kernel, outs, "finish_attn", scratch)(ids, *pieces, gain)


def swap(value, axis):
    return lax.ppermute(value, axis, [(0, 1), (1, 0)])


def sent(value, axis, bits):
    return lax.ppermute(value, axis, [(i, i ^ bits) for i in range(lax.axis_size(axis))])


def gather_group(value):
    core = swap(value, "c")
    across = swap(value, "x")
    return value, core, across, swap(across, "c")


def scatter_group(near, far):
    total = near.astype(F32) + swap(far, "c").astype(F32)
    return total[0] + swap(total[1].astype(BF16), "x").astype(F32)


def scatter_halves(near, far):
    far_total = far[0].astype(F32) + swap(far[1], "c").astype(F32)
    crossing = swap(far_total.astype(BF16), "x")
    return near[0].astype(F32) + swap(near[1], "c").astype(F32) + crossing.astype(F32)


def exchange(pieces):
    return lax.all_to_all(pieces, "z", split_axis=0, concat_axis=0, tiled=True)


def spread(pieces):
    return [
        pieces[0],
        swap(pieces[1], "c"),
        swap(pieces[2], "x"),
        lax.ppermute(pieces[3], ("x", "c"), [(i, 3 - i) for i in range(SPANS)]),
    ]


def beside(mine, dim):
    if lax.axis_size("y") == 2:
        return [mine, swap(mine, "y")]
    return [lax.all_gather(mine, "y", axis=dim, tiled=True)]


def along_z(mine):
    if lax.axis_size("z") != 4:
        return [mine] + [sent(mine, "z", k) for k in range(1, lax.axis_size("z"))]
    far = sent(mine, "z", 3)
    return [mine, sent(mine, "z", 1), sent(far, "z", 1), far]


def onto_z(pieces):
    far = pieces[3].astype(F32) + sent(pieces[2], "z", 1).astype(F32)
    near = pieces[0].astype(F32) + sent(pieces[1], "z", 1).astype(F32)
    return (near + sent(far.astype(BF16), "z", 3).astype(F32)).astype(BF16)


def settled(pieces, parts, dim):
    if parts == 2:
        sums = [
            (pieces[2 * k].astype(F32) + swap(pieces[2 * k + 1], "y").astype(F32)).astype(BF16) for k in range(4)
        ]
    else:
        sums = [lax.psum_scatter(piece, "y", scatter_dimension=dim, tiled=True) for piece in pieces]
    return onto_z(sums)


def halved(values, rest, axis, dim):
    if lax.axis_size(axis) != 2:
        values, rest = lax.psum((values, rest), axis)
        return lax.dynamic_index_in_dim(values, lax.axis_index(axis), dim, keepdims=False), rest
    here = lax.axis_index(axis)
    kept = lax.dynamic_index_in_dim(values, here, dim, keepdims=False)
    gone = lax.dynamic_index_in_dim(values, 1 - here, dim, keepdims=False)
    came = swap(jnp.concatenate([gone.reshape(-1), rest]), axis)
    return kept + came[: kept.size].reshape(kept.shape), rest + came[kept.size :]


def over_z(value):
    return value + sum(sent(value, "z", k) for k in range(1, lax.axis_size("z")))


def unit(values):
    scale = lax.rsqrt(jnp.mean(values * values, axis=-1, keepdims=True) + EPSILON)
    return values * scale, scale


def unit_back(values, scale, grad):
    inner = jnp.mean(grad * values, axis=-1, keepdims=True)
    return scale * grad - values * (scale * scale * scale) * inner


def per_device(tokens, w_query, w_key, w_value, w_out, w_gate, w_up, w_down, norm_attn, norm_ffn, grad_out):
    sequences, count = lax.axis_size("y"), lax.axis_size("z")
    parts = 2 if sequences == 2 else 1
    block, width = tokens.shape
    shard = w_query.shape[0]
    t = lax.axis_index("x") * 2 + lax.axis_index("c")
    ids = jnp.stack([lax.axis_index("z"), t, lax.axis_index("y")]).astype(jnp.int32)
    gain_attn = norm_attn.astype(F32)[:, None]
    gain_ffn = norm_ffn.astype(F32)[:, None]

    fence = lax.optimization_barrier

    resid = tokens.astype(F32)
    unit_one, scale_one = unit(resid)
    attn_pieces, low_one = fence((prepare_attn(ids, w_query, w_key, w_value, w_out, gain_attn), unit_one.astype(BF16)))
    attn_mine = join_attn(ids, spread(attn_pieces))
    lane = jnp.arange(LANES)
    freq = ROPE_BASE ** (-(lane % (HEAD // 2) * 2.0) / HEAD)
    inner = jnp.arange(block, dtype=F32)[:, None] * freq
    outer = (jnp.arange(SEQUENCE_LENGTH // block, dtype=F32) * block)[:, None] * freq
    sign = jnp.where(lane < HEAD // 2, -1.0, 1.0)
    tables = (jnp.cos(inner), jnp.sin(inner) * sign, jnp.cos(outer), jnp.sin(outer) * sign)
    attn_mine, ffn_pieces, tables, low_one = fence(
        (attn_mine, prepare_ffn(ids, w_gate, w_up, w_down, gain_ffn), tables, low_one)
    )

    attn_three, attn_one = sent(attn_mine, "z", 3), sent(attn_mine, "z", 1)
    own = beside(attn_mine, 1)
    ffn_mine = join_ffn(ids, spread(ffn_pieces))
    core, across = swap(low_one, "c"), swap(low_one, "x")
    ffn_mine, attn_three, attn_one, own = fence((ffn_mine, attn_three, attn_one, own))
    attn_two = sent(attn_three, "z", 1)
    three_one = beside(jnp.stack([attn_three, attn_one]), 2)
    gate_three = sent(ffn_mine[0], "z", 3)
    attn_two, three_one, gate_three, ffn_mine, core, across = fence(
        (attn_two, three_one, gate_three, ffn_mine, core, across)
    )
    x_one = (low_one, core, across, swap(across, "c"))
    two = beside(attn_two, 1)
    attn_weights = [
        [(array, ()) for array in own],
        [(array, (1,)) for array in three_one],
        [(array, ()) for array in two],
        [(array, (0,)) for array in three_one],
    ]
    gate_one, up_three = sent(ffn_mine[0], "z", 1), sent(ffn_mine[1], "z", 3)
    made = project(ids, x_one, attn_weights, tables)
    made, gate_one, up_three, gate_three, ffn_mine, grad_in = fence(
        (made, gate_one, up_three, gate_three, ffn_mine, grad_out)
    )

    made = exchange(made)
    ffn_own = beside(ffn_mine, 1)
    g_rows = gather_group(grad_in)
    by_one = jnp.stack([ffn_mine[1], gate_three])
    first = jnp.stack([gate_three, gate_one, up_three])
    made, ffn_own, g_rows, by_one, first, down_mine, orel = fence(
        (made, ffn_own, g_rows, by_one, first, ffn_mine[2], out_weights(ids, attn_weights))
    )
    by_one, down_three = sent(by_one, "z", 1), sent(down_mine, "z", 3)
    first = beside(first, 1)
    other = swap(made[:, :, SPANS * HEAD :], "c")
    attended, q_seq, kv_seq, o_seq, lse = attend(ids, made, other)
    attended, down_three, by_one, first, up_three, down_mine = fence(
        (attended, down_three, by_one, first, up_three, down_mine)
    )
    attended = exchange(attended)
    by_one = beside(by_one, 1)
    down_one = sent(down_mine, "z", 1)
    both_two = jnp.stack([up_three, down_three])
    attended, by_one, down_one, down_three, both_two = fence((attended, by_one, down_one, down_three, both_two))
    both_two = sent(both_two, "z", 1)
    down_three, down_one = beside(down_three, 0), beside(down_one, 0)
    near, far, att = out_project(ids, attended, orel)
    branch_attn = scatter_group(near, far)
    state = resid + branch_attn
    unit_two, scale_two = unit(state)
    low_two, both_two, down_three, down_one = fence((unit_two.astype(BF16), both_two, down_three, down_one))
    x_two = gather_group(low_two)
    both_two = beside(both_two, 1)
    x_two, both_two = fence((x_two, both_two))

    ffn_weights = []
    for p in range(parts):
        ffn_weights += [(ffn_own[p], (m,), m, 0, p) for m in range(3)]
        ffn_weights += [(first[p], (i,), *place, p) for i, place in enumerate(((0, 3), (0, 1), (1, 3)))]
        ffn_weights += [(by_one[p], (i,), *place, p) for i, place in enumerate(((1, 1), (0, 2)))]
        ffn_weights += [(down_three[p], (Ellipsis,), 2, 3, p), (down_one[p], (Ellipsis,), 2, 1, p)]
        ffn_weights += [(both_two[p], (0,), 1, 2, p), (both_two[p], (1,), 2, 2, p)]
    ffn_far, two_far, kept_far = feed(ids, x_two[2:], g_rows[2:], ffn_weights)
    crossing = (two_far[0].astype(F32) + swap(two_far[1], "c").astype(F32)).astype(BF16)
    crossing, x_near = fence((crossing, x_two[:2]))
    crossing = swap(crossing, "x")
    ffn_near, two_near, kept_near = feed(ids, x_near, g_rows[:2], ffn_weights)
    two_near, crossing = fence((two_near, crossing))
    grad_unit_two = two_near[0].astype(F32) + swap(two_near[1], "c").astype(F32) + crossing.astype(F32)
    grad_state = grad_out.astype(F32) + unit_back(state, scale_two, grad_unit_two)
    state_low, kept_near, ffn_near, ffn_far, grad_unit_two = fence(
        (grad_state.astype(BF16), kept_near, ffn_near, ffn_far, grad_unit_two)
    )
    across, core = swap(state_low, "x"), swap(state_low, "c")
    feed_grads = feed_weights(ids, x_two, g_rows, kept_near, kept_far, parts)
    across, core, feed_grads = fence((across, core, feed_grads))
    g_state = (state_low, core, across, swap(across, "c"))

    def home(total):
        pieces = total.reshape(*total.shape[:-2], SPANS, shard, total.shape[-1])
        return spread([lax.dynamic_index_in_dim(pieces, t ^ r, pieces.ndim - 3, keepdims=False) for r in range(SPANS)])

    def crossed(grads, k):
        if parts == 1:
            return lax.psum_scatter(grads[k], "y", scatter_dimension=1, tiled=True)
        return swap(grads[2 * k + 1], "y")

    def added(grads, k, came):
        return came if parts == 1 else (grads[2 * k].astype(F32) + came.astype(F32)).astype(BF16)

    two_came = crossed(feed_grads, 2)
    grad_att, out_grads = out_back(ids, g_state, att, orel, parts)
    grad_att = exchange(grad_att)
    onward = added(feed_grads, 2, two_came)
    grad_att, onward, feed_grads, out_grads = fence((grad_att, onward, feed_grads, out_grads))
    onward = sent(onward, "z", 1)
    three_came = crossed(feed_grads, 3)
    if parts == 2:
        out_sums = out_grads[0].astype(F32) + swap(out_grads[1], "y").astype(F32)
    else:
        out_sums = lax.psum_scatter(out_grads[0], "y", scatter_dimension=2, tiled=True)
    dq, keep, give = attend_back(ids, q_seq, kv_seq, o_seq, lse, tables, grad_att)
    dq, keep, give, onward, three_came, feed_grads, ffn_near, ffn_far, out_sums = fence(
        (dq, keep, give, onward, three_came, feed_grads, ffn_near, ffn_far, out_sums.astype(BF16))
    )
    one_came = crossed(feed_grads, 1)
    grads_heads = exchange(pack(ids, dq, keep, swap(give, "c")))
    branch_ffn = scatter_halves(ffn_near, ffn_far)
    result = state + branch_ffn
    gain_two = jnp.sum(grad_unit_two * unit_two, axis=0)
    squares = jnp.stack([jnp.sum(result * result), jnp.sum(branch_attn * branch_attn), jnp.sum(branch_ffn * branch_ffn)])
    onward = (added(feed_grads, 3, three_came).astype(F32) + onward.astype(F32)).astype(BF16)
    onward, onward_down = onward[:2], onward[2:]
    one_sum = added(feed_grads, 1, one_came)
    grads_heads, result, squares, gain_two, onward, onward_down, one_sum, feed_grads = fence(
        (grads_heads, result, squares, gain_two, onward, onward_down, one_sum, feed_grads)
    )
    onward = sent(onward, "z", 3)
    feed_one = sent(one_sum, "z", 1)
    grads_qkv, qkv_grads = project_weights(ids, grads_heads, x_one, parts)
    grads_qkv, qkv_grads = fence((grads_qkv, qkv_grads))
    near, far, gain_one = project_tokens(ids, grads_qkv, x_one, attn_weights)
    if parts == 2:
        gone = [(kept, swap(piece, "y")) for kept, piece in zip(qkv_grads[:2], qkv_grads[2:])]
    else:
        gone = [(lax.psum_scatter(piece, "y", scatter_dimension=2, tiled=True),) for piece in qkv_grads]
    own_came = crossed(feed_grads, 0)
    gains = jnp.stack([gain_one[0], gain_two]).reshape(2, sequences, 2, 2, shard)
    sums = settle_attn(ids, gone, out_sums)
    sums, feed_grads, onward, onward_down, feed_one, near, far, own_came, gains = fence(
        (sums, feed_grads, onward, onward_down, feed_one, near, far, own_came, gains)
    )
    onto_three = (sums[3].astype(F32) + sent(sums[2], "z", 1).astype(F32)).astype(BF16)
    onto_one = sent(sums[1], "z", 1)
    onward_down = sent(onward_down, "z", 3)
    total = near.astype(F32) + swap(far, "c").astype(F32)
    gains, squares = halved(gains, squares, "c", 3)
    crossing = swap(total[1].astype(BF16), "x")
    gains, squares = halved(gains, squares, "y", 1)
    feed_total = added(feed_grads, 0, own_came).astype(F32) + jnp.concatenate([onward, onward_down]).astype(F32)
    feed_total = (feed_total + feed_one.astype(F32)).astype(BF16)
    onto_three, onto_one, crossing, feed_total, gains, squares = fence(
        (onto_three, onto_one, crossing, feed_total, gains, squares)
    )
    onto_three = sent(onto_three, "z", 3)
    feed_home = home(feed_total)
    grad_unit_one = total[0] + crossing.astype(F32)
    grad_tokens = (grad_state + unit_back(resid, scale_one, grad_unit_one)).astype(BF16)
    gains, squares = halved(gains, squares, "x", 1)
    onto_three, onto_one, feed_home, gains, squares, grad_tokens = fence(
        (onto_three, onto_one, feed_home, gains, squares, grad_tokens)
    )
    attn_home = spread(part_attn(ids, sums[0], onto_one, onto_three))
    attn_home[1], gains, squares = fence((attn_home[1], gains, squares))
    totals = over_z(jnp.concatenate([gains.reshape(-1), squares]))
    grad_gate, grad_up, grad_down = finish_ffn(ids, feed_home, gain_ffn)
    grad_query, grad_key, grad_value, grad_outproj = finish_attn(ids, attn_home, gain_attn)
    entries = block * width * sequences * SPANS * count
    return (
        result.astype(BF16),
        grad_tokens,
        grad_query,
        grad_key,
        grad_value,
        grad_outproj.T,
        grad_gate,
        grad_up,
        grad_down.T,
        totals[:shard] / gain_attn[:, 0],
        totals[shard : 2 * shard] / gain_ffn[:, 0],
        jnp.sqrt(totals[2 * shard :] / entries),
    )


def solution(mesh):
    fsdp, tensor = mesh.shape["fsdp"], mesh.shape["tensor"]
    split = Mesh(mesh.devices.reshape(fsdp // SPANS, 2, 2, tensor), ("y", "x", "c", "z"))
    rows = ("y", "x", "c")
    tok = P(("y", "x", "c", "z"), None)
    col, row, vec = P(rows, "z"), P("z", rows), P(rows)
    return jax.shard_map(
        per_device,
        mesh=split,
        in_specs=(tok, col, col, col, row, col, col, row, vec, vec, tok),
        out_specs=(tok, tok, col, col, col, row, col, col, row, vec, vec, P()),
        check_vma=False,
    )
```

```python
import functools
import jax
import jax.numpy as jnp
from jax import lax
from jax.experimental import pallas as pl
from jax.experimental.pallas import tpu as pltpu
from jax.sharding import Mesh, PartitionSpec as P

HEAD = 96
LANES = 128
SEQUENCE_LENGTH = 4096
SPANS = 4
EPSILON = 1e-05
ROPE_BASE = 100000.0
MASKED = -1e30
LOG2E = 1.4426950408889634
NT = (((1,), (1,)), ((), ()))
NN = (((1,), (0,)), ((), ()))
TN = (((0,), (0,)), ((), ()))
F32 = jnp.float32
BF16 = jnp.bfloat16


def mm(left, right, dims):
    return lax.dot_general(left, right, dims, preferred_element_type=F32)


def widen(piece):
    return jnp.concatenate([piece, jnp.zeros((piece.shape[0], LANES - HEAD), piece.dtype)], axis=1)


def swapped(value):
    half = HEAD // 2
    return jnp.concatenate([value[:, half:HEAD], value[:, :half]], axis=1)


def rotary(tables, place):
    cos_in, sin_in, cos_out, sin_out = tables
    at = pl.ds(place, 1)
    cosine = cos_out[at, :] * cos_in[...] - sin_out[at, :] * sin_in[...]
    return cosine, sin_out[at, :] * cos_in[...] + cos_out[at, :] * sin_in[...]


def attend_kernel(ids, own, other, out, q_s, kv_s, o_s, lse_s, acc_s, vt_s, *, block, tile):
    z, t = ids[0], ids[1]
    c = lax.rem(t, 2)
    spans = 4
    rows_all = q_s.shape[0]
    for zj in range(4):
        for r in range(spans):
            at = pl.multiple_of(((t ^ r) * spans + zj) * block, block)
            at_other = pl.multiple_of(((t ^ 1 ^ r) * spans + zj) * block, block)
            q_s[pl.ds(at, block), :] = widen(own[zj, :, r * HEAD : (r + 1) * HEAD])
            kv_s[c, pl.ds(at, block), :] = widen(own[zj, :, (spans + r) * HEAD : (spans + r + 1) * HEAD])
            kv_s[1 - c, pl.ds(at_other, block), :] = widen(other[zj, :, r * HEAD : (r + 1) * HEAD])
    factor = HEAD ** (-0.5) * LOG2E
    is_count = lax.broadcasted_iota(jnp.int32, (tile, LANES), 1) == HEAD

    def values(i, _):
        rows = pl.ds(pl.multiple_of(i * tile, tile), tile)
        vals = kv_s[1, rows, :]
        vt_s[:, rows] = jnp.transpose(jnp.where(is_count, jnp.ones_like(vals), vals))
        return 0

    lax.fori_loop(0, rows_all // tile, values, 0)

    def step(query, j, before, mask):
        rows = pl.ds(pl.multiple_of(j * tile, tile), tile)
        scores = mm(kv_s[0, rows, :], query, NT) * factor
        if mask is not None:
            scores = jnp.where(mask, scores, MASKED)
        top = jnp.maximum(before, jnp.max(scores, axis=0, keepdims=True))
        expo = jnp.exp2(scores - top).astype(BF16)
        acc_s[...] = acc_s[...] * jnp.exp2(before - top) + mm(vt_s[:, rows], expo, NN)
        return top

    def row_block(i, _):
        at = pl.multiple_of(i * tile, tile)
        query = q_s[pl.ds(at, tile), :]
        acc_s[...] = jnp.zeros_like(acc_s)
        top = lax.fori_loop(0, i, lambda j, top: step(query, j, top, None), jnp.full((1, tile), MASKED, F32))
        mask = lax.broadcasted_iota(jnp.int32, (tile, tile), 0) <= lax.broadcasted_iota(jnp.int32, (tile, tile), 1)
        top = step(query, i, top, mask)
        acc = acc_s[...]
        denom = acc[HEAD : HEAD + 1, :]
        o_s[pl.ds(at, tile), :] = jnp.transpose(acc / denom).astype(BF16)
        lse_s[:, pl.ds(at, tile)] = jnp.broadcast_to(top + jnp.log2(denom), (8, tile))
        return 0

    lax.fori_loop(0, rows_all // tile, row_block, 0)
    for zj in range(4):
        for r in range(spans):
            at = pl.multiple_of(((t ^ r) * spans + zj) * block, block)
            out[zj, :, r * HEAD : (r + 1) * HEAD] = o_s[pl.ds(at, block), :HEAD]


VM = pl.BlockSpec(memory_space=pltpu.VMEM)
SM = pl.BlockSpec(memory_space=pltpu.SMEM)


def shape(dims, dtype=BF16):
    return jax.ShapeDtypeStruct(dims, dtype)


def params(room):
    return pltpu.CompilerParams(vmem_limit_bytes=room * 1024 * 1024)


def attend(ids, own, other, tile=1024):
    block = own.shape[1]
    rows = block * 16
    return pl.pallas_call(
        functools.partial(attend_kernel, block=block, tile=tile),
        out_shape=[shape((4, block, 4 * HEAD)), shape((rows, LANES)), shape((2, rows, LANES)), shape((rows, LANES)), shape((8, rows), F32)],
        in_specs=[SM] + [VM] * 2,
        out_specs=[VM] * 5,
        scratch_shapes=[pltpu.VMEM((LANES, tile), F32), pltpu.VMEM((LANES, rows), BF16)],
        compiler_params=params(22),
        cost_estimate=pl.CostEstimate(flops=int(21e9), bytes_accessed=1, transcendentals=0),
        name="attend",
    )(ids, own, other)


def attend_back_kernel(ids, q_s, kv_s, o_s, lse_s, cos_in, sin_in, cos_out, sin_out, g, dq_out, keep_out, give_out, g_s, qx_s, kx_s, delta_s, dq_s, dk_s, dv_s, *, block, tile):
    z, t = ids[0], ids[1]
    spans = 4
    rows_all = q_s.shape[0]
    tiles = rows_all // tile
    for zj in range(4):
        for r in range(spans):
            at = pl.multiple_of(((t ^ r) * spans + zj) * block, block)
            g_s[pl.ds(at, block), :] = widen(g[zj, :, r * HEAD : (r + 1) * HEAD])

    def prepare(i, _):
        at = pl.multiple_of(i * tile, tile)
        rows = pl.ds(at, tile)
        query = q_s[rows, :]
        keys = kv_s[0, rows, :]
        qx_s[rows, :LANES] = query
        qx_s[rows, LANES:] = widen(swapped(query))
        kx_s[rows, :LANES] = keys
        kx_s[rows, LANES:] = widen(swapped(keys))
        both = g_s[rows, :].astype(F32) * o_s[rows, :].astype(F32)
        delta = jnp.sum(both, axis=1, keepdims=True)
        delta_s[:, rows] = jnp.transpose(jnp.broadcast_to(delta, (tile, LANES)))[:8]
        dq_s[rows, :] = jnp.zeros((tile, 2 * LANES), F32)
        return 0

    lax.fori_loop(0, tiles, prepare, 0)
    factor = HEAD ** (-0.5) * LOG2E
    scale = HEAD ** (-0.5)

    def step(i, keys, vals, kx, mask):
        rows = pl.ds(pl.multiple_of(i * tile, tile), tile)
        query = qx_s[rows, :]
        grad = g_s[rows, :]
        scores = mm(keys, query[:, :LANES], NT) * factor - lse_s[:1, rows]
        if mask is not None:
            scores = jnp.where(mask, scores, MASKED)
        prob = jnp.exp2(scores)
        through = mm(vals, grad, NT)
        ds = (prob * (through - delta_s[:1, rows])).astype(BF16)
        dv_s[...] += mm(prob.astype(BF16), grad, NN)
        dk_s[...] += mm(ds, query, NN)
        dq_s[rows, :] += mm(ds, kx, TN)

    def column_block(j, _):
        rows = pl.ds(pl.multiple_of(j * tile, tile), tile)
        kx = kx_s[rows, :]
        keys = kx[:, :LANES]
        vals = kv_s[1, rows, :]
        dk_s[...] = jnp.zeros_like(dk_s)
        dv_s[...] = jnp.zeros_like(dv_s)
        mask = lax.broadcasted_iota(jnp.int32, (tile, tile), 0) <= lax.broadcasted_iota(jnp.int32, (tile, tile), 1)
        step(j, keys, vals, kx, mask)
        lax.fori_loop(j + 1, tiles, lambda i, _: (step(i, keys, vals, kx, None), 0)[1], 0)
        dk = dk_s[...] * scale
        turns = [rotary((cos_in, sin_in, cos_out, sin_out), j * (tile // block) + b) for b in range(tile // block)]
        cosine, sine = (jnp.concatenate(parts, axis=0) for parts in zip(*turns))
        dk = dk[:, :LANES] * cosine - dk[:, LANES:] * sine
        dv = dv_s[...]
        first = lax.rem(t, 2) == 0
        keep_out[rows, :] = jnp.where(first, dk, dv).astype(BF16)
        give_out[rows, :] = jnp.where(first, dv, dk).astype(BF16)
        return 0

    lax.fori_loop(0, tiles, column_block, 0)
    for zj in range(4):
        for r in range(spans):
            rows = pl.ds(pl.multiple_of(((t ^ r) * spans + zj) * block, block), block)
            cosine, sine = rotary((cos_in, sin_in, cos_out, sin_out), (t ^ r) * spans + zj)
            dq = dq_s[rows, :] * scale
            dq_out[zj, :, r * HEAD : (r + 1) * HEAD] = (
                dq[:, :LANES] * cosine - dq[:, LANES:] * sine
            ).astype(BF16)[:, :HEAD]


def attend_back(ids, q, kv, o, lse, tables, grads, tile=1024):
    block = grads.shape[1]
    rows = block * 16
    return pl.pallas_call(
        functools.partial(attend_back_kernel, block=block, tile=tile),
        out_shape=[shape((4, block, 4 * HEAD))] + [shape((rows, LANES))] * 2,
        in_specs=[SM] + [VM] * 9,
        out_specs=[VM] * 3,
        scratch_shapes=[
            pltpu.VMEM((rows, LANES), BF16),
            pltpu.VMEM((rows, 2 * LANES), BF16),
            pltpu.VMEM((rows, 2 * LANES), BF16),
            pltpu.VMEM((8, rows), F32),
            pltpu.VMEM((rows, 2 * LANES), F32),
            pltpu.VMEM((tile, 2 * LANES), F32),
            pltpu.VMEM((tile, LANES), F32),
        ],
        compiler_params=params(36),
        cost_estimate=pl.CostEstimate(flops=int(39e9), bytes_accessed=1, transcendentals=0),
        name="attend_back",
    )(ids, q, kv, o, lse, *tables, grads)


def offsets(ids, count, part):
    if count == 1:
        return [0]
    return [pl.multiple_of(ids[2] * part, LANES), pl.multiple_of((1 - ids[2]) * part, LANES)]


def call(kernel, outs, name, scratch=(), micros=0, room=14):
    def run(ids, *args):
        return pl.pallas_call(
            kernel,
            out_shape=[shape(*o) if isinstance(o[0], tuple) else shape(o) for o in outs],
            in_specs=[SM] + [VM] * len(args),
            out_specs=[VM] * len(outs),
            scratch_shapes=[pltpu.VMEM(*item) for item in scratch],
            compiler_params=params(room),
            cost_estimate=pl.CostEstimate(flops=int(micros * 1e9) + 1, bytes_accessed=1, transcendentals=0),
            name=name,
        )(ids, *args)

    return run


def split(refs, *counts):
    refs = list(refs)
    groups = []
    for count in counts:
        groups.append(refs[:count])
        refs = refs[count:]
    return groups


def prepare_attn(ids, w_query, w_key, w_value, w_out, gain):
    shard = w_query.shape[0]

    def kernel(ids, query, key, value, out, gain, *refs):
        pieces, made = split(refs, SPANS, 1)
        made = made[0]
        scale = gain[...]

        def turned(ref, at):
            return jnp.transpose(ref[:, at * HEAD : (at + 1) * HEAD].astype(F32) * scale).astype(BF16)

        for place in range(SPANS):
            made[place, :HEAD] = turned(query, place)
            made[place, HEAD : 2 * HEAD] = turned(value if place % 2 else key, place // 2)
            made[place, 2 * HEAD :] = jnp.transpose(out[:, place * HEAD : (place + 1) * HEAD].astype(F32)).astype(BF16)
        for r in range(SPANS):
            pieces[r][...] = made[ids[1] ^ r]

    scratch = [((SPANS, 3 * HEAD, shard), BF16)]
    return call(kernel, [(3 * HEAD, shard)] * SPANS, "prepare_attn", scratch)(
        ids, w_query, w_key, w_value, w_out.T, gain
    )


def prepare_ffn(ids, w_gate, w_up, w_down, gain):
    shard = w_gate.shape[0]
    units = w_gate.shape[1] // SPANS

    def kernel(ids, gate, up, down, gain, *pieces):
        scale = gain[...]
        for r in range(SPANS):
            at = pl.multiple_of((ids[1] ^ r) * units, LANES)
            pieces[r][0] = (gate[:, pl.ds(at, units)].astype(F32) * scale).astype(BF16)
            pieces[r][1] = (up[:, pl.ds(at, units)].astype(F32) * scale).astype(BF16)
            pieces[r][2] = down[:, pl.ds(at, units)]

    return call(kernel, [(3, shard, units)] * SPANS, "prepare_ffn")(ids, w_gate, w_up, w_down.T, gain)


def join_attn(ids, pieces):
    rows, shard = pieces[0].shape

    def kernel(ids, *refs):
        pieces, (out,), (made,) = split(refs, SPANS, 1, 1)
        for r, piece in enumerate(pieces):
            made[ids[1] ^ r] = piece[...]
        for place in range(SPANS):
            out[:, place * shard : (place + 1) * shard] = made[place]

    return call(kernel, [(rows, SPANS * shard)], "join_attn", [((SPANS, rows, shard), BF16)])(ids, *pieces)[0]


def join_ffn(ids, pieces):
    _, shard, units = pieces[0].shape

    def kernel(ids, *refs):
        pieces, (out,) = split(refs, SPANS, 1)
        for r, piece in enumerate(pieces):
            out[:, pl.ds(pl.multiple_of((ids[1] ^ r) * shard, 16), shard), :] = piece[...]

    return call(kernel, [(3, SPANS * shard, units)], "join_ffn")(ids, *pieces)[0]


def part_attn(ids, own, one, three):
    rows, part = own.shape
    shard = part // SPANS

    def kernel(ids, own, one, three, *refs):
        pieces, (made,) = split(refs, SPANS, 1)
        total = (own[...].astype(F32) + one[...].astype(F32) + three[...].astype(F32)).astype(BF16)
        for place in range(SPANS):
            made[place] = total[:, place * shard : (place + 1) * shard]
        for r, piece in enumerate(pieces):
            piece[...] = made[ids[1] ^ r]

    return call(kernel, [(rows, shard)] * SPANS, "part_attn", [((SPANS, rows, shard), BF16)])(ids, own, one, three)


def distinct(items):
    arrays = list({id(item[0]): item[0] for item in items}.values())
    index = {id(array): i for i, array in enumerate(arrays)}

    def rows_of(refs, item, rows):
        return refs[index[id(item[0])]][(*item[1], rows)]

    return arrays, rows_of


def project(ids, x, weights, tables):
    block = x[0].shape[0]
    parts = len(weights[0])
    part = weights[0][0][0].shape[-1]
    arrays, rows_of = distinct([item for items in weights for item in items])
    first = slice(0, 2 * HEAD)

    def kernel(ids, *refs):
        xs, ws, tables, (out,) = split(refs, SPANS, len(arrays), 4, 1)
        z, t = ids[0], ids[1]
        at = offsets(ids, parts, part)
        is_value = lax.rem(t, 2) == 1
        for r, x in enumerate(xs):
            cosine, sine = rotary(tables, (t ^ r) * SPANS + z)
            cosine, sine = cosine[:, :HEAD], sine[:, :HEAD]
            cos_kv = jnp.where(is_value, 1.0, cosine)
            sin_kv = jnp.where(is_value, 0.0, sine)
            for k in range(4):
                made = sum(mm(x[:, pl.ds(at[p], part)], rows_of(ws, weights[k][p], first), NT) for p in range(parts))
                query, other = made[:, :HEAD], made[:, HEAD:]
                out[z ^ k, :, r * HEAD : (r + 1) * HEAD] = (query * cosine + swapped(query) * sine).astype(BF16)
                out[z ^ k, :, (SPANS + r) * HEAD : (SPANS + r + 1) * HEAD] = (
                    other * cos_kv + swapped(other) * sin_kv
                ).astype(BF16)

    return call(kernel, [(4, block, 8 * HEAD)], "project")(ids, *x, *arrays, *tables)[0]


def out_weights(ids, weights):
    parts = len(weights[0])
    part = weights[0][0][0].shape[-1]
    arrays, rows_of = distinct([item for items in weights for item in items])

    def kernel(ids, *refs):
        ws, (orel,) = split(refs, len(arrays), 1)
        at = offsets(ids, parts, part)
        for j in range(4):
            for p in range(parts):
                orel[j * HEAD : (j + 1) * HEAD, pl.ds(at[p], part)] = rows_of(ws, weights[j][p], slice(2 * HEAD, 3 * HEAD))

    return call(kernel, [(4 * HEAD, parts * part)], "out_weights")(ids, *arrays)[0]


def out_project(ids, pieces, orel):
    block, width = pieces.shape[1], orel.shape[1]

    def kernel(ids, pieces, orel, near, far, att):
        for j in range(4):
            for r in range(SPANS):
                att[r * block : (r + 1) * block, j * HEAD : (j + 1) * HEAD] = pieces[ids[0] ^ j, :, r * HEAD : (r + 1) * HEAD]
        for r in (1, 3, 2, 0):
            made = mm(att[r * block : (r + 1) * block, :], orel[...], NN).astype(BF16)
            (far if r % 2 else near)[r // 2] = made

    outs = [(2, block, width)] * 2 + [(4 * block, 4 * HEAD)]
    return call(kernel, outs, "out_project")(ids, pieces, orel)


def out_back(ids, grads, att, orel, parts):
    block, width = grads[0].shape
    part = width // parts

    def kernel(ids, *refs):
        gs, (att, orel), (ds,), douts, (g_s,) = split(refs, SPANS, 2, 1, parts, 1)
        at = offsets(ids, parts, part)
        for r, grad in enumerate(gs):
            g_s[r * block : (r + 1) * block, :] = grad[...]
        made = mm(g_s[...], orel[...], NT).astype(BF16)
        for r in range(SPANS):
            for j in range(4):
                ds[ids[0] ^ j, :, r * HEAD : (r + 1) * HEAD] = made[r * block : (r + 1) * block, j * HEAD : (j + 1) * HEAD]
        for p in range(parts):
            total = mm(att[...], g_s[:, pl.ds(at[p], part)], TN)
            for k in range(4):
                douts[p][k] = total[k * HEAD : (k + 1) * HEAD].astype(BF16)

    outs = [(4, block, 4 * HEAD)] + [(4, HEAD, part)] * parts
    made = call(kernel, outs, "out_back", [((4 * block, width), BF16)])(ids, *grads, att, orel)
    return made[0], made[1:]


def pack(ids, queries, mine, theirs):
    _, block, wide = queries.shape

    def kernel(ids, queries, mine, theirs, out):
        t = ids[1]
        for zj in range(4):
            out[zj, :, :wide] = queries[zj]
            for r in range(SPANS):
                rows = pl.ds(pl.multiple_of(((t ^ r) * SPANS + zj) * block, block), block)
                total = (mine[rows, :].astype(F32) + theirs[rows, :].astype(F32)).astype(BF16)
                out[zj, :, wide + r * HEAD : wide + (r + 1) * HEAD] = total[:, :HEAD]

    return call(kernel, [(4, block, 2 * wide)], "pack")(ids, queries, mine, theirs)[0]


def project_weights(ids, grads, x, parts):
    block, width = x[0].shape
    part = width // parts

    def kernel(ids, *refs):
        (grads,), xs, (d_out,), das, (x_s,) = split(refs, 1, SPANS, 1, 2 * parts, 1)
        at = offsets(ids, parts, part)
        for j in range(4):
            for r in range(SPANS):
                for half in range(2):
                    lanes = slice((half * SPANS + r) * HEAD, (half * SPANS + r + 1) * HEAD)
                    d_out[r * block : (r + 1) * block, (2 * j + half) * HEAD : (2 * j + half + 1) * HEAD] = grads[
                        ids[0] ^ j, :, lanes
                    ]
        for r, x in enumerate(xs):
            x_s[r * block : (r + 1) * block, :] = x[...]
        for p in reversed(range(parts)):
            total = mm(d_out[...], x_s[:, pl.ds(at[p], part)], TN)
            for k in range(4):
                das[2 * p + (k < 2)][k % 2] = total[2 * k * HEAD : (2 * k + 2) * HEAD].astype(BF16)

    outs = [(4 * block, 8 * HEAD)] + [(2, 2 * HEAD, part)] * (2 * parts)
    made = call(kernel, outs, "project_weights", [((4 * block, width), BF16)], 100)(ids, grads, *x)
    return made[0], made[1:]


def project_tokens(ids, grads, x, weights):
    rows = grads.shape[0]
    block = rows // SPANS
    parts = len(weights[0])
    part = weights[0][0][0].shape[-1]
    width = parts * part
    arrays, rows_of = distinct([item for items in weights for item in items])

    def kernel(ids, *refs):
        (d_s,), xs, ws, (near, far, sums), (a_s,) = split(refs, 1, SPANS, len(arrays), 3, 1)
        at = offsets(ids, parts, part)
        for j in range(4):
            for p in range(parts):
                a_s[2 * j * HEAD : (2 * j + 2) * HEAD, pl.ds(at[p], part)] = rows_of(ws, weights[j][p], slice(0, 2 * HEAD))
        total = None
        for r in (1, 3, 2, 0):
            made = mm(d_s[r * block : (r + 1) * block, :], a_s[...], NN)
            term = jnp.sum(made * xs[r][...].astype(F32), axis=0, keepdims=True)
            total = term if total is None else total + term
            (far if r % 2 else near)[r // 2] = made.astype(BF16)
        sums[...] = jnp.broadcast_to(total, (8, width))

    outs = [((2, block, width), BF16)] * 2 + [((8, width), F32)]
    return call(kernel, outs, "project_tokens", [((8 * HEAD, width), BF16)], 100)(ids, grads, *x, *arrays)


def settle_attn(ids, grads, out_sums):
    flat = [array for pair in grads for array in pair]
    each = len(grads[0])
    _, high, part = flat[0].shape
    low = out_sums.shape[1]

    def kernel(ids, *refs):
        late, early, (out_s,), outs = split(refs, each, each, 1, 4)
        for k, out in enumerate(outs):
            pair = early if k < 2 else late
            total = pair[0][k % 2]
            if each == 2:
                total = (total.astype(F32) + pair[1][k % 2].astype(F32)).astype(BF16)
            out[:high, :] = total
            out[high:, :] = out_s[k]

    return call(kernel, [(high + low, part)] * 4, "settle_attn")(ids, *flat, out_sums)


def feed(ids, x, grads, weights):
    block, width = x[0].shape
    part, units = weights[0][0].shape[-2:]
    parts = width // part
    rows, every = 2 * block, 4 * units
    arrays = list({id(item[0]): item[0] for item in weights}.values())
    index = {id(array): i for i, array in enumerate(arrays)}

    def kernel(ids, *refs):
        xs, gs, ws, ffn, two, (hid, dgate, dup), (x_s, g_s, w_s) = split(refs, 2, 2, len(arrays), 2, 2, 3, 3)
        at = [pl.multiple_of(place, LANES) for place in offsets(ids, parts, part)]
        for r in range(2):
            x_s[r * block : (r + 1) * block, :] = xs[r][...]
            g_s[r * block : (r + 1) * block, :] = gs[r][...]
        for array, where, m, k, p in weights:
            w_s[m, pl.ds(at[p], part), k * units : (k + 1) * units] = ws[index[id(array)]][where]

        def eighth(i, _):
            lanes = pl.ds(pl.multiple_of(i // 2 * units, LANES), units)
            at = pl.ds(pl.multiple_of(lax.rem(i, 2) * block, block), block)
            gate = mm(x_s[at, :], w_s[0, :, lanes], NN)
            up = mm(x_s[at, :], w_s[1, :, lanes], NN)
            back = mm(g_s[at, :], w_s[2, :, lanes], NN)
            sigma = 0.5 * jnp.tanh(0.5 * gate) + 0.5
            swish = gate * sigma
            hid[at, lanes] = (swish * up).astype(BF16)
            dup[at, lanes] = (back * swish).astype(BF16)
            dgate[at, lanes] = (back * up * (sigma + swish * (1.0 - sigma))).astype(BF16)
            return 0

        lax.fori_loop(0, 8, eighth, 0)
        cut = width // 3

        def third(p, _):
            lanes = pl.ds(pl.multiple_of(p * cut, LANES), cut)
            made = mm(dgate[...], w_s[0, lanes, :], NT) + mm(dup[...], w_s[1, lanes, :], NT)
            for r in range(2):
                two[r][:, lanes] = made[r * block : (r + 1) * block].astype(BF16)
            made = mm(hid[...], w_s[2, lanes, :], NT)
            for r in range(2):
                ffn[r][:, lanes] = made[r * block : (r + 1) * block].astype(BF16)
            return 0

        lax.fori_loop(0, 3, third, 0)

    outs = [(block, width)] * 4 + [(rows, every)] * 3
    scratch = [((rows, width), BF16), ((rows, width), BF16), ((3, width, every), BF16)]
    made = call(kernel, outs, "feed", scratch, 18, 34)(ids, *x, *grads, *arrays)
    return made[:2], made[2:4], made[4:]


def feed_weights(ids, x, grads, near, far, parts):
    block, width = x[0].shape
    part = width // parts
    half, every = near[0].shape
    units = every // 4

    def kernel(ids, *refs):
        xs, gs, ns, fs, outs, (rows_s, h_s) = split(refs, SPANS, SPANS, 3, 3, 4 * parts, 2)
        at = offsets(ids, parts, part)
        for r in range(SPANS):
            rows_s[0, r * block : (r + 1) * block, :] = xs[r][...]
            rows_s[1, r * block : (r + 1) * block, :] = gs[r][...]
        for m in range(3):
            h_s[m, :half] = ns[m][...]
            h_s[m, half:] = fs[m][...]

        def one(m, _):
            side = lax.rem(m + 1, 3)
            left = m // 2
            for p in reversed(range(parts)):
                total = mm(rows_s[left, :, pl.ds(at[p], part)], h_s[side], TN)
                for k in range(4):
                    outs[k * parts + p][m] = total[:, k * units : (k + 1) * units].astype(BF16)
            return 0

        lax.fori_loop(0, 3, one, 0)

    outs = [(3, part, units)] * (4 * parts)
    scratch = [((2, 4 * block, width), BF16), ((3, 4 * block, every), BF16)]
    return call(kernel, outs, "feed_weights", scratch, 17, 40)(ids, *x, *grads, *near, *far)


def finish_ffn(ids, pieces, gain):
    _, shard, units = pieces[0].shape
    every = SPANS * units

    def kernel(ids, *refs):
        pieces, (gain,), (gate, up, down) = split(refs, SPANS, 1, 3)
        scale = gain[...]
        for r, piece in enumerate(pieces):
            lanes = pl.ds(pl.multiple_of((ids[1] ^ r) * units, LANES), units)
            gate[:, lanes] = piece[0].astype(F32) * scale
            up[:, lanes] = piece[1].astype(F32) * scale
            down[:, lanes] = piece[2].astype(F32)

    return call(kernel, [((shard, every), F32)] * 3, "finish_ffn")(ids, *pieces, gain)


def finish_attn(ids, pieces, gain):
    shard = pieces[0].shape[1]

    def kernel(ids, *refs):
        pieces, (gain,), (query, key, value, out_w), (made,) = split(refs, SPANS, 1, 4, 1)
        scale = gain[...]
        for r, piece in enumerate(pieces):
            made[ids[1] ^ r] = piece[...].astype(F32)
        for place in range(SPANS):
            lanes = slice(place * HEAD, (place + 1) * HEAD)
            half = slice(place // 2 * HEAD, (place // 2 + 1) * HEAD)
            out_w[:, lanes] = jnp.transpose(made[place, 2 * HEAD :])
            query[:, lanes] = jnp.transpose(made[place, :HEAD]) * scale
            (value if place % 2 else key)[:, half] = jnp.transpose(made[place, HEAD : 2 * HEAD]) * scale

    outs = [((shard, wide * HEAD), F32) for wide in (4, 2, 2, 4)]
    scratch = [((SPANS, 3 * HEAD, shard), F32)]
    return call(kernel, outs, "finish_attn", scratch)(ids, *pieces, gain)


def swap(value, axis):
    return lax.ppermute(value, axis, [(0, 1), (1, 0)])


def sent(value, axis, bits):
    return lax.ppermute(value, axis, [(i, i ^ bits) for i in range(lax.axis_size(axis))])


def gather_group(value):
    core = swap(value, "c")
    across = swap(value, "x")
    return value, core, across, swap(across, "c")


def scatter_group(near, far):
    total = near.astype(F32) + swap(far, "c").astype(F32)
    return total[0] + swap(total[1].astype(BF16), "x").astype(F32)


def scatter_halves(near, far):
    far_total = far[0].astype(F32) + swap(far[1], "c").astype(F32)
    crossing = swap(far_total.astype(BF16), "x")
    return near[0].astype(F32) + swap(near[1], "c").astype(F32) + crossing.astype(F32)


def exchange(pieces):
    return lax.all_to_all(pieces, "z", split_axis=0, concat_axis=0, tiled=True)


def spread(pieces):
    return [
        pieces[0],
        swap(pieces[1], "c"),
        swap(pieces[2], "x"),
        lax.ppermute(pieces[3], ("x", "c"), [(i, 3 - i) for i in range(SPANS)]),
    ]


def beside(mine, dim):
    if lax.axis_size("y") == 2:
        return [mine, swap(mine, "y")]
    return [lax.all_gather(mine, "y", axis=dim, tiled=True)]


def along_z(mine):
    if lax.axis_size("z") != 4:
        return [mine] + [sent(mine, "z", k) for k in range(1, lax.axis_size("z"))]
    far = sent(mine, "z", 3)
    return [mine, sent(mine, "z", 1), sent(far, "z", 1), far]


def onto_z(pieces):
    far = pieces[3].astype(F32) + sent(pieces[2], "z", 1).astype(F32)
    near = pieces[0].astype(F32) + sent(pieces[1], "z", 1).astype(F32)
    return (near + sent(far.astype(BF16), "z", 3).astype(F32)).astype(BF16)


def settled(pieces, parts, dim):
    if parts == 2:
        sums = [
            (pieces[2 * k].astype(F32) + swap(pieces[2 * k + 1], "y").astype(F32)).astype(BF16) for k in range(4)
        ]
    else:
        sums = [lax.psum_scatter(piece, "y", scatter_dimension=dim, tiled=True) for piece in pieces]
    return onto_z(sums)


def halved(values, rest, axis, dim):
    if lax.axis_size(axis) != 2:
        values, rest = lax.psum((values, rest), axis)
        return lax.dynamic_index_in_dim(values, lax.axis_index(axis), dim, keepdims=False), rest
    here = lax.axis_index(axis)
    kept = lax.dynamic_index_in_dim(values, here, dim, keepdims=False)
    gone = lax.dynamic_index_in_dim(values, 1 - here, dim, keepdims=False)
    came = swap(jnp.concatenate([gone.reshape(-1), rest]), axis)
    return kept + came[: kept.size].reshape(kept.shape), rest + came[kept.size :]


def over_z(value):
    return value + sum(sent(value, "z", k) for k in range(1, lax.axis_size("z")))


def unit(values):
    scale = lax.rsqrt(jnp.mean(values * values, axis=-1, keepdims=True) + EPSILON)
    return values * scale, scale


def unit_back(values, scale, grad):
    inner = jnp.mean(grad * values, axis=-1, keepdims=True)
    return scale * grad - values * (scale * scale * scale) * inner


def per_device(tokens, w_query, w_key, w_value, w_out, w_gate, w_up, w_down, norm_attn, norm_ffn, grad_out):
    sequences, count = lax.axis_size("y"), lax.axis_size("z")
    parts = 2 if sequences == 2 else 1
    block, width = tokens.shape
    shard = w_query.shape[0]
    t = lax.axis_index("x") * 2 + lax.axis_index("c")
    ids = jnp.stack([lax.axis_index("z"), t, lax.axis_index("y")]).astype(jnp.int32)
    gain_attn = norm_attn.astype(F32)[:, None]
    gain_ffn = norm_ffn.astype(F32)[:, None]

    fence = lax.optimization_barrier

    resid = tokens.astype(F32)
    unit_one, scale_one = unit(resid)
    attn_pieces, low_one = fence((prepare_attn(ids, w_query, w_key, w_value, w_out, gain_attn), unit_one.astype(BF16)))
    attn_mine = join_attn(ids, spread(attn_pieces))
    lane = jnp.arange(LANES)
    freq = ROPE_BASE ** (-(lane % (HEAD // 2) * 2.0) / HEAD)
    inner = jnp.arange(block, dtype=F32)[:, None] * freq
    outer = (jnp.arange(SEQUENCE_LENGTH // block, dtype=F32) * block)[:, None] * freq
    sign = jnp.where(lane < HEAD // 2, -1.0, 1.0)
    tables = (jnp.cos(inner), jnp.sin(inner) * sign, jnp.cos(outer), jnp.sin(outer) * sign)
    attn_mine, ffn_pieces, tables, low_one = fence(
        (attn_mine, prepare_ffn(ids, w_gate, w_up, w_down, gain_ffn), tables, low_one)
    )

    attn_three, attn_one = sent(attn_mine, "z", 3), sent(attn_mine, "z", 1)
    own = beside(attn_mine, 1)
    ffn_mine = join_ffn(ids, spread(ffn_pieces))
    core, across = swap(low_one, "c"), swap(low_one, "x")
    ffn_mine, attn_three, attn_one, own = fence((ffn_mine, attn_three, attn_one, own))
    attn_two = sent(attn_three, "z", 1)
    three_one = beside(jnp.stack([attn_three, attn_one]), 2)
    gate_three = sent(ffn_mine[0], "z", 3)
    attn_two, three_one, gate_three, ffn_mine, core, across = fence(
        (attn_two, three_one, gate_three, ffn_mine, core, across)
    )
    x_one = (low_one, core, across, swap(across, "c"))
    two = beside(attn_two, 1)
    attn_weights = [
        [(array, ()) for array in own],
        [(array, (1,)) for array in three_one],
        [(array, ()) for array in two],
        [(array, (0,)) for array in three_one],
    ]
    gate_one, up_three = sent(ffn_mine[0], "z", 1), sent(ffn_mine[1], "z", 3)
    made = project(ids, x_one, attn_weights, tables)
    made, gate_one, up_three, gate_three, ffn_mine, grad_in = fence(
        (made, gate_one, up_three, gate_three, ffn_mine, grad_out)
    )

    made = exchange(made)
    ffn_own = beside(ffn_mine, 1)
    g_rows = gather_group(grad_in)
    by_one = jnp.stack([ffn_mine[1], gate_three])
    first = jnp.stack([gate_three, gate_one, up_three])
    made, ffn_own, g_rows, by_one, first, down_mine, orel = fence(
        (made, ffn_own, g_rows, by_one, first, ffn_mine[2], out_weights(ids, attn_weights))
    )
    by_one, down_three = sent(by_one, "z", 1), sent(down_mine, "z", 3)
    first = beside(first, 1)
    other = swap(made[:, :, SPANS * HEAD :], "c")
    attended, q_seq, kv_seq, o_seq, lse = attend(ids, made, other)
    attended, down_three, by_one, first, up_three, down_mine = fence(
        (attended, down_three, by_one, first, up_three, down_mine)
    )
    attended = exchange(attended)
    by_one = beside(by_one, 1)
    down_one = sent(down_mine, "z", 1)
    both_two = jnp.stack([up_three, down_three])
    attended, by_one, down_one, down_three, both_two = fence((attended, by_one, down_one, down_three, both_two))
    both_two = sent(both_two, "z", 1)
    down_three, down_one = beside(down_three, 0), beside(down_one, 0)
    near, far, att = out_project(ids, attended, orel)
    branch_attn = scatter_group(near, far)
    state = resid + branch_attn
    unit_two, scale_two = unit(state)
    low_two, both_two, down_three, down_one = fence((unit_two.astype(BF16), both_two, down_three, down_one))
    x_two = gather_group(low_two)
    both_two = beside(both_two, 1)
    x_two, both_two = fence((x_two, both_two))

    ffn_weights = []
    for p in range(parts):
        ffn_weights += [(ffn_own[p], (m,), m, 0, p) for m in range(3)]
        ffn_weights += [(first[p], (i,), *place, p) for i, place in enumerate(((0, 3), (0, 1), (1, 3)))]
        ffn_weights += [(by_one[p], (i,), *place, p) for i, place in enumerate(((1, 1), (0, 2)))]
        ffn_weights += [(down_three[p], (Ellipsis,), 2, 3, p), (down_one[p], (Ellipsis,), 2, 1, p)]
        ffn_weights += [(both_two[p], (0,), 1, 2, p), (both_two[p], (1,), 2, 2, p)]
    ffn_far, two_far, kept_far = feed(ids, x_two[2:], g_rows[2:], ffn_weights)
    crossing = (two_far[0].astype(F32) + swap(two_far[1], "c").astype(F32)).astype(BF16)
    crossing, x_near = fence((crossing, x_two[:2]))
    crossing = swap(crossing, "x")
    ffn_near, two_near, kept_near = feed(ids, x_near, g_rows[:2], ffn_weights)
    two_near, crossing = fence((two_near, crossing))
    grad_unit_two = two_near[0].astype(F32) + swap(two_near[1], "c").astype(F32) + crossing.astype(F32)
    grad_state = grad_out.astype(F32) + unit_back(state, scale_two, grad_unit_two)
    state_low, kept_near, ffn_near, ffn_far, grad_unit_two = fence(
        (grad_state.astype(BF16), kept_near, ffn_near, ffn_far, grad_unit_two)
    )
    across, core = swap(state_low, "x"), swap(state_low, "c")
    feed_grads = feed_weights(ids, x_two, g_rows, kept_near, kept_far, parts)
    across, core, feed_grads = fence((across, core, feed_grads))
    g_state = (state_low, core, across, swap(across, "c"))

    def home(total):
        pieces = total.reshape(*total.shape[:-2], SPANS, shard, total.shape[-1])
        return spread([lax.dynamic_index_in_dim(pieces, t ^ r, pieces.ndim - 3, keepdims=False) for r in range(SPANS)])

    def crossed(grads, k):
        if parts == 1:
            return lax.psum_scatter(grads[k], "y", scatter_dimension=1, tiled=True)
        return swap(grads[2 * k + 1], "y")

    def added(grads, k, came):
        return came if parts == 1 else (grads[2 * k].astype(F32) + came.astype(F32)).astype(BF16)

    two_came = crossed(feed_grads, 2)
    grad_att, out_grads = out_back(ids, g_state, att, orel, parts)
    grad_att = exchange(grad_att)
    onward = added(feed_grads, 2, two_came)
    grad_att, onward, feed_grads, out_grads = fence((grad_att, onward, feed_grads, out_grads))
    onward = sent(onward, "z", 1)
    three_came = crossed(feed_grads, 3)
    if parts == 2:
        out_sums = out_grads[0].astype(F32) + swap(out_grads[1], "y").astype(F32)
    else:
        out_sums = lax.psum_scatter(out_grads[0], "y", scatter_dimension=2, tiled=True)
    dq, keep, give = attend_back(ids, q_seq, kv_seq, o_seq, lse, tables, grad_att)
    dq, keep, give, onward, three_came, feed_grads, ffn_near, ffn_far, out_sums = fence(
        (dq, keep, give, onward, three_came, feed_grads, ffn_near, ffn_far, out_sums.astype(BF16))
    )
    one_came = crossed(feed_grads, 1)
    grads_heads = exchange(pack(ids, dq, keep, swap(give, "c")))
    branch_ffn = scatter_halves(ffn_near, ffn_far)
    result = state + branch_ffn
    gain_two = jnp.sum(grad_unit_two * unit_two, axis=0)
    squares = jnp.stack([jnp.sum(result * result), jnp.sum(branch_attn * branch_attn), jnp.sum(branch_ffn * branch_ffn)])
    onward = (added(feed_grads, 3, three_came).astype(F32) + onward.astype(F32)).astype(BF16)
    onward, onward_down = onward[:2], onward[2:]
    one_sum = added(feed_grads, 1, one_came)
    grads_heads, result, squares, gain_two, onward, onward_down, one_sum, feed_grads = fence(
        (grads_heads, result, squares, gain_two, onward, onward_down, one_sum, feed_grads)
    )
    onward = sent(onward, "z", 3)
    feed_one = sent(one_sum, "z", 1)
    grads_qkv, qkv_grads = project_weights(ids, grads_heads, x_one, parts)
    grads_qkv, qkv_grads = fence((grads_qkv, qkv_grads))
    near, far, gain_one = project_tokens(ids, grads_qkv, x_one, attn_weights)
    if parts == 2:
        gone = [(kept, swap(piece, "y")) for kept, piece in zip(qkv_grads[:2], qkv_grads[2:])]
    else:
        gone = [(lax.psum_scatter(piece, "y", scatter_dimension=2, tiled=True),) for piece in qkv_grads]
    own_came = swap(feed_grads[1][:2], "y") if parts == 2 else crossed(feed_grads, 0)
    gains = jnp.stack([gain_one[0], gain_two]).reshape(2, sequences, 2, 2, shard)
    sums = settle_attn(ids, gone, out_sums)
    own_gone = feed_grads[1][2:]
    sums, feed_grads, onward, onward_down, feed_one, near, far, own_came, own_gone, gains = fence(
        (sums, feed_grads, onward, onward_down, feed_one, near, far, own_came, own_gone, gains)
    )
    onto_three = (sums[3].astype(F32) + sent(sums[2], "z", 1).astype(F32)).astype(BF16)
    own_came = jnp.concatenate([own_came, swap(own_gone, "y")]) if parts == 2 else own_came
    onto_one = sent(sums[1], "z", 1)
    onward_down = sent(onward_down, "z", 3)
    total = near.astype(F32) + swap(far, "c").astype(F32)
    gains, squares = halved(gains, squares, "c", 3)
    crossing = swap(total[1].astype(BF16), "x")
    gains, squares = halved(gains, squares, "y", 1)
    feed_total = added(feed_grads, 0, own_came).astype(F32) + jnp.concatenate([onward, onward_down]).astype(F32)
    feed_total = (feed_total + feed_one.astype(F32)).astype(BF16)
    onto_three, onto_one, crossing, feed_total, gains, squares = fence(
        (onto_three, onto_one, crossing, feed_total, gains, squares)
    )
    onto_three = sent(onto_three, "z", 3)
    feed_home = home(feed_total)
    grad_unit_one = total[0] + crossing.astype(F32)
    grad_tokens = (grad_state + unit_back(resid, scale_one, grad_unit_one)).astype(BF16)
    gains, squares = halved(gains, squares, "x", 1)
    onto_three, onto_one, feed_home, gains, squares, grad_tokens = fence(
        (onto_three, onto_one, feed_home, gains, squares, grad_tokens)
    )
    attn_home = spread(part_attn(ids, sums[0], onto_one, onto_three))
    attn_home[1], gains, squares = fence((attn_home[1], gains, squares))
    totals = over_z(jnp.concatenate([gains.reshape(-1), squares]))
    grad_gate, grad_up, grad_down = finish_ffn(ids, feed_home, gain_ffn)
    grad_query, grad_key, grad_value, grad_outproj = finish_attn(ids, attn_home, gain_attn)
    entries = block * width * sequences * SPANS * count
    return (
        result.astype(BF16),
        grad_tokens,
        grad_query,
        grad_key,
        grad_value,
        grad_outproj.T,
        grad_gate,
        grad_up,
        grad_down.T,
        totals[:shard] / gain_attn[:, 0],
        totals[shard : 2 * shard] / gain_ffn[:, 0],
        jnp.sqrt(totals[2 * shard :] / entries),
    )


def solution(mesh):
    fsdp, tensor = mesh.shape["fsdp"], mesh.shape["tensor"]
    split = Mesh(mesh.devices.reshape(fsdp // SPANS, 2, 2, tensor), ("y", "x", "c", "z"))
    rows = ("y", "x", "c")
    tok = P(("y", "x", "c", "z"), None)
    col, row, vec = P(rows, "z"), P("z", rows), P(rows)
    return jax.shard_map(
        per_device,
        mesh=split,
        in_specs=(tok, col, col, col, row, col, col, row, vec, vec, tok),
        out_specs=(tok, tok, col, col, col, row, col, col, row, vec, vec, P()),
        check_vma=False,
    )
```
